32 devices in a mesh: dp: 8 (over z, x), mp: 4 (over y, core).
Axes of the slice: x: 2, y: 2, z: 4, core: 2. Of those that a mesh axis runs over, the one named last changes fastest.
Arguments:
- block_input: bfloat16 [4096, 2048], P(('dp', 'mp')), may hold values from -6 to 6
- norm_gain: bfloat16 [2048], replicated, may hold values from 0.099609375 to 1.8984375
- w_in: bfloat16 [2, 2048, 4096], P(None, None, 'mp'), may hold values from -0.125 to 0.125
- conv_w: bfloat16 [4, 4096], P(None, 'mp'), may hold values from -3 to 3
- conv_b: bfloat16 [4096], P('mp'), may hold values from -3 to 3
- w_x: bfloat16 [4096, 160], P('mp'), may hold values from -0.09375 to 0.09375
- w_dt: bfloat16 [128, 4096], P(None, 'mp'), may hold values from -0.5 to 0.5
- b_dt: bfloat16 [4096], P('mp'), may hold values from -5 to -1
- d_skip: bfloat16 [4096], P('mp'), may hold values from 0.099609375 to 1.8984375
- w_out: bfloat16 [4096, 2048], P('mp'), may hold values from -0.09375 to 0.09375
- out_grad: bfloat16 [4096, 2048], P(('dp', 'mp')), may hold values from -6 to 6
- seq_counts: int32 [8, 3], P('dp'), may hold values from 0 to 16, as said below
Outputs:
- block_out: bfloat16 [4096, 2048], P(('dp', 'mp'))
- input_grad: bfloat16 [4096, 2048], P(('dp', 'mp'))
- norm_gain_grad: float32 [2048], replicated
- w_in_grad: float32 [2, 2048, 4096], P(None, None, 'mp')
- conv_w_grad: float32 [4, 4096], P(None, 'mp')
- conv_b_grad: float32 [4096], P('mp')
- w_x_grad: float32 [4096, 160], P('mp')
- w_dt_grad: float32 [128, 4096], P(None, 'mp')
- b_dt_grad: float32 [4096], P('mp')
- d_skip_grad: float32 [4096], P('mp')
- w_out_grad: float32 [4096, 2048], P('mp')
The draws below stay inside these ranges and needn't reach their ends.
Inputs may be any that keep to these rules, and one draw needn't show every extreme that they name: `seq_counts`: row g holds the counts of sequences of 512, 128 and 32 tokens in data group g, in that order; they fill the group's 512 tokens exactly.
All inputs are finite; a program needn't handle non-finite values.
Results may differ from the reference program's by a relative error of at most 0.012.
Values may be sent and summed in bfloat16 or wider, within the bound.
No kernel may reach another device: no remote copies, remote signals or barrier semaphores. Data moves between devices by JAX's collectives and lax.ppermute only.
A program may use at most 448 MiB of HBM per device.

```python
import jax
import jax.numpy as jnp
from jax import lax

D = 2048
E = 4096
N = 16
R = 128
KW = 4
LONG = 512
TOKENS = 4096
N_DP = 8


def draw_seq_counts(key, part):
    key = jax.random.fold_in(key, 7)
    first_key, second_key = jax.random.split(key, 2)
    bucket_pick = jax.random.randint(first_key, (N_DP,), 0, 6)
    forced_group = jax.random.randint(second_key, (), 0, N_DP)
    bucket_pick = jnp.where(jnp.arange(N_DP) == forced_group, 0, bucket_pick)
    long_count = jnp.where(bucket_pick == 5, 1, 0)
    middle_count = jnp.where(bucket_pick == 5, 0, bucket_pick)
    short_count = jnp.where(bucket_pick == 5, 0, 16 - 4 * bucket_pick)
    return jnp.stack([long_count, middle_count, short_count], 1).astype(jnp.int32)


def steps_of(own_key, extent, cuts, least, largest):
    def one(dim, blocks):
        heights = jax.random.uniform(jax.random.fold_in(jax.random.fold_in(own_key, 6), dim), (blocks,), jnp.float32, least / len(cuts), largest / len(cuts))
        return jnp.repeat(jnp.exp(heights), extent[dim] // blocks).reshape((-1,) + (1,) * (len(extent) - dim - 1))

    factor_of = one(*cuts[0])
    for cut in cuts[1:]:
        factor_of = factor_of * one(*cut)
    return factor_of


def bell_draw(rng, extent, scale, limit, cuts=(), kind=jnp.bfloat16):
    loudness = steps_of(rng, extent, cuts, -0.22, 0.18) if cuts else 1.0
    values = jax.random.normal(rng, extent, jnp.float32) * scale * loudness
    return jnp.minimum(jnp.maximum(values, -limit), limit).astype(kind)


def setup_inputs(seed: int = 0) -> dict:
    streams_of = jax.random.split(jax.random.key(seed), 13)
    block_input = bell_draw(streams_of[0], (TOKENS, D), 1.0, 6.0, ((0, 32),))
    norm_gain = jnp.clip(1.0 + 0.18 * jax.random.normal(streams_of[1], (D,), jnp.float32), 0.099609375, 1.8984375).astype(jnp.bfloat16)
    w_in = bell_draw(streams_of[2], (2, D, E), D ** -0.5, 0.125, ((2, 4),))
    conv_w = bell_draw(streams_of[3], (KW, E), KW ** -0.5, 3.0, ((1, 4),))
    conv_b = bell_draw(streams_of[4], (E,), 0.5, 3.0, ((0, 4),))
    w_x = bell_draw(streams_of[5], (E, R + 2 * N), E ** -0.5, 0.09375, ((0, 4),))
    w_dt = bell_draw(streams_of[6], (R, E), R ** -0.5, 0.5, ((1, 4),))
    b_dt = jnp.clip(-5.0 + 4.0 * jax.random.uniform(streams_of[7], (E,), jnp.float32) ** steps_of(streams_of[7], (E,), ((0, 4),), -0.2, 0.2), -5.0, -1.0).astype(jnp.bfloat16)
    d_skip = jnp.clip(1.0 + 0.18 * jax.random.normal(streams_of[8], (E,), jnp.float32), 0.099609375, 1.8984375).astype(jnp.bfloat16)
    w_out = bell_draw(streams_of[9], (E, D), E ** -0.5, 0.09375, ((0, 4),))
    out_grad = bell_draw(streams_of[10], (TOKENS, D), 1.0, 6.0, ((0, 32),))
    seq_counts = draw_seq_counts(jax.random.fold_in(streams_of[12], 71), 0)
    return dict(block_input=block_input, norm_gain=norm_gain, w_in=w_in, conv_w=conv_w, conv_b=conv_b, w_x=w_x, w_dt=w_dt, b_dt=b_dt, d_skip=d_skip, w_out=w_out, out_grad=out_grad, seq_counts=seq_counts)


HIGHEST = lax.Precision.HIGHEST

@jax.custom_vjp
def low(v):
    return lax.optimization_barrier(v.astype(jnp.bfloat16)).astype(jnp.float32)

@jax.custom_vjp
def low_back(v):
    return v

def low_keep(v):
    return (low(v), None)

def low_pass(kept, grad):
    return (grad,)

def back_keep(v):
    return (v, None)

def back_low(kept, grad):
    return (low(grad),)
low.defvjp(low_keep, low_pass)
low_back.defvjp(back_keep, back_low)

def boundaries(bucket_row, length):
    position = jnp.arange(length, dtype=jnp.int32)
    short_len = length // 16
    middle_len = length // 4
    short_end = bucket_row[2] * short_len
    middle_end = short_end + bucket_row[1] * middle_len
    first_short = (position < short_end) & (position % short_len == 0)
    first_middle = (position >= short_end) & (position < middle_end) & ((position - short_end) % middle_len == 0)
    first_long = (position == middle_end) & (position < length)
    opening = first_short | first_middle | first_long
    return jnp.where(opening, 0.0, 1.0).astype(jnp.float32)

def shift_down(values, lag):
    return jnp.concatenate([jnp.zeros((lag,) + values.shape[1:], values.dtype), values[:-lag]], 0)

def conv_taps(inner, keep_mask):
    allow_one = keep_mask
    allow_two = allow_one * shift_down(keep_mask, 1)
    allow_three = allow_two * shift_down(keep_mask, 2)
    taps = [inner, allow_one[:, None] * shift_down(inner, 1), allow_two[:, None] * shift_down(inner, 2), allow_three[:, None] * shift_down(inner, 3)]
    return (taps, [allow_one, allow_two, allow_three])

def recurrence(keep_mask, step_size, acts, keys, queries):
    length = keys.shape[0]
    span_len = min(64, length)
    block_count = length // span_len

    def position(state, row_item):
        keep_now, step_now, act_now, key_now, query_now = row_item
        decay_rate = keep_now * (1.0 - step_now[None, :] * (key_now * key_now)[:, None])
        state = decay_rate * state + (step_now * act_now)[None, :] * key_now[:, None]
        return (state, lax.optimization_barrier(jnp.sum(query_now[:, None] * state, 0)))

    def segment(state, rows_item):
        return lax.scan(position, state, rows_item)
    pieces = tuple((v.reshape((block_count, span_len) + v.shape[1:]) for v in (keep_mask, step_size, acts, keys, queries)))
    start_state = jnp.zeros((keys.shape[1], step_size.shape[1]), step_size.dtype)
    _, outputs = lax.scan(jax.checkpoint(segment), start_state, pieces)
    return outputs.reshape(length, step_size.shape[1])

def group_forward(rows_in, keep_mask, params):
    norm_gain, w_in, conv_w, conv_b, w_x, w_dt, b_dt, d_skip, w_out = params
    inv_root = lax.rsqrt(lax.optimization_barrier(jnp.mean(rows_in * rows_in, -1, keepdims=True)) + 1e-05)
    normed = low(rows_in * inv_root * norm_gain)
    mixed = low_back(jnp.einsum('td,kdc->tkc', normed, w_in, precision=HIGHEST))
    inner = mixed[:, 0]
    gate_in = mixed[:, 1]
    taps, _ = conv_taps(inner, keep_mask)
    conv_pre = conv_b + sum((conv_w[index] * taps[index] for index in range(len(taps))))
    acts = low(jax.nn.silu(conv_pre))
    proj = low_back(jnp.dot(acts, w_x, precision=HIGHEST))
    low_rank = low(proj[:, :R])
    keys = proj[:, R:R + N]
    queries = proj[:, R + N:]
    pre_act = low_back(jnp.dot(low_rank, w_dt, precision=HIGHEST) + b_dt)
    beta = jax.nn.sigmoid(pre_act)
    key_square = lax.optimization_barrier(jnp.sum(keys * keys, -1, keepdims=True))
    step_size = beta / (1.0 + beta * key_square)
    mixer = recurrence(keep_mask, step_size, acts, keys, queries) + d_skip * acts
    gated = low(mixer * jax.nn.silu(gate_in))
    return rows_in + jnp.dot(gated, w_out, precision=HIGHEST)

def reference(block_input, norm_gain, w_in, conv_w, conv_b, w_x, w_dt, b_dt, d_skip, w_out, out_grad, seq_counts):
    floats = tuple((v.astype(jnp.float32) for v in (block_input, norm_gain, w_in, conv_w, conv_b, w_x, w_dt, b_dt, d_skip, w_out)))
    keep_all = jax.vmap(lambda bucket_row: boundaries(bucket_row, LONG))(seq_counts)

    def forward(inputs_all, *params):
        grouped = inputs_all.reshape(N_DP, LONG, D)

        def one_group(group_item):
            return group_forward(group_item[0], group_item[1], params)
        outputs = lax.map(jax.checkpoint(one_group), (grouped, keep_all))
        return outputs.reshape(N_DP * LONG, D)
    result, pullback = jax.vjp(forward, *floats)
    grads = pullback(out_grad.astype(jnp.float32))
    return (result.astype(jnp.bfloat16), grads[0].astype(jnp.bfloat16), grads[1], grads[2], grads[3], grads[4], grads[5], grads[6], grads[7], grads[8], grads[9])
```

```python
import jax
import jax.numpy as jnp
from jax import lax
from jax.experimental import pallas as pl
from jax.experimental.pallas import tpu as pltpu
from jax.sharding import PartitionSpec as P

R = 128
CHUNK = 32

def boundaries(bucket_row, length):
    position = jnp.arange(length, dtype=jnp.int32)
    short_len = length // 16
    middle_len = length // 4
    short_end = bucket_row[2] * short_len
    middle_end = short_end + bucket_row[1] * middle_len
    first_short = (position < short_end) & (position % short_len == 0)
    first_middle = (
        (position >= short_end)
        & (position < middle_end)
        & ((position - short_end) % middle_len == 0)
    )
    first_long = (position == middle_end) & (position < length)
    opening = first_short | first_middle | first_long
    return jnp.where(opening, 0.0, 1.0).astype(jnp.float32)


def shift_down(values, lag):
    return jnp.concatenate([jnp.zeros((lag,) + values.shape[1:], values.dtype), values[:-lag]], 0)


def shift_up(values, lag):
    return jnp.concatenate([values[lag:], jnp.zeros((lag,) + values.shape[1:], values.dtype)], 0)


def conv_taps(inner, keep_mask):
    allow_two = keep_mask * shift_down(keep_mask, 1)
    allow_three = allow_two * shift_down(keep_mask, 2)
    taps = [
        inner,
        keep_mask[:, None] * shift_down(inner, 1),
        allow_two[:, None] * shift_down(inner, 2),
        allow_three[:, None] * shift_down(inner, 3),
    ]
    return (taps, [keep_mask, allow_two, allow_three])


def col_sums(values):
    rows = values[0].shape[0]
    if rows != 8:
        return jnp.concatenate([jnp.sum(v, 0, keepdims=True) for v in values], 0)
    row = lax.broadcasted_iota(jnp.int32, (8, 128), 0)
    span = 1
    while len(values) > 1:
        low = (row // span) % 2 == 0
        values = [
            jnp.where(low, a, b) + pltpu.roll(jnp.where(low, b, a), 8 - span, axis=0)
            for a, b in zip(values[0::2], values[1::2])
        ]
        span *= 2
    return values[0]


def fwd_kernel(chunk, n, keys, queries, keeps, step_ref, acts_ref, mix_ref, states_ref, carry):
    index = pl.program_id(0)
    tiles = carry.shape[1]

    @pl.when(index == 0)
    def _():
        carry[...] = jnp.zeros_like(carry)

    keep = keeps[index]
    start = tuple(carry[j] * keep for j in range(n))

    def eight(block, state):
        state = list(state)
        for i in range(8):
            rows = pl.ds(i, tiles, stride=8)
            step = step_ref[block, rows, :]
            act = acts_ref[block, rows, :]
            token = block * 8 + i
            base = (index * chunk + token) * n
            total = None
            for j in range(n):
                k = keys[base + j]
                state[j] = state[j] + (step * k) * (act - state[j] * k)
                states_ref[token, j] = state[j]
                part = state[j] * queries[base + j]
                total = part if total is None else total + part
            mix_ref[block, rows, :] = total
        return tuple(state)

    final = lax.fori_loop(0, chunk // 8, eight, start)
    for j in range(n):
        carry[j] = final[j]


def scan_forward(keys, queries, keeps, step, acts, chunk, n):
    blocks, height, _ = step.shape
    tiles = height // 8
    length = blocks * 8
    count = length // chunk
    wide = pl.BlockSpec((chunk // 8, height, 128), lambda c: (c, 0, 0))
    scal = pl.BlockSpec(memory_space=pltpu.SMEM)
    return pl.pallas_call(
        lambda *refs: fwd_kernel(chunk, n, *refs),
        grid=(count,),
        in_specs=[scal, scal, scal, wide, wide],
        out_specs=[wide, pl.BlockSpec((chunk, n, tiles, 128), lambda c: (c, 0, 0, 0))],
        out_shape=[
            jax.ShapeDtypeStruct(step.shape, jnp.float32),
            jax.ShapeDtypeStruct((length, n, tiles, 128), jnp.float32),
        ],
        scratch_shapes=[pltpu.VMEM((n, tiles, 128), jnp.float32)],
        compiler_params=pltpu.CompilerParams(vmem_limit_bytes=48 << 20),
    )(keys, queries, keeps, step, acts)


def bwd_kernel(
    chunk, n, keys, queries, keeps, step_ref, acts_ref, ygrad_ref, states_ref, prior_ref,
    sgrad_ref, agrad_ref, kred_ref, qred_ref, carry
):
    order = pl.program_id(0)
    index = pl.num_programs(0) - 1 - order
    tiles = carry.shape[1]

    @pl.when(order == 0)
    def _():
        carry[...] = jnp.zeros_like(carry)

    keep = keeps[index]

    def token_step(block, i, adjoint, prior_of):
        rows = pl.ds(i, tiles, stride=8)
        step = step_ref[block, rows, :]
        act = acts_ref[block, rows, :]
        ygrad = ygrad_ref[block, rows, :]
        token = block * 8 + i
        base = (index * chunk + token) * n
        drive = None
        fade = None
        kparts = []
        qparts = []
        for j in range(n):
            k = keys[base + j]
            adj = adjoint[j] + ygrad * queries[base + j]
            prior = prior_of(token, j)
            ka = adj * k
            kp = prior * k
            weighted = step * adj
            kparts.append(weighted * (act - (kp + kp)))
            qparts.append(states_ref[token, j] * ygrad)
            loss = ka * kp
            drive = ka if drive is None else drive + ka
            fade = loss if fade is None else fade + loss
            adjoint[j] = adj - (step * k) * ka
        sgrad_ref[block, rows, :] = act * drive - fade
        agrad_ref[block, rows, :] = step * drive
        for first in range(0, n, 8):
            kred_ref[token, first:first + 8, :] = col_sums(kparts[first:first + 8])
            qred_ref[token, first:first + 8, :] = col_sums(qparts[first:first + 8])
        return adjoint

    def eight(turn, adjoint):
        block = chunk // 8 - 1 - turn
        adjoint = list(adjoint)
        for i in range(7, -1, -1):
            if i > 0:
                adjoint = token_step(block, i, adjoint, lambda token, j: states_ref[token - 1, j])
            else:
                first = block == 0
                held = jnp.where(first, keep, 1.0)
                back = jnp.maximum(block * 8 - 1, 0)
                adjoint = token_step(
                    block, i, adjoint,
                    lambda token, j: jnp.where(first, prior_ref[0, j], states_ref[back, j]) * held,
                )
        return tuple(adjoint)

    final = lax.fori_loop(0, chunk // 8, eight, tuple(carry[j] for j in range(n)))
    for j in range(n):
        carry[j] = final[j] * keep


def scan_backward(keys, queries, keeps, step, acts, ygrad, states, chunk, n):
    blocks, height, _ = step.shape
    tiles = height // 8
    length = blocks * 8
    count = length // chunk
    last = count - 1
    wide = pl.BlockSpec((chunk // 8, height, 128), lambda c: (last - c, 0, 0))
    scal = pl.BlockSpec(memory_space=pltpu.SMEM)
    red = pl.BlockSpec((chunk, n, 128), lambda c: (last - c, 0, 0))
    return pl.pallas_call(
        lambda *refs: bwd_kernel(chunk, n, *refs),
        grid=(count,),
        in_specs=[
            scal, scal, scal, wide, wide, wide,
            pl.BlockSpec((chunk, n, tiles, 128), lambda c: (last - c, 0, 0, 0)),
            pl.BlockSpec((1, n, tiles, 128), lambda c: (jnp.maximum((last - c) * chunk - 1, 0), 0, 0, 0)),
        ],
        out_specs=[wide, wide, red, red],
        out_shape=[jax.ShapeDtypeStruct(step.shape, jnp.float32)] * 2
        + [jax.ShapeDtypeStruct((length, n, 128), jnp.float32)] * 2,
        scratch_shapes=[pltpu.VMEM((n, tiles, 128), jnp.float32)],
        compiler_params=pltpu.CompilerParams(vmem_limit_bytes=48 << 20),
    )(keys, queries, keeps, step, acts, ygrad, states, states)

def to_tiles(values):
    length, channels = values.shape
    parts = values.reshape(length // 8, 8, channels // 128, 128).transpose(0, 2, 1, 3)
    return parts.reshape(length // 8, channels // 16, 128)


def from_tiles(values):
    blocks, height, _ = values.shape
    parts = values.reshape(blocks, height // 8, 8, 128).transpose(0, 2, 1, 3)
    return parts.reshape(blocks * 8, height * 16)


def sum_over(values, axis):
    return lax.psum(values.astype(jnp.bfloat16), axis).astype(jnp.float32)


def on_device(
    block_input,
    norm_gain,
    w_in,
    conv_w,
    conv_b,
    w_x,
    w_dt,
    b_dt,
    d_skip,
    w_out,
    out_grad,
    seq_counts,
):
    row_count = block_input.shape[0]
    length = row_count * lax.axis_size("mp")
    state_size = (w_x.shape[1] - R) // 2
    source_rows = block_input.astype(jnp.float32)
    inv_root = lax.rsqrt(jnp.mean(source_rows * source_rows, -1, keepdims=True) + 1e-05)
    normed = (source_rows * inv_root * norm_gain).astype(jnp.bfloat16)
    all_normed = lax.all_gather(normed, "mp", axis=0, tiled=True)
    all_ograd = lax.all_gather(out_grad, "mp", axis=0, tiled=True)
    inner = jnp.dot(all_normed, w_in[0], preferred_element_type=jnp.float32)
    gate_in = jnp.dot(all_normed, w_in[1], preferred_element_type=jnp.float32)
    keep_mask = boundaries(seq_counts[0], length)
    taps, allows = conv_taps(inner, keep_mask)
    conv_pre = conv_b + sum((conv_w[index] * taps[index] for index in range(len(taps))))
    acts = jax.nn.silu(conv_pre).astype(jnp.bfloat16)
    acts_full = acts.astype(jnp.float32)
    proj = lax.psum(jnp.dot(acts, w_x, preferred_element_type=jnp.float32), "mp")
    low_rank = proj[:, :R].astype(jnp.bfloat16)
    keys = proj[:, R : R + state_size]
    queries = proj[:, R + state_size :]
    pre_act = jnp.dot(low_rank, w_dt, preferred_element_type=jnp.float32) + b_dt
    beta = jax.nn.sigmoid(pre_act)
    key_square = jnp.sum(keys * keys, 1, keepdims=True)
    denom = 1.0 + beta * key_square
    step_size = beta / denom
    flat_keys = keys.reshape(-1)
    flat_queries = queries.reshape(-1)
    keeps = keep_mask[::CHUNK]
    step_tiles = to_tiles(step_size)
    acts_tiles = to_tiles(acts_full)
    mix_tiles, states = scan_forward(
        flat_keys, flat_queries, keeps, step_tiles, acts_tiles, CHUNK, state_size
    )
    mixer = from_tiles(mix_tiles) + d_skip * acts_full
    gate_sig = jax.nn.sigmoid(gate_in)
    gate_silu = gate_in * gate_sig
    gated = (mixer * gate_silu).astype(jnp.bfloat16)
    gated_rows = lax.dot_general(
        all_ograd, w_out, (((1,), (1,)), ((), ())), preferred_element_type=jnp.float32
    )
    gate_grad = (gated_rows * mixer * gate_sig * (1.0 + gate_in * (1.0 - gate_sig))).astype(
        jnp.bfloat16
    )
    mixer_grad = gated_rows * gate_silu
    tokens = (((0,), (0,)), ((), ()))
    w_out_part = lax.dot_general(gated, all_ograd, tokens, preferred_element_type=jnp.float32)
    w_gate_part = lax.dot_general(all_normed, gate_grad, tokens, preferred_element_type=jnp.float32)
    w_out_grad = sum_over(w_out_part, "dp")
    w_gate_grad = sum_over(w_gate_part, "dp")
    sgrad_tiles, agrad_tiles, key_red, query_red = scan_backward(
        flat_keys,
        flat_queries,
        keeps,
        step_tiles,
        acts_tiles,
        to_tiles(mixer_grad),
        states,
        CHUNK,
        state_size,
    )
    branch_out = lax.psum_scatter(
        jnp.dot(gated, w_out, preferred_element_type=jnp.float32).astype(jnp.bfloat16),
        "mp",
        scatter_dimension=0,
        tiled=True,
    ).astype(jnp.float32)
    block_out = (source_rows + branch_out).astype(jnp.bfloat16)
    d_skip_grad = jnp.sum(mixer_grad * acts_full, 0)
    step_grad = from_tiles(sgrad_tiles)
    act_grad = from_tiles(agrad_tiles)
    square_denom = denom * denom
    ksq_grad = jnp.sum(step_grad * (-(beta * beta) / square_denom), 1, keepdims=True)
    pre_grad = (step_grad / square_denom * beta * (1.0 - beta)).astype(jnp.bfloat16)
    b_dt_grad = jnp.sum(pre_grad, 0, dtype=jnp.float32)
    w_dt_grad = lax.dot_general(low_rank, pre_grad, tokens, preferred_element_type=jnp.float32)
    low_grad = lax.dot_general(
        pre_grad, w_dt, (((1,), (1,)), ((), ())), preferred_element_type=jnp.float32
    )
    key_grad = jnp.sum(key_red, -1) + 2.0 * keys * ksq_grad
    query_grad = jnp.sum(query_red, -1)
    proj_grad = lax.psum(jnp.concatenate([low_grad, key_grad, query_grad], 1), "mp").astype(
        jnp.bfloat16
    )
    w_x_grad = lax.dot_general(acts, proj_grad, tokens, preferred_element_type=jnp.float32)
    acts_grad = (
        act_grad
        + mixer_grad * d_skip
        + lax.dot_general(
            proj_grad, w_x, (((1,), (1,)), ((), ())), preferred_element_type=jnp.float32
        )
    )
    conv_sig = jax.nn.sigmoid(conv_pre)
    conv_grad = acts_grad * conv_sig * (1.0 + conv_pre * (1.0 - conv_sig))
    conv_b_grad = jnp.sum(conv_grad, 0)
    conv_w_grad = jnp.stack([jnp.sum(conv_grad * tap_rows, 0) for tap_rows in taps], 0)
    inner_grad = conv_w[0] * conv_grad + sum(
        (
            shift_up(allows[index - 1][:, None] * conv_grad * conv_w[index], index)
            for index in range(1, len(taps))
        )
    )
    inner_grad = inner_grad.astype(jnp.bfloat16)
    w_inner_part = lax.dot_general(
        all_normed, inner_grad, tokens, preferred_element_type=jnp.float32
    )
    w_inner_grad = sum_over(w_inner_part, "dp")
    across = (((1,), (1,)), ((), ()))
    normed_grad = lax.psum_scatter(
        lax.dot_general(inner_grad, w_in[0], across, preferred_element_type=jnp.float32)
        + lax.dot_general(gate_grad, w_in[1], across, preferred_element_type=jnp.float32),
        "mp",
        scatter_dimension=0,
        tiled=True,
    )
    scaled = normed_grad * norm_gain
    gain_part = jnp.sum(normed_grad * source_rows * inv_root, 0)
    cubed = inv_root * inv_root * inv_root
    input_grad = inv_root * scaled - source_rows * cubed * jnp.mean(
        scaled * source_rows, -1, keepdims=True
    )
    input_grad = (out_grad.astype(jnp.float32) + input_grad).astype(jnp.bfloat16)
    norm_gain_grad = lax.psum(gain_part, ("dp", "mp"))
    conv_w_grad, conv_b_grad, w_x_grad, w_dt_grad, b_dt_grad, d_skip_grad = lax.psum(
        (conv_w_grad, conv_b_grad, w_x_grad, w_dt_grad, b_dt_grad, d_skip_grad), "dp"
    )
    return (
        block_out,
        input_grad,
        norm_gain_grad,
        jnp.stack([w_inner_grad, w_gate_grad]),
        conv_w_grad,
        conv_b_grad,
        w_x_grad,
        w_dt_grad,
        b_dt_grad,
        d_skip_grad,
        w_out_grad,
    )


def solution(mesh):
    in_specs = (
        P(("dp", "mp"), None),
        P(),
        P(None, None, "mp"),
        P(None, "mp"),
        P("mp"),
        P("mp", None),
        P(None, "mp"),
        P("mp"),
        P("mp"),
        P("mp", None),
        P(("dp", "mp"), None),
        P("dp", None),
    )
    out_specs = (
        P(("dp", "mp"), None),
        P(("dp", "mp"), None),
        P(),
        P(None, None, "mp"),
        P(None, "mp"),
        P("mp"),
        P("mp", None),
        P(None, "mp"),
        P("mp"),
        P("mp"),
        P("mp", None),
    )
    return jax.shard_map(
        on_device, mesh=mesh, in_specs=in_specs, out_specs=out_specs, check_vma=False
    )
```

```python
import jax
import jax.numpy as jnp
from jax import lax
from jax.experimental import pallas as pl
from jax.experimental.pallas import tpu as pltpu
from jax.sharding import PartitionSpec as P

R = 128
CHUNK = 64
LINE = 4

def boundaries(bucket_row, length):
    position = jnp.arange(length, dtype=jnp.int32)
    short_len = length // 16
    middle_len = length // 4
    short_end = bucket_row[2] * short_len
    middle_end = short_end + bucket_row[1] * middle_len
    first_short = (position < short_end) & (position % short_len == 0)
    first_middle = (
        (position >= short_end)
        & (position < middle_end)
        & ((position - short_end) % middle_len == 0)
    )
    first_long = (position == middle_end) & (position < length)
    opening = first_short | first_middle | first_long
    return jnp.where(opening, 0.0, 1.0).astype(jnp.float32)


def shift_down(values, lag):
    return jnp.concatenate([jnp.zeros((lag,) + values.shape[1:], values.dtype), values[:-lag]], 0)


def estimate(micros):
    return pl.CostEstimate(flops=0, bytes_accessed=int(micros * 3.3e6), transcendentals=0)


TOKENS = (((0,), (0,)), ((), ()))
ACROSS = (((1,), (1,)), ((), ()))


def product(left, right, dims=(((1,), (0,)), ((), ()))):
    return lax.dot_general(left, right, dims, preferred_element_type=jnp.float32)


def fixed(shape):
    return pl.BlockSpec(shape, lambda *_: (0,) * len(shape), pipeline_mode=pl.Buffered(1))


def anywhere():
    return pl.BlockSpec(memory_space=pl.ANY)


def whole(shape):
    return pl.BlockSpec(shape, lambda *_: (0,) * len(shape))


def row_sums(values):
    if values[0].shape[0] != 8:
        return jnp.concatenate([jnp.sum(value, 0, keepdims=True) for value in values], 0)
    row = lax.broadcasted_iota(jnp.int32, (8, 128), 0)
    span = 1
    while len(values) > 1:
        low = (row // span) % 2 == 0
        values = [
            jnp.where(low, a, b) + pltpu.roll(jnp.where(low, b, a), 8 - span, axis=0)
            for a, b in zip(values[0::2], values[1::2])
        ]
        span *= 2
    return values[0]


def forward_kernel(chunk, n, length, scalars, step_ref, acts_ref, mix_ref, states_ref, carry):
    index = pl.program_id(0)
    tiles = carry.shape[1]

    @pl.when(index == 0)
    def _():
        carry[...] = jnp.zeros_like(carry)

    def eight(block, state):
        keep = scalars[(2 * n + 1) * length + index * (chunk // 8) + block]
        state = [value * keep for value in state]
        for i in range(8):
            rows = pl.ds(i, tiles, stride=8)
            step = step_ref[block, rows, :]
            act = acts_ref[block, rows, :]
            token = block * 8 + i
            base = (index * chunk + token) * n
            total = None
            for j in range(n):
                k = scalars[base + j]
                state[j] = state[j] + (step * k) * (act - state[j] * k)
                states_ref[token, j] = state[j]
                part = state[j] * scalars[n * length + base + j]
                total = part if total is None else total + part
            mix_ref[block, rows, :] = total
        return tuple(state)

    final = lax.fori_loop(0, chunk // 8, eight, tuple(carry[j] for j in range(n)))
    for j in range(n):
        carry[j] = final[j]


def scan_forward(values, step, acts, chunk, n, after):
    blocks, height, _ = step.shape
    tiles = height // 8
    length = blocks * 8
    wide = pl.BlockSpec((chunk // 8, height, 128), lambda c: (c, 0, 0))
    scalars = pl.BlockSpec(memory_space=pltpu.SMEM)
    return pl.pallas_call(
        lambda *refs: forward_kernel(
            chunk, n, length, *refs[:3], *refs[3 + len(after) :]
        ),
        grid=(length // chunk,),
        in_specs=[scalars, wide, wide] + [anywhere()] * len(after),
        out_specs=[wide, pl.BlockSpec((chunk, n, tiles, 128), lambda c: (c, 0, 0, 0))],
        out_shape=[
            jax.ShapeDtypeStruct(step.shape, jnp.float32),
            jax.ShapeDtypeStruct((length, n, tiles, 128), jnp.float32),
        ],
        scratch_shapes=[pltpu.VMEM((n, tiles, 128), jnp.float32)],
        compiler_params=pltpu.CompilerParams(vmem_limit_bytes=48 << 20),
        cost_estimate=estimate(16),
        name="scan_forward",
    )(values, step, acts, *after)


def backward_kernel(
    chunk,
    n,
    last,
    carry_in,
    sums_in,
    length,
    scalars,
    step_ref,
    acts_ref,
    ygrad_ref,
    states_ref,
    prior_ref,
    skip_ref,
    pre_ref,
    agrad_ref,
    kgrad_ref,
    qgrad_ref,
    fade_ref,
    sums_ref,
    carry,
    kred,
    qred,
):
    order = pl.program_id(0)
    index = last - order
    tiles = carry.shape[1]

    @pl.when(order == 0)
    def _():
        if carry_in is None:
            carry[...] = jnp.zeros_like(carry)
            sums_ref[...] = jnp.zeros_like(sums_ref)
        else:
            carry[...] = carry_in[...]
            sums_ref[...] = sums_in[...]

    skip = skip_ref[...]

    def token_step(block, i, adjoint, prior_of):
        rows = pl.ds(i, tiles, stride=8)
        step = step_ref[block, rows, :]
        act = acts_ref[block, rows, :]
        ygrad = ygrad_ref[block, rows, :]
        token = block * 8 + i
        where = index * chunk + token
        base = where * n
        drive = None
        loss = None
        kparts = []
        qparts = []
        for j in range(n):
            k = scalars[base + j]
            adj = adjoint[j] + ygrad * scalars[n * length + base + j]
            prior = prior_of(token, j)
            ka = adj * k
            kp = prior * k
            kparts.append((step * adj) * (act - (kp + kp)))
            qparts.append(states_ref[token, j] * ygrad)
            part = ka * kp
            drive = ka if drive is None else drive + ka
            loss = part if loss is None else loss + part
            adjoint[j] = adj - (step * k) * ka
        step_grad = act * drive - loss
        scaled = step_grad * step
        pre = scaled * (1.0 - step * (1.0 + scalars[2 * n * length + where]))
        pre_ref[block, rows, :] = pre
        agrad_ref[block, rows, :] = step * drive + ygrad * skip
        sums_ref[0] += pre.astype(jnp.bfloat16).astype(jnp.float32)
        sums_ref[1] += ygrad * act
        for first in range(0, n, 8):
            kred[token, first : first + 8, :] = row_sums(kparts[first : first + 8])
            qred[token, first : first + 8, :] = row_sums(qparts[first : first + 8])
        return scaled * step

    def eight(turn, adjoint):
        block = chunk // 8 - 1 - turn
        adjoint = list(adjoint)
        keep = scalars[(2 * n + 1) * length + index * (chunk // 8) + block]
        fades = [None] * 8
        for i in range(7, 0, -1):
            fades[i] = token_step(block, i, adjoint, lambda token, j: states_ref[token - 1, j])
        first = block == 0
        back = jnp.maximum(block * 8 - 1, 0)
        fades[0] = token_step(
            block,
            0,
            adjoint,
            lambda token, j: jnp.where(first, prior_ref[0, j], states_ref[back, j]) * keep,
        )
        fade_ref[pl.ds(pl.multiple_of(block * 8, 8), 8), :] = row_sums(fades)
        return tuple(value * keep for value in adjoint)

    final = lax.fori_loop(0, chunk // 8, eight, tuple(carry[j] for j in range(n)))
    for j in range(n):
        carry[j] = final[j]
    kgrad_ref[...] = jnp.sum(kred[...], -1)
    qgrad_ref[...] = jnp.sum(qred[...], -1)


def scan_backward(
    values, step, acts, ygrad, states, skip, chunk, n, span, before, after
):
    blocks, height, _ = step.shape
    tiles = height // 8
    length = blocks * 8
    last = span[1] - 1
    wide = pl.BlockSpec((chunk // 8, height, 128), lambda c: (last - c, 0, 0))
    scalars = pl.BlockSpec(memory_space=pltpu.SMEM)
    narrow = pl.BlockSpec((chunk, n), lambda c: (last - c, 0))
    kept = pl.BlockSpec((n, tiles, 128), lambda c: (0, 0, 0))
    pair = pl.BlockSpec((2, tiles, 128), lambda c: (0, 0, 0))
    in_specs = [
        scalars,
        wide,
        wide,
        wide,
        pl.BlockSpec((chunk, n, tiles, 128), lambda c: (last - c, 0, 0, 0)),
        pl.BlockSpec(
            (1, n, tiles, 128), lambda c: (jnp.maximum((last - c) * chunk - 1, 0), 0, 0, 0)
        ),
        pl.BlockSpec((tiles, 128), lambda c: (0, 0)),
    ]
    operands = [values, step, acts, ygrad, states, states, skip]
    aliases = {}
    base = len(operands)
    if before is not None:
        in_specs += [pair, kept] + [anywhere()] * 5
        operands += [before[5], before[6]] + list(before[:5])
        aliases = {base + 2 + turn: turn for turn in range(5)}
    in_specs += [anywhere()] * len(after)
    operands += list(after)

    def kernel(*refs):
        sums_in, carry_in = refs[base : base + 2] if before is not None else (None, None)
        outs = refs[len(operands) :]
        backward_kernel(
            chunk, n, last, carry_in, sums_in, length, *refs[:base], *outs[:6], *outs[6:]
        )

    return pl.pallas_call(
        kernel,
        grid=(span[1] - span[0],),
        in_specs=in_specs,
        out_specs=[
            wide,
            wide,
            narrow,
            narrow,
            pl.BlockSpec((chunk, 128), lambda c: (last - c, 0)),
            pair,
            kept,
        ],
        out_shape=[jax.ShapeDtypeStruct(step.shape, jnp.float32)] * 2
        + [jax.ShapeDtypeStruct((length, n), jnp.float32)] * 2
        + [
            jax.ShapeDtypeStruct((length, 128), jnp.float32),
            jax.ShapeDtypeStruct((2, tiles, 128), jnp.float32),
            jax.ShapeDtypeStruct((n, tiles, 128), jnp.float32),
        ],
        scratch_shapes=[
            pltpu.VMEM((chunk, n, 128), jnp.float32),
            pltpu.VMEM((chunk, n, 128), jnp.float32),
        ],
        input_output_aliases=aliases,
        compiler_params=pltpu.CompilerParams(vmem_limit_bytes=48 << 20),
        cost_estimate=estimate(32 * chunk * (span[1] - span[0]) / length),
        name="scan_backward",
    )(*operands)


def taps_of(inner, allows):
    return [inner] + [
        pltpu.roll(inner, lag, axis=0) * allows[:, lag - 1 : lag] for lag in range(1, 4)
    ]


def project_in(pieces, masks, w_in, allows, conv_w, conv_b, w_x_rows):
    rank = lax.axis_index("mp")
    rows, depth = pieces[0].shape
    count = len(pieces)
    length = rows * count
    channels = w_in.shape[2]
    tile = min(256, channels)
    width = w_x_rows.shape[0]
    places = jnp.stack([(rank ^ mask) * rows for mask in masks]).astype(jnp.int32)

    def kernel(places_ref, *refs):
        sources = refs[:count]
        w_ref, allow_ref, cw_ref, cb_ref, wx_ref = refs[count : count + 5]
        normed_ref, inner_ref, acts_ref, proj_ref = refs[count + 5 :]
        step = pl.program_id(0)

        @pl.when(step == 0)
        def _():
            for turn in range(count):
                at = pl.multiple_of(places_ref[turn], rows)
                normed_ref[pl.ds(at, rows), :] = sources[turn][...]
            proj_ref[...] = jnp.zeros_like(proj_ref)

        inner = jnp.dot(normed_ref[...], w_ref[0], preferred_element_type=jnp.float32)
        inner_ref[...] = inner
        weights = cw_ref[...].astype(jnp.float32)
        pre = cb_ref[...].astype(jnp.float32)
        for lag, tap in enumerate(taps_of(inner, allow_ref[...])):
            pre = pre + weights[lag : lag + 1] * tap
        acts = (pre * jax.nn.sigmoid(pre)).astype(jnp.bfloat16)
        acts_ref[...] = acts.astype(jnp.float32)
        proj_ref[...] += product(acts, wx_ref[...], ACROSS)

    column = pl.BlockSpec((length, tile), lambda c, places_ref: (0, c))
    return pl.pallas_call(
        kernel,
        grid_spec=pltpu.PrefetchScalarGridSpec(
            num_scalar_prefetch=1,
            grid=(channels // tile,),
            in_specs=[fixed((rows, depth))] * count
            + [
                pl.BlockSpec((1, depth, tile), lambda c, places_ref: (0, 0, c)),
                fixed(allows.shape),
                pl.BlockSpec((4, tile), lambda c, places_ref: (0, c)),
                pl.BlockSpec((1, tile), lambda c, places_ref: (0, c)),
                pl.BlockSpec((width, tile), lambda c, places_ref: (0, c)),
            ],
            out_specs=[whole((length, depth)), column, column, whole((length, width))],
        ),
        out_shape=[
            jax.ShapeDtypeStruct((length, depth), jnp.bfloat16),
            jax.ShapeDtypeStruct((length, channels), jnp.float32),
            jax.ShapeDtypeStruct((length, channels), jnp.float32),
            jax.ShapeDtypeStruct((length, width), jnp.float32),
        ],
        compiler_params=pltpu.CompilerParams(vmem_limit_bytes=56 << 20),
        cost_estimate=estimate(8),
        name="project_in",
    )(places, *pieces, w_in, allows, conv_w, conv_b.reshape(1, -1), w_x_rows)


def project_gate(pieces, masks, normed, w_in, w_out, after):
    rank = lax.axis_index("mp")
    rows, depth = pieces[0].shape
    count = len(pieces)
    length = rows * count
    channels = w_in.shape[2]
    tile = min(256, channels)
    places = jnp.stack([(rank ^ mask) * rows for mask in masks]).astype(jnp.int32)

    def kernel(places_ref, *refs):
        sources = refs[:count]
        normed_ref, w_ref, wo_ref = refs[count : count + 3]
        ograd_ref, silu_ref, grad_ref, slope_ref = refs[-4:]

        @pl.when(pl.program_id(0) == 0)
        def _():
            for turn in range(count):
                at = pl.multiple_of(places_ref[turn], rows)
                ograd_ref[pl.ds(at, rows), :] = sources[turn][...]

        gate = product(normed_ref[...], w_ref[0])
        gated_rows = product(ograd_ref[...], wo_ref[...], ACROSS)
        sig = jax.nn.sigmoid(gate)
        silu = gate * sig
        silu_ref[...] = silu
        grad_ref[...] = gated_rows * silu
        slope_ref[...] = gated_rows * sig * (1.0 + gate * (1.0 - sig))

    column = pl.BlockSpec((length, tile), lambda c, places_ref: (0, c))
    return pl.pallas_call(
        kernel,
        grid_spec=pltpu.PrefetchScalarGridSpec(
            num_scalar_prefetch=1,
            grid=(channels // tile,),
            in_specs=[fixed((rows, depth))] * count
            + [
                fixed((length, depth)),
                pl.BlockSpec((1, depth, tile), lambda c, places_ref: (1, 0, c)),
                pl.BlockSpec((tile, depth), lambda c, places_ref: (c, 0)),
            ]
            + [anywhere()] * len(after),
            out_specs=[whole((length, depth)), column, column, column],
        ),
        out_shape=[jax.ShapeDtypeStruct((length, depth), jnp.bfloat16)]
        + [jax.ShapeDtypeStruct((length, channels), jnp.float32)] * 3,
        compiler_params=pltpu.CompilerParams(vmem_limit_bytes=60 << 20),
        cost_estimate=estimate(11),
        name="project_gate",
    )(places, *pieces, normed, w_in, w_out, *after)


def finish_inner(agrad, proj_grad, w_x_rows, inner, allows, conv_w, conv_b, after):
    length, channels = inner.shape
    tile = min(256, channels)
    width = w_x_rows.shape[0]

    def kernel(ag_ref, pg_ref, wx_ref, inner_ref, allow_ref, cw_ref, cb_ref, *refs):
        out_ref, sums_ref = refs[-2:]
        acts_grad = ag_ref[...] + product(pg_ref[...], wx_ref[...])
        allow = allow_ref[...]
        taps = taps_of(inner_ref[...], allow)
        weights = cw_ref[...].astype(jnp.float32)
        pre = cb_ref[...].astype(jnp.float32)
        for lag, tap in enumerate(taps):
            pre = pre + weights[lag : lag + 1] * tap
        sig = jax.nn.sigmoid(pre)
        conv_grad = acts_grad * sig * (1.0 + pre * (1.0 - sig))
        rows = [jnp.sum(conv_grad * tap, 0, keepdims=True) for tap in taps]
        rows.append(jnp.sum(conv_grad, 0, keepdims=True))
        sums_ref[...] = jnp.concatenate(rows + [jnp.zeros((3, tile), jnp.float32)], 0)
        total = weights[0:1] * conv_grad
        for lag in range(1, 4):
            sent = conv_grad * allow[:, lag - 1 : lag] * weights[lag : lag + 1]
            total = total + pltpu.roll(sent, length - lag, axis=0)
        out_ref[...] = total.astype(jnp.bfloat16)

    column = pl.BlockSpec((length, tile), lambda c: (0, c))
    return pl.pallas_call(
        kernel,
        grid=(channels // tile,),
        in_specs=[
            column,
            fixed((length, width)),
            pl.BlockSpec((width, tile), lambda c: (0, c)),
            column,
            fixed(allows.shape),
            pl.BlockSpec((4, tile), lambda c: (0, c)),
            pl.BlockSpec((1, tile), lambda c: (0, c)),
        ]
        + [anywhere()] * len(after),
        out_specs=[column, pl.BlockSpec((8, tile), lambda c: (0, c))],
        out_shape=[
            jax.ShapeDtypeStruct((length, channels), jnp.bfloat16),
            jax.ShapeDtypeStruct((8, channels), jnp.float32),
        ],
        compiler_params=pltpu.CompilerParams(vmem_limit_bytes=56 << 20),
        cost_estimate=estimate(6),
        name="finish_inner",
    )(agrad, proj_grad, w_x_rows, inner, allows, conv_w, conv_b.reshape(1, -1), *after)


def factor_products(jobs, others, masks, depth, extra=None, after=()):
    rank = lax.axis_index("mp")
    count = len(masks)
    length = jobs[0][0].shape[0]
    rows = length // count
    part = depth // LINE
    channels = jobs[0][2][0].shape[1]
    factors_first = [job[3] for job in jobs]
    sizes = [(channels, part) if first else (part, channels) for first in factors_first]
    more = 0 if extra is None else extra.shape[1]
    own = line_place() % 2
    order = jnp.stack([1 - own, 3 - own, own, 2 + own])
    places = jnp.stack([(rank ^ mask) * rows for mask in masks])
    numbers = jnp.concatenate([order, places]).astype(jnp.int32)
    in_specs = []
    operands = [numbers]
    for rows_of, half, factors, _ in jobs:
        in_specs.append(pl.BlockSpec((length, part), lambda b, numbers_ref: (0, numbers_ref[b])))
        operands.append(rows_of)
        for other in others:
            for mask in masks:
                in_specs.append(
                    pl.BlockSpec(
                        (rows, part),
                        lambda b, numbers_ref, half=half: (0, half * LINE + numbers_ref[b]),
                    )
                )
                operands.append(other[mask])
        for factor in factors:
            in_specs.append(fixed(factor.shape))
            operands.append(factor)
    if more:
        in_specs.append(
            pl.BlockSpec((1, more, channels), lambda b, numbers_ref: (numbers_ref[b], 0, 0))
        )
        operands.append(extra)
    in_specs += [anywhere()] * len(after)
    operands += list(after)

    def kernel(numbers_ref, *refs):
        scratch = refs[-1]
        outs = refs[len(operands) - 1 : -1]
        step = pl.program_id(0)
        at = 0
        for turn, first in enumerate(factors_first):
            source = refs[at]
            at += 1
            total = None
            groups = [refs[at + g * count : at + (g + 1) * count] for g in range(len(others))]
            at += len(others) * count
            for g in range(len(others) + 1):
                if g:
                    for piece, ref in enumerate(groups[g - 1]):
                        place = pl.multiple_of(numbers_ref[LINE + piece], rows)
                        scratch[pl.ds(place, rows), :] = ref[...]
                    value = scratch[...]
                else:
                    value = source[...]
                factor = refs[at + g][...]
                pair = (factor, value) if first else (value, factor)
                term = product(*pair, TOKENS)
                total = term if total is None else total + term
            at += len(others) + 1
            total = total.astype(jnp.bfloat16)
            height = sizes[turn][0]

            @pl.when(step < LINE // 2)
            def _():
                outs[2 * turn][0, :height, :] = total

            @pl.when(step >= LINE // 2)
            def _():
                outs[2 * turn + 1][0, :height, :] = total

        if more:

            @pl.when(step < LINE // 2)
            def _():
                outs[0][0, sizes[0][0] :, :] = refs[at][0]

            @pl.when(step >= LINE // 2)
            def _():
                outs[1][0, sizes[0][0] :, :] = refs[at][0]

    early = lambda b, numbers_ref: (jnp.minimum(b, LINE // 2 - 1), 0, 0)
    late = lambda b, numbers_ref: (jnp.maximum(b - LINE // 2, 0), 0, 0)
    return pl.pallas_call(
        kernel,
        grid_spec=pltpu.PrefetchScalarGridSpec(
            num_scalar_prefetch=1,
            grid=(LINE,),
            in_specs=in_specs,
            out_specs=[
                pl.BlockSpec((1, height + more, width), index)
                for height, width in sizes
                for index in (early, late)
            ],
            scratch_shapes=[pltpu.VMEM((length, part), jnp.bfloat16)],
        ),
        out_shape=[
            jax.ShapeDtypeStruct((LINE // 2, height + more, width), jnp.bfloat16)
            for height, width in sizes
            for _ in range(2)
        ],
        compiler_params=pltpu.CompilerParams(vmem_limit_bytes=56 << 20),
        cost_estimate=estimate(4 * len(jobs)),
        name="factor_products",
    )(*operands)


def add_blocks(kept, got, bit, after):
    count, rows, width = kept.shape
    own = (line_place() // bit) % 2
    order = jnp.stack([1 - own, own]) if count == 2 else jnp.zeros((1,), jnp.int32)

    def kernel(order_ref, kept_ref, got_ref, *refs):
        total = kept_ref[...].astype(jnp.float32) + got_ref[...].astype(jnp.float32)
        total = total.astype(jnp.bfloat16)
        if count == 1:
            refs[-1][...] = total
            return
        step = pl.program_id(0)

        @pl.when(step == 0)
        def _():
            refs[-2][...] = total

        @pl.when(step == 1)
        def _():
            refs[-1][...] = total

    block = pl.BlockSpec((1, rows, width), lambda b, order_ref: (order_ref[b], 0, 0))
    result = pl.BlockSpec((1, rows, width), lambda b, order_ref: (0, 0, 0))
    return pl.pallas_call(
        kernel,
        grid_spec=pltpu.PrefetchScalarGridSpec(
            num_scalar_prefetch=1,
            grid=(count,),
            in_specs=[block, block] + [anywhere()] * len(after),
            out_specs=[result] * count,
        ),
        out_shape=[jax.ShapeDtypeStruct((1, rows, width), jnp.bfloat16)] * count,
        compiler_params=pltpu.CompilerParams(vmem_limit_bytes=40 << 20),
        cost_estimate=estimate(1),
        name="add_blocks",
    )(order.astype(jnp.int32), kept, got, *after)


def project_back(pre, w_dt, key_grad, query_grad, keys, fade, after):
    length, channels = pre.shape
    rank_width = w_dt.shape[0]
    n = keys.shape[1]
    tile = min(256, length)

    def kernel(pre_ref, w_ref, kg_ref, qg_ref, keys_ref, fade_ref, *refs):
        out_ref = refs[-1]
        out_ref[:, :rank_width] = product(pre_ref[...].astype(jnp.bfloat16), w_ref[...], ACROSS)
        spread = jnp.sum(fade_ref[...], 1, keepdims=True)
        out_ref[:, rank_width : rank_width + n] = kg_ref[...] - 2.0 * keys_ref[...] * spread
        out_ref[:, rank_width + n :] = qg_ref[...]

    rows = lambda width: pl.BlockSpec((tile, width), lambda c: (c, 0))
    return pl.pallas_call(
        kernel,
        grid=(length // tile,),
        in_specs=[rows(channels), fixed(w_dt.shape), rows(n), rows(n), rows(n), rows(128)]
        + [anywhere()] * len(after),
        out_specs=rows(rank_width + 2 * n),
        out_shape=jax.ShapeDtypeStruct((length, rank_width + 2 * n), jnp.float32),
        compiler_params=pltpu.CompilerParams(vmem_limit_bytes=40 << 20),
        cost_estimate=estimate(3),
        name="project_back",
    )(pre, w_dt, key_grad, query_grad, keys, fade, *after)


def narrow_products(low_rank, pre, proj_grad, acts, after):
    length, channels = pre.shape
    tile = min(256, channels)
    rank_width, width = low_rank.shape[1], proj_grad.shape[1]
    padding = -(rank_width + width) % (16 * LINE)
    total = rank_width + width + padding

    def kernel(low_ref, pre_ref, pg_ref, acts_ref, *refs):
        out_ref = refs[-1]
        first = product(low_ref[...], pre_ref[...].astype(jnp.bfloat16), TOKENS)
        out_ref[:rank_width, :] = first.astype(jnp.bfloat16)
        second = product(pg_ref[...], acts_ref[...].astype(jnp.bfloat16), TOKENS)
        out_ref[rank_width : rank_width + width, :] = second.astype(jnp.bfloat16)
        if padding:
            out_ref[rank_width + width :, :] = jnp.zeros((padding, tile), jnp.bfloat16)

    column = pl.BlockSpec((length, tile), lambda c: (0, c))
    return pl.pallas_call(
        kernel,
        grid=(channels // tile,),
        in_specs=[fixed(low_rank.shape), column, fixed(proj_grad.shape), column]
        + [anywhere()] * len(after),
        out_specs=pl.BlockSpec((total, tile), lambda c: (0, c)),
        out_shape=jax.ShapeDtypeStruct((total, channels), jnp.bfloat16),
        compiler_params=pltpu.CompilerParams(vmem_limit_bytes=48 << 20),
        cost_estimate=estimate(4),
        name="narrow_products",
    )(low_rank, pre, proj_grad, acts, *after)


def to_tiles(values):
    length, channels = values.shape
    parts = values.reshape(length // 8, 8, channels // 128, 128).transpose(0, 2, 1, 3)
    return parts.reshape(length // 8, channels // 16, 128)


def from_tiles(values):
    blocks, height, _ = values.shape
    parts = values.reshape(blocks, height // 8, 8, 128).transpose(0, 2, 1, 3)
    return parts.reshape(blocks * 8, height * 16)


def swap(values, axis, offset):
    size = lax.axis_size(axis)
    return lax.ppermute(values, axis, [(i, i ^ offset) for i in range(size)])


def bits_down(size):
    bits = []
    bit = size // 2
    while bit:
        bits.append(bit)
        bit //= 2
    return bits


def gather_pieces(values, axis):
    pieces = {0: values}
    for bit in bits_down(lax.axis_size(axis)):
        for mask in list(pieces):
            pieces[mask | bit] = swap(pieces[mask], axis, bit)
    return pieces


def nothing(other):
    return other[(slice(0, 1),) * other.ndim].reshape(()).astype(jnp.float32) * 0.0


def sum_mp(values, after=None):
    rank = lax.axis_index("mp")
    half = values.shape[0] // 2
    odd = rank % 2
    mine = lax.dynamic_slice_in_dim(values, odd * half, half, 0)
    other = lax.dynamic_slice_in_dim(values, (1 - odd) * half, half, 0)
    mine = mine + swap(other, "mp", 1)
    bit = 2
    while bit < lax.axis_size("mp"):
        mine = mine + swap(mine, "mp", bit)
        bit *= 2
    if after is not None:
        mine = mine + nothing(after)
    other = swap(mine, "mp", 1)
    whole = jnp.zeros(values.shape, values.dtype)
    whole = lax.dynamic_update_slice_in_dim(whole, mine, odd * half, 0)
    return lax.dynamic_update_slice_in_dim(whole, other, (1 - odd) * half, 0)


def scatter_mp(values):
    rank = lax.axis_index("mp")
    size = lax.axis_size("mp")
    rows = values.shape[0] // size
    blocks = values.reshape(1, size, rows, values.shape[1])
    bit = 1
    while bit < size:
        left, here, _, width = blocks.shape
        pairs = blocks.reshape(left, here // 2, 2, rows, width)
        own = (rank // bit) % 2
        keep = lax.dynamic_index_in_dim(pairs, own, 2, keepdims=False)
        give = lax.dynamic_index_in_dim(pairs, 1 - own, 2, keepdims=False).astype(jnp.bfloat16)
        blocks = keep.astype(jnp.float32) + swap(give, "mp", bit).astype(jnp.float32)
        bit *= 2
    return blocks.reshape(rows, values.shape[1])


def trade_side(values):
    side = lax.axis_size("dp") // LINE
    rank = lax.axis_index("dp") % side
    width = values.shape[1] // side
    parts = []
    for mask in range(side):
        part = lax.dynamic_slice_in_dim(values, (rank ^ mask) * width, width, 1)
        parts.append(swap(part, "dp", mask) if mask else part)
    return parts


def line_place():
    return lax.axis_index("dp") // (lax.axis_size("dp") // LINE)


def near_step(give, keep, after):
    side = lax.axis_size("dp") // LINE
    return add_blocks(keep, swap(give, "dp", side), 2, after)


def far_step(give, keep, after):
    side = lax.axis_size("dp") // LINE
    return add_blocks(keep, swap(give, "dp", 2 * side), 2, after)[0][0]


def spread(piece, apart=False):
    rows = piece.shape[0]
    held = [(piece, [0])]
    for bit in bits_down(lax.axis_size("dp")):
        if apart:
            parts = [[one] for one in held]
        elif len(held) > 1:
            parts = [held[:-1], held[-1:]] if bit == 1 else [held]
        else:
            parts = [held]
        for part in parts:
            masks = [mask for _, group in part for mask in group]
            arrays = [array for array, _ in part]
            sent = arrays[0] if len(arrays) == 1 else jnp.concatenate(arrays, 0)
            held.append((swap(sent, "dp", bit), [mask | bit for mask in masks]))
    table = {mask: (array, which) for array, masks in held for which, mask in enumerate(masks)}
    return table, [array for array, _ in held[1:]]


def join(pieces, rows, height, lines_first, target=None, buffer=None):
    side = lax.axis_size("dp") // LINE
    rank = lax.axis_index("dp")
    masks = list(pieces)
    count = len(masks)
    width = pieces[masks[0]][0].shape[1]
    more = rows - height
    origin = jnp.stack([rank ^ mask for mask in masks])
    line, flank = origin // side, origin % side
    down, right = (line, flank) if lines_first else (flank, line)
    grid_down, grid_right = (LINE, side) if lines_first else (side, LINE)
    shape = (height * grid_down, width * grid_right)
    low_shape = (more * grid_down, width * grid_right)
    if width % 128:
        total = jnp.zeros(shape, jnp.float32)
        low = jnp.zeros(low_shape, jnp.float32)
        for step, mask in enumerate(masks):
            array, which = pieces[mask]
            value = array[which * rows : (which + 1) * rows].astype(jnp.float32)
            right_at = right[step] * width
            total = lax.dynamic_update_slice(total, value[:height], (down[step] * height, right_at))
            if more:
                low = lax.dynamic_update_slice(low, value[height:], (down[step] * more, right_at))
        if target is not None:
            if buffer is None:
                buffer = jnp.zeros((2,) + shape, jnp.float32)
            total = lax.dynamic_update_slice(buffer, total[None], (target, 0, 0))
        return (total, low) if more else total
    places = jnp.stack([down, right]).astype(jnp.int32)

    def kernel(places_ref, *refs):
        outs = refs[-2:] if more else refs[-1:]
        step = pl.program_id(0)
        for turn in range(count):

            @pl.when(step == turn)
            def _():
                value = refs[turn][:height, :].astype(jnp.float32)
                outs[0][...] = value if target is None else value[None]
                if more:
                    outs[1][...] = refs[turn][height:, :].astype(jnp.float32)

    in_specs = [
        pl.BlockSpec((rows, width), lambda step, places_ref, which=pieces[mask][1]: (which, 0))
        for mask in masks
    ]
    operands = [places] + [pieces[mask][0] for mask in masks]
    aliases = {}
    if target is None:
        out_shapes = [jax.ShapeDtypeStruct(shape, jnp.float32)]
        out_specs = [
            pl.BlockSpec(
                (height, width),
                lambda step, places_ref: (places_ref[0, step], places_ref[1, step]),
            )
        ]
    else:
        out_shapes = [jax.ShapeDtypeStruct((2,) + shape, jnp.float32)]
        out_specs = [
            pl.BlockSpec(
                (1, height, width),
                lambda step, places_ref: (target, places_ref[0, step], places_ref[1, step]),
            )
        ]
        if buffer is not None:
            in_specs.append(pl.BlockSpec(memory_space=pl.ANY))
            operands.append(buffer)
            aliases = {len(operands) - 1: 0}
    if more:
        out_shapes.append(jax.ShapeDtypeStruct(low_shape, jnp.float32))
        out_specs.append(
            pl.BlockSpec(
                (more, width), lambda step, places_ref: (places_ref[0, step], places_ref[1, step])
            )
        )
    results = pl.pallas_call(
        kernel,
        grid_spec=pltpu.PrefetchScalarGridSpec(
            num_scalar_prefetch=1,
            grid=(count,),
            in_specs=in_specs,
            out_specs=out_specs,
        ),
        out_shape=out_shapes,
        input_output_aliases=aliases,
        compiler_params=pltpu.CompilerParams(vmem_limit_bytes=40 << 20),
        cost_estimate=estimate(count * 0.6),
        name="join",
    )(*operands)
    return results if more else results[0]


def tie(values, other):
    return values + nothing(other).astype(values.dtype)


def on_device(
    block_input,
    norm_gain,
    w_in,
    conv_w,
    conv_b,
    w_x,
    w_dt,
    b_dt,
    d_skip,
    w_out,
    out_grad,
    seq_counts,
):
    row_count, depth = block_input.shape
    size = lax.axis_size("mp")
    side = lax.axis_size("dp") // LINE
    length = row_count * size
    channels = w_in.shape[2]
    state_size = (w_x.shape[1] - R) // 2
    source_rows = block_input.astype(jnp.float32)
    inv_root = lax.rsqrt(jnp.mean(source_rows * source_rows, -1, keepdims=True) + 1e-05)
    normed = (source_rows * inv_root * norm_gain).astype(jnp.bfloat16)
    normed_pieces = gather_pieces(normed, "mp")
    masks = list(normed_pieces)
    ograd_pieces = gather_pieces(tie(out_grad, normed_pieces[masks[1]]), "mp")
    both = jnp.concatenate([normed, out_grad], 1)
    beside = [swap(both, "dp", mask) for mask in range(1, side)]
    keep_mask = boundaries(seq_counts[0], length)
    allow_two = keep_mask * shift_down(keep_mask, 1)
    allow_three = allow_two * shift_down(keep_mask, 2)
    allows = jnp.stack([keep_mask, allow_two, allow_three], 1)
    w_x_rows = w_x.T
    group_normed, inner, acts, proj_part = project_in(
        list(normed_pieces.values()),
        masks,
        w_in,
        allows,
        conv_w,
        conv_b,
        w_x_rows,
    )
    group_ograd, gate_silu, mixer_grad, gate_slope = project_gate(
        list(ograd_pieces.values()), list(ograd_pieces), group_normed, w_in, w_out, beside
    )
    proj = sum_mp(proj_part, gate_silu)
    others = []
    for rows in beside:
        others.append(gather_pieces(tie(rows, proj), "mp"))
    low_rank = proj[:, :R].astype(jnp.bfloat16)
    keys = proj[:, R : R + state_size]
    queries = proj[:, R + state_size :]
    beta = jax.nn.sigmoid(product(low_rank, w_dt) + b_dt)
    key_square = jnp.sum(keys * keys, 1)
    step_size = beta / (1.0 + beta * key_square[:, None])
    scalars = jnp.concatenate(
        [keys.reshape(-1), queries.reshape(-1), key_square, keep_mask[::8]]
    )
    step_tiles = to_tiles(step_size)
    acts_tiles = to_tiles(acts)
    mix_tiles, states = scan_forward(
        scalars,
        step_tiles,
        acts_tiles,
        CHUNK,
        state_size,
        (gate_silu, gate_slope),
    )
    mixer = from_tiles(mix_tiles) + d_skip * acts
    gated = (mixer * gate_silu).astype(jnp.bfloat16)
    gate_grad = (mixer * gate_slope).astype(jnp.bfloat16)
    back_args = (
        scalars,
        step_tiles,
        acts_tiles,
        to_tiles(mixer_grad),
        states,
        d_skip.astype(jnp.float32).reshape(channels // 128, 128),
        CHUNK,
        state_size,
    )
    chunks = length // CHUNK
    fetched = [rows[masks[1]] for rows in others]
    later = scan_backward(*back_args, (chunks // 2, chunks), None, [gated, gate_grad] + fetched)
    gate_job = (group_normed, 0, trade_side(gate_grad), False)
    out_job = (group_ograd, 1, trade_side(gated), True)
    gate_give, gate_keep, out_give, out_keep = factor_products(
        [gate_job, out_job], others, masks, depth, None, (later[6],)
    )
    pre_tiles, agrad_tiles, key_grad, query_grad, fade, sums, _ = scan_backward(
        *back_args, (0, chunks // 2), later, (gate_give, out_give)
    )
    pre_full = from_tiles(pre_tiles)
    gate_give, gate_keep = near_step(gate_give, gate_keep, (fade,))
    proj_back = project_back(pre_full, w_dt, key_grad, query_grad, keys, fade, (gate_give,))
    out_give, out_keep = near_step(out_give, out_keep, (proj_back,))
    proj_grad = sum_mp(proj_back).astype(jnp.bfloat16)
    gate_piece = far_step(gate_give, gate_keep, ())
    gate_pieces, gate_came = spread(gate_piece)
    inner_grad, conv_sums = finish_inner(
        from_tiles(agrad_tiles),
        proj_grad,
        w_x_rows,
        inner,
        allows,
        conv_w,
        conv_b,
        (out_give, gate_piece),
    )
    inner_parts = trade_side(inner_grad)
    out_piece = far_step(out_give, out_keep, (inner_grad,))
    out_pieces, out_came = spread(out_piece)
    narrow = narrow_products(low_rank, pre_full, proj_grad, acts, (inner_grad,))
    branch_out = scatter_mp(product(tie(gated, inner_grad), w_out))
    block_out = (source_rows + branch_out).astype(jnp.bfloat16)
    extra = sum((part.astype(jnp.float32) for part in trade_side(narrow))).astype(jnp.bfloat16)
    width = channels // side
    tall = narrow.shape[0] // LINE
    extra = extra.reshape(LINE, tall, width)
    inner_job = (group_normed, 0, inner_parts, False)
    inner_give, inner_keep = factor_products([inner_job], others, masks, depth, extra)
    w_in_grad = join(gate_pieces, depth // LINE, depth // LINE, True, 1)
    w_out_grad = join(out_pieces, width, width, False)
    inner_give, inner_keep = near_step(inner_give, inner_keep, (out_piece, gate_came[0]))
    inner_piece = far_step(inner_give, inner_keep, gate_came[1:3] + out_came[:1])
    normed_grad = scatter_mp(
        product(inner_grad, w_in[0], ACROSS) + product(gate_grad, w_in[1], ACROSS)
    )
    scaled = normed_grad * norm_gain
    gain_part = jnp.sum(normed_grad * source_rows * inv_root, 0)
    cubed = inv_root * inv_root * inv_root
    input_grad = inv_root * scaled - source_rows * cubed * jnp.mean(
        scaled * source_rows, -1, keepdims=True
    )
    input_grad = (out_grad.astype(jnp.float32) + input_grad).astype(jnp.bfloat16)
    for bit in bits_down(size):
        gain_part = gain_part + swap(gain_part, "mp", bit)
    partial = [conv_sums[:5].reshape(-1), sums.reshape(-1), gain_part]
    partial = jnp.concatenate([value.astype(jnp.bfloat16) for value in partial])
    used = partial.shape[0]
    count = -(-used // (16 * width)) * 16
    partial = jnp.concatenate([partial, jnp.zeros(count * width - used, jnp.bfloat16)])
    tail = jnp.concatenate([inner_piece, partial.reshape(count, width)], 0)
    pieces, _ = spread(tail, True)
    w_in_grad, low = join(pieces, tail.shape[0], depth // LINE, True, 0, w_in_grad)
    low = low.reshape(LINE, -1, channels)
    narrow = low[:, :tall].reshape(LINE * tall, channels)
    total = low[:, tall : tall + count].reshape(LINE, count, side, width)
    total = jnp.sum(total, (0, 2)).reshape(-1)
    return (
        block_out,
        input_grad,
        total[7 * channels : used],
        w_in_grad,
        total[: 4 * channels].reshape(4, channels),
        total[4 * channels : 5 * channels],
        narrow[R : 2 * R + 2 * state_size].T,
        narrow[:R],
        total[5 * channels : 6 * channels],
        total[6 * channels : 7 * channels],
        w_out_grad,
    )


def solution(mesh):
    in_specs = (
        P(("dp", "mp"), None),
        P(),
        P(None, None, "mp"),
        P(None, "mp"),
        P("mp"),
        P("mp", None),
        P(None, "mp"),
        P("mp"),
        P("mp"),
        P("mp", None),
        P(("dp", "mp"), None),
        P("dp", None),
    )
    out_specs = (
        P(("dp", "mp"), None),
        P(("dp", "mp"), None),
        P(),
        P(None, None, "mp"),
        P(None, "mp"),
        P("mp"),
        P("mp", None),
        P(None, "mp"),
        P("mp"),
        P("mp"),
        P("mp", None),
    )
    return jax.shard_map(
        on_device, mesh=mesh, in_specs=in_specs, out_specs=out_specs, check_vma=False
    )
```

```python
import jax
import jax.numpy as jnp
from jax import lax
from jax.experimental import pallas as pl
from jax.experimental.pallas import tpu as pltpu
from jax.sharding import PartitionSpec as P

R = 128
CHUNK = 64
LINE = 4

def boundaries(bucket_row, length):
    position = jnp.arange(length, dtype=jnp.int32)
    short_len = length // 16
    middle_len = length // 4
    short_end = bucket_row[2] * short_len
    middle_end = short_end + bucket_row[1] * middle_len
    first_short = (position < short_end) & (position % short_len == 0)
    first_middle = (
        (position >= short_end)
        & (position < middle_end)
        & ((position - short_end) % middle_len == 0)
    )
    first_long = (position == middle_end) & (position < length)
    opening = first_short | first_middle | first_long
    return jnp.where(opening, 0.0, 1.0).astype(jnp.float32)


def shift_down(values, lag):
    return jnp.concatenate([jnp.zeros((lag,) + values.shape[1:], values.dtype), values[:-lag]], 0)


def estimate(micros):
    return pl.CostEstimate(flops=1, bytes_accessed=1, transcendentals=0)


TOKENS = (((0,), (0,)), ((), ()))
ACROSS = (((1,), (1,)), ((), ()))


def product(left, right, dims=(((1,), (0,)), ((), ()))):
    return lax.dot_general(left, right, dims, preferred_element_type=jnp.float32)


def fixed(shape):
    return pl.BlockSpec(shape, lambda *_: (0,) * len(shape), pipeline_mode=pl.Buffered(1))


def anywhere():
    return pl.BlockSpec(memory_space=pl.ANY)


def whole(shape):
    return pl.BlockSpec(shape, lambda *_: (0,) * len(shape))


def row_sums(values):
    if values[0].shape[0] != 8:
        return jnp.concatenate([jnp.sum(value, 0, keepdims=True) for value in values], 0)
    row = lax.broadcasted_iota(jnp.int32, (8, 128), 0)
    span = 1
    while len(values) > 1:
        low = (row // span) % 2 == 0
        values = [
            jnp.where(low, a, b) + pltpu.roll(jnp.where(low, b, a), 8 - span, axis=0)
            for a, b in zip(values[0::2], values[1::2])
        ]
        span *= 2
    return values[0]


def forward_kernel(chunk, n, length, scalars, step_ref, acts_ref, mix_ref, states_ref, carry):
    index = pl.program_id(0)
    tiles = carry.shape[1]

    @pl.when(index == 0)
    def _():
        carry[...] = jnp.zeros_like(carry)

    def eight(block, state):
        keep = scalars[(2 * n + 1) * length + index * (chunk // 8) + block]
        state = [value * keep for value in state]
        for i in range(8):
            rows = pl.ds(i, tiles, stride=8)
            step = step_ref[block, rows, :]
            act = acts_ref[block, rows, :]
            token = block * 8 + i
            base = (index * chunk + token) * n
            total = None
            for j in range(n):
                k = scalars[base + j]
                state[j] = state[j] + (step * k) * (act - state[j] * k)
                states_ref[token, j] = state[j]
                part = state[j] * scalars[n * length + base + j]
                total = part if total is None else total + part
            mix_ref[block, rows, :] = total
        return tuple(state)

    final = lax.fori_loop(0, chunk // 8, eight, tuple(carry[j] for j in range(n)))
    for j in range(n):
        carry[j] = final[j]


def scan_forward(values, step, acts, chunk, n, after):
    blocks, height, _ = step.shape
    tiles = height // 8
    length = blocks * 8
    wide = pl.BlockSpec((chunk // 8, height, 128), lambda c: (c, 0, 0))
    scalars = pl.BlockSpec(memory_space=pltpu.SMEM)
    return pl.pallas_call(
        lambda *refs: forward_kernel(
            chunk, n, length, *refs[:3], *refs[3 + len(after) :]
        ),
        grid=(length // chunk,),
        in_specs=[scalars, wide, wide] + [anywhere()] * len(after),
        out_specs=[wide, pl.BlockSpec((chunk, n, tiles, 128), lambda c: (c, 0, 0, 0))],
        out_shape=[
            jax.ShapeDtypeStruct(step.shape, jnp.float32),
            jax.ShapeDtypeStruct((length, n, tiles, 128), jnp.float32),
        ],
        scratch_shapes=[pltpu.VMEM((n, tiles, 128), jnp.float32)],
        compiler_params=pltpu.CompilerParams(vmem_limit_bytes=48 << 20),
        cost_estimate=estimate(16),
        name="scan_forward",
    )(values, step, acts, *after)


def backward_kernel(
    chunk,
    n,
    last,
    carry_in,
    sums_in,
    length,
    scalars,
    step_ref,
    acts_ref,
    ygrad_ref,
    states_ref,
    prior_ref,
    skip_ref,
    pre_ref,
    agrad_ref,
    kgrad_ref,
    qgrad_ref,
    fade_ref,
    sums_ref,
    carry,
    kred,
    qred,
):
    order = pl.program_id(0)
    index = last - order
    tiles = carry.shape[1]

    @pl.when(order == 0)
    def _():
        if carry_in is None:
            carry[...] = jnp.zeros_like(carry)
            sums_ref[...] = jnp.zeros_like(sums_ref)
        else:
            carry[...] = carry_in[...]
            sums_ref[...] = sums_in[...]

    skip = skip_ref[...]

    def token_step(block, i, adjoint, prior_of):
        rows = pl.ds(i, tiles, stride=8)
        step = step_ref[block, rows, :]
        act = acts_ref[block, rows, :]
        ygrad = ygrad_ref[block, rows, :]
        token = block * 8 + i
        where = index * chunk + token
        base = where * n
        drive = None
        loss = None
        kparts = []
        qparts = []
        for j in range(n):
            k = scalars[base + j]
            adj = adjoint[j] + ygrad * scalars[n * length + base + j]
            prior = prior_of(token, j)
            ka = adj * k
            kp = prior * k
            kparts.append((step * adj) * (act - (kp + kp)))
            qparts.append(states_ref[token, j] * ygrad)
            part = ka * kp
            drive = ka if drive is None else drive + ka
            loss = part if loss is None else loss + part
            adjoint[j] = adj - (step * k) * ka
        step_grad = act * drive - loss
        scaled = step_grad * step
        pre = scaled * (1.0 - step * (1.0 + scalars[2 * n * length + where]))
        pre_ref[block, rows, :] = pre
        agrad_ref[block, rows, :] = step * drive + ygrad * skip
        sums_ref[0] += pre.astype(jnp.bfloat16).astype(jnp.float32)
        sums_ref[1] += ygrad * act
        for first in range(0, n, 8):
            kred[token, first : first + 8, :] = row_sums(kparts[first : first + 8])
            qred[token, first : first + 8, :] = row_sums(qparts[first : first + 8])
        return scaled * step

    def eight(turn, adjoint):
        block = chunk // 8 - 1 - turn
        adjoint = list(adjoint)
        keep = scalars[(2 * n + 1) * length + index * (chunk // 8) + block]
        fades = [None] * 8
        for i in range(7, 0, -1):
            fades[i] = token_step(block, i, adjoint, lambda token, j: states_ref[token - 1, j])
        first = block == 0
        back = jnp.maximum(block * 8 - 1, 0)
        fades[0] = token_step(
            block,
            0,
            adjoint,
            lambda token, j: jnp.where(first, prior_ref[0, j], states_ref[back, j]) * keep,
        )
        fade_ref[pl.ds(pl.multiple_of(block * 8, 8), 8), :] = row_sums(fades)
        return tuple(value * keep for value in adjoint)

    final = lax.fori_loop(0, chunk // 8, eight, tuple(carry[j] for j in range(n)))
    for j in range(n):
        carry[j] = final[j]
    kgrad_ref[...] = jnp.sum(kred[...], -1)
    qgrad_ref[...] = jnp.sum(qred[...], -1)


def scan_backward(
    values, step, acts, ygrad, states, skip, chunk, n, span, before, after
):
    blocks, height, _ = step.shape
    tiles = height // 8
    length = blocks * 8
    last = span[1] - 1
    wide = pl.BlockSpec((chunk // 8, height, 128), lambda c: (last - c, 0, 0))
    scalars = pl.BlockSpec(memory_space=pltpu.SMEM)
    narrow = pl.BlockSpec((chunk, n), lambda c: (last - c, 0))
    kept = pl.BlockSpec((n, tiles, 128), lambda c: (0, 0, 0))
    pair = pl.BlockSpec((2, tiles, 128), lambda c: (0, 0, 0))
    in_specs = [
        scalars,
        wide,
        wide,
        wide,
        pl.BlockSpec((chunk, n, tiles, 128), lambda c: (last - c, 0, 0, 0)),
        pl.BlockSpec(
            (1, n, tiles, 128), lambda c: (jnp.maximum((last - c) * chunk - 1, 0), 0, 0, 0)
        ),
        pl.BlockSpec((tiles, 128), lambda c: (0, 0)),
    ]
    operands = [values, step, acts, ygrad, states, states, skip]
    aliases = {}
    base = len(operands)
    if before is not None:
        in_specs += [pair, kept] + [anywhere()] * 5
        operands += [before[5], before[6]] + list(before[:5])
        aliases = {base + 2 + turn: turn for turn in range(5)}
    in_specs += [anywhere()] * len(after)
    operands += list(after)

    def kernel(*refs):
        sums_in, carry_in = refs[base : base + 2] if before is not None else (None, None)
        outs = refs[len(operands) :]
        backward_kernel(
            chunk, n, last, carry_in, sums_in, length, *refs[:base], *outs[:6], *outs[6:]
        )

    return pl.pallas_call(
        kernel,
        grid=(span[1] - span[0],),
        in_specs=in_specs,
        out_specs=[
            wide,
            wide,
            narrow,
            narrow,
            pl.BlockSpec((chunk, 128), lambda c: (last - c, 0)),
            pair,
            kept,
        ],
        out_shape=[jax.ShapeDtypeStruct(step.shape, jnp.float32)] * 2
        + [jax.ShapeDtypeStruct((length, n), jnp.float32)] * 2
        + [
            jax.ShapeDtypeStruct((length, 128), jnp.float32),
            jax.ShapeDtypeStruct((2, tiles, 128), jnp.float32),
            jax.ShapeDtypeStruct((n, tiles, 128), jnp.float32),
        ],
        scratch_shapes=[
            pltpu.VMEM((chunk, n, 128), jnp.float32),
            pltpu.VMEM((chunk, n, 128), jnp.float32),
        ],
        input_output_aliases=aliases,
        compiler_params=pltpu.CompilerParams(vmem_limit_bytes=48 << 20),
        cost_estimate=estimate(32 * chunk * (span[1] - span[0]) / length),
        name="scan_backward",
    )(*operands)


def taps_of(inner, allows):
    return [inner] + [
        pltpu.roll(inner, lag, axis=0) * allows[:, lag - 1 : lag] for lag in range(1, 4)
    ]


def project_in(pieces, masks, w_in, allows, conv_w, conv_b, w_x_rows):
    rank = lax.axis_index("mp")
    rows, depth = pieces[0].shape
    count = len(pieces)
    length = rows * count
    channels = w_in.shape[2]
    tile = min(256, channels)
    width = w_x_rows.shape[0]
    places = jnp.stack([(rank ^ mask) * rows for mask in masks]).astype(jnp.int32)

    def kernel(places_ref, *refs):
        sources = refs[:count]
        w_ref, allow_ref, cw_ref, cb_ref, wx_ref = refs[count : count + 5]
        normed_ref, inner_ref, acts_ref, proj_ref = refs[count + 5 :]
        step = pl.program_id(0)

        @pl.when(step == 0)
        def _():
            for turn in range(count):
                at = pl.multiple_of(places_ref[turn], rows)
                normed_ref[pl.ds(at, rows), :] = sources[turn][...]
            proj_ref[...] = jnp.zeros_like(proj_ref)

        inner = jnp.dot(normed_ref[...], w_ref[0], preferred_element_type=jnp.float32)
        inner_ref[...] = inner
        weights = cw_ref[...].astype(jnp.float32)
        pre = cb_ref[...].astype(jnp.float32)
        for lag, tap in enumerate(taps_of(inner, allow_ref[...])):
            pre = pre + weights[lag : lag + 1] * tap
        acts = (pre * jax.nn.sigmoid(pre)).astype(jnp.bfloat16)
        acts_ref[...] = acts.astype(jnp.float32)
        proj_ref[...] += product(acts, wx_ref[...], ACROSS)

    column = pl.BlockSpec((length, tile), lambda c, places_ref: (0, c))
    return pl.pallas_call(
        kernel,
        grid_spec=pltpu.PrefetchScalarGridSpec(
            num_scalar_prefetch=1,
            grid=(channels // tile,),
            in_specs=[fixed((rows, depth))] * count
            + [
                pl.BlockSpec((1, depth, tile), lambda c, places_ref: (0, 0, c)),
                fixed(allows.shape),
                pl.BlockSpec((4, tile), lambda c, places_ref: (0, c)),
                pl.BlockSpec((1, tile), lambda c, places_ref: (0, c)),
                pl.BlockSpec((width, tile), lambda c, places_ref: (0, c)),
            ],
            out_specs=[whole((length, depth)), column, column, whole((length, width))],
        ),
        out_shape=[
            jax.ShapeDtypeStruct((length, depth), jnp.bfloat16),
            jax.ShapeDtypeStruct((length, channels), jnp.float32),
            jax.ShapeDtypeStruct((length, channels), jnp.float32),
            jax.ShapeDtypeStruct((length, width), jnp.float32),
        ],
        compiler_params=pltpu.CompilerParams(vmem_limit_bytes=56 << 20),
        cost_estimate=estimate(8),
        name="project_in",
    )(places, *pieces, w_in, allows, conv_w, conv_b.reshape(1, -1), w_x_rows)


def project_gate(pieces, masks, normed, w_in, w_out, after):
    rank = lax.axis_index("mp")
    rows, depth = pieces[0].shape
    count = len(pieces)
    length = rows * count
    channels = w_in.shape[2]
    tile = min(256, channels)
    places = jnp.stack([(rank ^ mask) * rows for mask in masks]).astype(jnp.int32)

    def kernel(places_ref, *refs):
        sources = refs[:count]
        normed_ref, w_ref, wo_ref = refs[count : count + 3]
        ograd_ref, silu_ref, grad_ref, slope_ref = refs[-4:]

        @pl.when(pl.program_id(0) == 0)
        def _():
            for turn in range(count):
                at = pl.multiple_of(places_ref[turn], rows)
                ograd_ref[pl.ds(at, rows), :] = sources[turn][...]

        gate = product(normed_ref[...], w_ref[0])
        gated_rows = product(ograd_ref[...], wo_ref[...], ACROSS)
        sig = jax.nn.sigmoid(gate)
        silu = gate * sig
        silu_ref[...] = silu
        grad_ref[...] = gated_rows * silu
        slope_ref[...] = gated_rows * sig * (1.0 + gate * (1.0 - sig))

    column = pl.BlockSpec((length, tile), lambda c, places_ref: (0, c))
    return pl.pallas_call(
        kernel,
        grid_spec=pltpu.PrefetchScalarGridSpec(
            num_scalar_prefetch=1,
            grid=(channels // tile,),
            in_specs=[fixed((rows, depth))] * count
            + [
                fixed((length, depth)),
                pl.BlockSpec((1, depth, tile), lambda c, places_ref: (1, 0, c)),
                pl.BlockSpec((tile, depth), lambda c, places_ref: (c, 0)),
            ]
            + [anywhere()] * len(after),
            out_specs=[whole((length, depth)), column, column, column],
        ),
        out_shape=[jax.ShapeDtypeStruct((length, depth), jnp.bfloat16)]
        + [jax.ShapeDtypeStruct((length, channels), jnp.float32)] * 3,
        compiler_params=pltpu.CompilerParams(vmem_limit_bytes=60 << 20),
        cost_estimate=estimate(11),
        name="project_gate",
    )(places, *pieces, normed, w_in, w_out, *after)


def finish_inner(agrad, proj_grad, w_x_rows, inner, allows, conv_w, conv_b, after):
    length, channels = inner.shape
    tile = min(256, channels)
    width = w_x_rows.shape[0]

    def kernel(ag_ref, pg_ref, wx_ref, inner_ref, allow_ref, cw_ref, cb_ref, *refs):
        out_ref, sums_ref = refs[-2:]
        acts_grad = ag_ref[...] + product(pg_ref[...], wx_ref[...])
        allow = allow_ref[...]
        taps = taps_of(inner_ref[...], allow)
        weights = cw_ref[...].astype(jnp.float32)
        pre = cb_ref[...].astype(jnp.float32)
        for lag, tap in enumerate(taps):
            pre = pre + weights[lag : lag + 1] * tap
        sig = jax.nn.sigmoid(pre)
        conv_grad = acts_grad * sig * (1.0 + pre * (1.0 - sig))
        rows = [jnp.sum(conv_grad * tap, 0, keepdims=True) for tap in taps]
        rows.append(jnp.sum(conv_grad, 0, keepdims=True))
        sums_ref[...] = jnp.concatenate(rows + [jnp.zeros((3, tile), jnp.float32)], 0)
        total = weights[0:1] * conv_grad
        for lag in range(1, 4):
            sent = conv_grad * allow[:, lag - 1 : lag] * weights[lag : lag + 1]
            total = total + pltpu.roll(sent, length - lag, axis=0)
        out_ref[...] = total.astype(jnp.bfloat16)

    column = pl.BlockSpec((length, tile), lambda c: (0, c))
    return pl.pallas_call(
        kernel,
        grid=(channels // tile,),
        in_specs=[
            column,
            fixed((length, width)),
            pl.BlockSpec((width, tile), lambda c: (0, c)),
            column,
            fixed(allows.shape),
            pl.BlockSpec((4, tile), lambda c: (0, c)),
            pl.BlockSpec((1, tile), lambda c: (0, c)),
        ]
        + [anywhere()] * len(after),
        out_specs=[column, pl.BlockSpec((8, tile), lambda c: (0, c))],
        out_shape=[
            jax.ShapeDtypeStruct((length, channels), jnp.bfloat16),
            jax.ShapeDtypeStruct((8, channels), jnp.float32),
        ],
        compiler_params=pltpu.CompilerParams(vmem_limit_bytes=56 << 20),
        cost_estimate=estimate(6),
        name="finish_inner",
    )(agrad, proj_grad, w_x_rows, inner, allows, conv_w, conv_b.reshape(1, -1), *after)


def factor_products(jobs, others, masks, depth, stacked, extra=None, after=()):
    rank = lax.axis_index("mp")
    count = len(masks)
    length = jobs[0][0].shape[0]
    rows = length // count
    part = depth // LINE
    channels = jobs[0][2][0].shape[1]
    factors_first = [job[3] for job in jobs]
    places = jnp.stack([(rank ^ mask) * rows for mask in masks]).astype(jnp.int32)
    in_specs = []
    operands = [places]
    for rows_of, half, factors, _ in jobs:
        in_specs.append(pl.BlockSpec((length, part), lambda b, _: (0, b)))
        operands.append(rows_of)
        for other in others:
            for mask in masks:
                in_specs.append(
                    pl.BlockSpec(
                        (rows, part),
                        lambda b, _, half=half: (0, half * LINE + b),
                    )
                )
                operands.append(other[mask])
        for factor in factors:
            in_specs.append(fixed(factor.shape))
            operands.append(factor)
    more = 0 if extra is None else extra.shape[1]
    if more:
        in_specs.append(pl.BlockSpec((1, more, channels), lambda b, _: (b, 0, 0)))
        operands.append(extra)
    in_specs += [anywhere()] * len(after)
    operands += list(after)

    def kernel(places_ref, *refs):
        scratch = refs[-1]
        outs = refs[len(operands) - 1 : -1]

        at = 0
        for turn, first in enumerate(factors_first):
            source = refs[at]
            at += 1
            total = None
            groups = [refs[at + g * count : at + (g + 1) * count] for g in range(len(others))]
            at += len(others) * count
            for g in range(len(others) + 1):
                if g:
                    for piece, ref in enumerate(groups[g - 1]):
                        place = pl.multiple_of(places_ref[piece], rows)
                        scratch[pl.ds(place, rows), :] = ref[...]
                    value = scratch[...]
                else:
                    value = source[...]
                factor = refs[at + g][...]
                pair = (factor, value) if first else (value, factor)
                term = product(*pair, TOKENS)
                total = term if total is None else total + term
            at += len(others) + 1
            if stacked:
                outs[0][0, turn] = total.astype(jnp.bfloat16)
            elif more:
                outs[0][0, :part, :] = total.astype(jnp.bfloat16)
                outs[0][0, part:, :] = refs[at][0]
            else:
                outs[turn][...] = total.astype(jnp.bfloat16)

    if stacked:
        out_specs = [pl.BlockSpec((1, len(jobs), part, part), lambda b, _: (b, 0, 0, 0))]
        out_shape = [jax.ShapeDtypeStruct((LINE, len(jobs), part, part), jnp.bfloat16)]
    elif more:
        out_specs = [pl.BlockSpec((1, part + more, channels), lambda b, _: (b, 0, 0))]
        out_shape = [jax.ShapeDtypeStruct((LINE, part + more, channels), jnp.bfloat16)]
    else:
        out_specs = [
            pl.BlockSpec((channels, part), lambda b, _: (0, b))
            if first
            else pl.BlockSpec((part, channels), lambda b, _: (b, 0))
            for first in factors_first
        ]
        out_shape = [
            jax.ShapeDtypeStruct(
                (channels, depth) if first else (depth, channels), jnp.bfloat16
            )
            for first in factors_first
        ]
    return pl.pallas_call(
        kernel,
        grid_spec=pltpu.PrefetchScalarGridSpec(
            num_scalar_prefetch=1,
            grid=(LINE,),
            in_specs=in_specs,
            out_specs=out_specs,
            scratch_shapes=[pltpu.VMEM((length, part), jnp.bfloat16)],
        ),
        out_shape=out_shape,
        compiler_params=pltpu.CompilerParams(vmem_limit_bytes=56 << 20),
        cost_estimate=estimate(5 * len(jobs)),
        name="factor_products",
    )(*operands)


def touch(values, after):
    return pl.pallas_call(
        lambda *refs: None,
        in_specs=[anywhere()] * (1 + len(after)),
        out_specs=anywhere(),
        out_shape=jax.ShapeDtypeStruct(values.shape, values.dtype),
        input_output_aliases={0: 0},
        name="touch",
    )(values, *after)


def project_back(pre, w_dt, key_grad, query_grad, keys, fade, after):
    length, channels = pre.shape
    rank_width = w_dt.shape[0]
    n = keys.shape[1]
    tile = min(256, length)

    def kernel(pre_ref, w_ref, kg_ref, qg_ref, keys_ref, fade_ref, *refs):
        out_ref = refs[-1]
        out_ref[:, :rank_width] = product(pre_ref[...].astype(jnp.bfloat16), w_ref[...], ACROSS)
        spread = jnp.sum(fade_ref[...], 1, keepdims=True)
        out_ref[:, rank_width : rank_width + n] = kg_ref[...] - 2.0 * keys_ref[...] * spread
        out_ref[:, rank_width + n :] = qg_ref[...]

    rows = lambda width: pl.BlockSpec((tile, width), lambda c: (c, 0))
    return pl.pallas_call(
        kernel,
        grid=(length // tile,),
        in_specs=[rows(channels), fixed(w_dt.shape), rows(n), rows(n), rows(n), rows(128)]
        + [anywhere()] * len(after),
        out_specs=rows(rank_width + 2 * n),
        out_shape=jax.ShapeDtypeStruct((length, rank_width + 2 * n), jnp.float32),
        compiler_params=pltpu.CompilerParams(vmem_limit_bytes=40 << 20),
        cost_estimate=estimate(3),
        name="project_back",
    )(pre, w_dt, key_grad, query_grad, keys, fade, *after)


def narrow_products(low_rank, pre, proj_grad, acts, conv_sums, sums):
    length, channels = pre.shape
    tile = min(256, channels)
    rank_width, width = low_rank.shape[1], proj_grad.shape[1]
    used = rank_width + width
    total = used + 32

    def kernel(low_ref, pre_ref, pg_ref, acts_ref, conv_ref, sums_ref, out_ref):
        first = product(low_ref[...], pre_ref[...].astype(jnp.bfloat16), TOKENS)
        out_ref[:rank_width, :] = first.astype(jnp.bfloat16)
        second = product(pg_ref[...], acts_ref[...].astype(jnp.bfloat16), TOKENS)
        out_ref[rank_width:used, :] = second.astype(jnp.bfloat16)
        rows = jnp.concatenate(
            [conv_ref[...], sums_ref[...], jnp.zeros((22, tile), jnp.float32)], 0
        )
        out_ref[used:, :] = rows.astype(jnp.bfloat16)

    column = lambda height: pl.BlockSpec((height, tile), lambda c: (0, c))
    return pl.pallas_call(
        kernel,
        grid=(channels // tile,),
        in_specs=[
            fixed(low_rank.shape),
            column(length),
            fixed(proj_grad.shape),
            column(length),
            column(8),
            column(2),
        ],
        out_specs=column(total),
        out_shape=jax.ShapeDtypeStruct((total, channels), jnp.bfloat16),
        compiler_params=pltpu.CompilerParams(vmem_limit_bytes=48 << 20),
        cost_estimate=estimate(4),
        name="narrow_products",
    )(low_rank, pre, proj_grad, acts, conv_sums, sums)


def project_normed(inner_grad, gate_grad, w_in, after):
    length, channels = inner_grad.shape
    depth = w_in.shape[1]
    tile = min(512, depth)
    height = min(512, length)

    def kernel(inner_ref, gate_ref, w_ref, *refs):
        refs[-1][...] = product(inner_ref[...], w_ref[0], ACROSS) + product(
            gate_ref[...], w_ref[1], ACROSS
        )

    rows = pl.BlockSpec((height, channels), lambda c, r: (r, 0))
    return pl.pallas_call(
        kernel,
        grid=(depth // tile, length // height),
        in_specs=[rows, rows, pl.BlockSpec((2, tile, channels), lambda c, r: (0, c, 0))]
        + [anywhere()] * len(after),
        out_specs=pl.BlockSpec((height, tile), lambda c, r: (r, c)),
        out_shape=jax.ShapeDtypeStruct((length, depth), jnp.float32),
        compiler_params=pltpu.CompilerParams(vmem_limit_bytes=48 << 20),
        cost_estimate=estimate(6),
        name="project_normed",
    )(inner_grad, gate_grad, w_in, *after)


def put_rows(values, rows, at):
    height, width = rows.shape

    def kernel(rows_ref, values_ref, out_ref):
        out_ref[0] = rows_ref[...]

    return pl.pallas_call(
        kernel,
        grid=(1,),
        in_specs=[whole((height, width)), anywhere()],
        out_specs=pl.BlockSpec((1, height, width), lambda c: (0, at // height, 0)),
        out_shape=jax.ShapeDtypeStruct(values.shape, values.dtype),
        input_output_aliases={1: 0},
        name="put_rows",
    )(rows, values)


def to_tiles(values):
    length, channels = values.shape
    parts = values.reshape(length // 8, 8, channels // 128, 128).transpose(0, 2, 1, 3)
    return parts.reshape(length // 8, channels // 16, 128)


def from_tiles(values):
    blocks, height, _ = values.shape
    parts = values.reshape(blocks, height // 8, 8, 128).transpose(0, 2, 1, 3)
    return parts.reshape(blocks * 8, height * 16)


def swap(values, axis, offset):
    size = lax.axis_size(axis)
    return lax.ppermute(values, axis, [(i, i ^ offset) for i in range(size)])


def bits_down(size):
    bits = []
    bit = size // 2
    while bit:
        bits.append(bit)
        bit //= 2
    return bits


def gather_pieces(values, axis):
    pieces = {0: values}
    for bit in bits_down(lax.axis_size(axis)):
        for mask in list(pieces):
            pieces[mask | bit] = swap(pieces[mask], axis, bit)
    return pieces


def nothing(other):
    return other[(slice(0, 1),) * other.ndim].reshape(()).astype(jnp.float32) * 0.0


def sum_mp(values, after=None):
    rank = lax.axis_index("mp")
    half = values.shape[0] // 2
    odd = rank % 2
    mine = lax.dynamic_slice_in_dim(values, odd * half, half, 0)
    other = lax.dynamic_slice_in_dim(values, (1 - odd) * half, half, 0)
    mine = mine + swap(other, "mp", 1)
    bit = 2
    while bit < lax.axis_size("mp"):
        mine = mine + swap(mine, "mp", bit)
        bit *= 2
    if after is not None:
        mine = mine + nothing(after)
    other = swap(mine, "mp", 1)
    whole = jnp.zeros(values.shape, values.dtype)
    whole = lax.dynamic_update_slice_in_dim(whole, mine, odd * half, 0)
    return lax.dynamic_update_slice_in_dim(whole, other, (1 - odd) * half, 0)


def scatter_mp(values):
    rank = lax.axis_index("mp")
    size = lax.axis_size("mp")
    rows = values.shape[0] // size
    blocks = values.reshape(1, size, rows, values.shape[1])
    bit = 1
    while bit < size:
        left, here, _, width = blocks.shape
        pairs = blocks.reshape(left, here // 2, 2, rows, width)
        own = (rank // bit) % 2
        keep = lax.dynamic_index_in_dim(pairs, own, 2, keepdims=False)
        give = lax.dynamic_index_in_dim(pairs, 1 - own, 2, keepdims=False).astype(jnp.bfloat16)
        blocks = keep.astype(jnp.float32) + swap(give, "mp", bit).astype(jnp.float32)
        bit *= 2
    return blocks.reshape(rows, values.shape[1])


def trade_side(values):
    side = lax.axis_size("dp") // LINE
    rank = lax.axis_index("dp") % side
    width = values.shape[1] // side
    parts = []
    for mask in range(side):
        part = lax.dynamic_slice_in_dim(values, (rank ^ mask) * width, width, 1)
        parts.append(swap(part, "dp", mask) if mask else part)
    return parts


def line_groups():
    side = lax.axis_size("dp") // LINE
    return [[z * side + x for z in range(LINE)] for x in range(side)]


def scatter_line(values):
    return lax.psum_scatter(
        values, "dp", scatter_dimension=0, tiled=True, axis_index_groups=line_groups()
    )


def gather_line(values):
    return lax.all_gather(values, "dp", axis=0, tiled=True, axis_index_groups=line_groups())


def side_pieces(values):
    pieces = {0: values}
    for bit in bits_down(lax.axis_size("dp") // LINE):
        for mask in list(pieces):
            pieces[mask | bit] = swap(pieces[mask], "dp", bit)
    return pieces


def join_blocks(pieces, tall, place, shape, buffer=None):
    side = lax.axis_size("dp") // LINE
    rank = lax.axis_index("dp") % side
    masks = list(pieces)
    count = len(masks)
    width = pieces[masks[0]].shape[2]
    flank = jnp.stack([rank ^ mask for mask in masks]).astype(jnp.int32)
    block = (1,) * (len(shape) - 2) + (tall, width)
    if width % 128:
        total = jnp.zeros(shape, jnp.float32) if buffer is None else buffer
        for step, mask in enumerate(masks):
            for number in range(LINE):
                value = pieces[mask][number, :tall].astype(jnp.float32).reshape(block)
                at = tuple(i * n for i, n in zip(place(number, flank[step]), block))
                total = lax.dynamic_update_slice(total, value, at)
        return total

    def kernel(flank_ref, *refs):
        step = pl.program_id(0)
        for turn in range(count):

            @pl.when(step == turn)
            def _():
                refs[-1][...] = refs[turn][...].astype(jnp.float32).reshape(block)

    def source(turn):
        def index(step, cut, flank_ref):
            return (jnp.where(step < turn, 0, jnp.where(step == turn, cut, LINE - 1)), 0, 0)

        return pl.BlockSpec((1, tall, width), index)

    in_specs = [source(turn) for turn in range(count)]
    operands = [flank] + [pieces[mask] for mask in masks]
    aliases = {}
    if buffer is not None:
        in_specs.append(anywhere())
        operands.append(buffer)
        aliases = {len(operands) - 1: 0}
    return pl.pallas_call(
        kernel,
        grid_spec=pltpu.PrefetchScalarGridSpec(
            num_scalar_prefetch=1,
            grid=(count, LINE),
            in_specs=in_specs,
            out_specs=pl.BlockSpec(
                block, lambda step, cut, flank_ref: place(cut, flank_ref[step])
            ),
        ),
        out_shape=jax.ShapeDtypeStruct(shape, jnp.float32),
        input_output_aliases=aliases,
        compiler_params=pltpu.CompilerParams(vmem_limit_bytes=40 << 20),
        cost_estimate=estimate(count * 2),
        name="join_blocks",
    )(*operands)


def tie(values, other):
    return values + nothing(other).astype(values.dtype)


def on_device(
    block_input,
    norm_gain,
    w_in,
    conv_w,
    conv_b,
    w_x,
    w_dt,
    b_dt,
    d_skip,
    w_out,
    out_grad,
    seq_counts,
):
    row_count, depth = block_input.shape
    size = lax.axis_size("mp")
    side = lax.axis_size("dp") // LINE
    length = row_count * size
    channels = w_in.shape[2]
    state_size = (w_x.shape[1] - R) // 2
    source_rows = block_input.astype(jnp.float32)
    inv_root = lax.rsqrt(jnp.mean(source_rows * source_rows, -1, keepdims=True) + 1e-05)
    normed = (source_rows * inv_root * norm_gain).astype(jnp.bfloat16)
    normed_pieces = gather_pieces(normed, "mp")
    masks = list(normed_pieces)
    ograd_pieces = gather_pieces(tie(out_grad, normed_pieces[masks[1]]), "mp")
    both = jnp.concatenate([normed, out_grad], 1)
    beside = [swap(both, "dp", mask) for mask in range(1, side)]
    keep_mask = boundaries(seq_counts[0], length)
    allow_two = keep_mask * shift_down(keep_mask, 1)
    allow_three = allow_two * shift_down(keep_mask, 2)
    allows = jnp.stack([keep_mask, allow_two, allow_three], 1)
    w_x_rows = w_x.T
    group_normed, inner, acts, proj_part = project_in(
        list(normed_pieces.values()),
        masks,
        w_in,
        allows,
        conv_w,
        conv_b,
        w_x_rows,
    )
    group_ograd, gate_silu, mixer_grad, gate_slope = project_gate(
        list(ograd_pieces.values()), list(ograd_pieces), group_normed, w_in, w_out, beside
    )
    proj = sum_mp(proj_part, gate_silu)
    others = []
    for rows in beside:
        rows = tie(rows, proj)
        others.append({mask: swap(rows, "mp", mask) if mask else rows for mask in masks})
    low_rank = proj[:, :R].astype(jnp.bfloat16)
    keys = proj[:, R : R + state_size]
    queries = proj[:, R + state_size :]
    beta = jax.nn.sigmoid(product(low_rank, w_dt) + b_dt)
    key_square = jnp.sum(keys * keys, 1)
    step_size = beta / (1.0 + beta * key_square[:, None])
    scalars = jnp.concatenate(
        [keys.reshape(-1), queries.reshape(-1), key_square, keep_mask[::8]]
    )
    step_tiles = to_tiles(step_size)
    acts_tiles = to_tiles(acts)
    mix_tiles, states = scan_forward(
        scalars,
        step_tiles,
        acts_tiles,
        CHUNK,
        state_size,
        (gate_silu, gate_slope),
    )
    mixer = from_tiles(mix_tiles) + d_skip * acts
    gated = (mixer * gate_silu).astype(jnp.bfloat16)
    gate_grad = (mixer * gate_slope).astype(jnp.bfloat16)
    back_args = (
        scalars,
        step_tiles,
        acts_tiles,
        to_tiles(mixer_grad),
        states,
        d_skip.astype(jnp.float32).reshape(channels // 128, 128),
        CHUNK,
        state_size,
    )
    chunks = length // CHUNK
    cut = chunks * 5 // 8
    later = scan_backward(*back_args, (cut, chunks), None, [gated, gate_grad])
    gate_job = (group_normed, 0, trade_side(gate_grad), False)
    out_job = (group_ograd, 1, trade_side(gated), True)
    stacked = channels // side == depth // LINE
    parts = factor_products(
        [gate_job, out_job], others, masks, depth, stacked, None, (later[6],)
    )
    scattered = [scatter_line(value) for value in parts]
    pre_tiles, agrad_tiles, key_grad, query_grad, fade, sums, _ = scan_backward(
        *back_args, (0, cut), later, parts
    )
    pre_full = from_tiles(pre_tiles)
    proj_back = project_back(pre_full, w_dt, key_grad, query_grad, keys, fade, ())
    proj_grad = sum_mp(proj_back).astype(jnp.bfloat16)
    inner_grad, conv_sums = finish_inner(
        from_tiles(agrad_tiles), proj_grad, w_x_rows, inner, allows, conv_w, conv_b, ()
    )
    inner_parts = trade_side(inner_grad)
    narrow = narrow_products(
        low_rank, pre_full, proj_grad, acts, conv_sums, sums.reshape(2, channels)
    )
    branch_out = scatter_mp(product(tie(gated, inner_grad), w_out))
    block_out = (source_rows + branch_out).astype(jnp.bfloat16)
    extra = sum((part.astype(jnp.float32) for part in trade_side(narrow))).astype(jnp.bfloat16)
    width = channels // side
    extra = extra.reshape(LINE, extra.shape[0] // LINE, width)
    gain_rows = -(-depth // (16 * width)) * 16
    extra = jnp.concatenate([extra, jnp.zeros((LINE, gain_rows, width), jnp.bfloat16)], 1)
    inner_job = (group_normed, 0, inner_parts, False)
    (inner_part,) = factor_products([inner_job], others, masks, depth, False, extra)
    scattered = [touch(value, (inner_part,)) for value in scattered]
    if stacked:
        gate_sum, out_sum = gather_line(scattered[0][:, 0]), gather_line(scattered[0][:, 1])
    else:
        gate_sum, out_sum = gather_line(scattered[0]), gather_line(scattered[1])
        gate_sum = gate_sum.reshape(LINE, depth // LINE, width)
        out_sum = out_sum.reshape(width, LINE, depth // LINE).transpose(1, 0, 2)
    gate_pieces, out_pieces = side_pieces(gate_sum), side_pieces(out_sum)
    normed_part = project_normed(inner_grad, gate_grad, w_in, (inner_part,))
    normed_grad = scatter_mp(normed_part)
    scaled = normed_grad * norm_gain
    gain_part = jnp.sum(normed_grad * source_rows * inv_root, 0)
    cubed = inv_root * inv_root * inv_root
    input_grad = inv_root * scaled - source_rows * cubed * jnp.mean(
        scaled * source_rows, -1, keepdims=True
    )
    input_grad = (out_grad.astype(jnp.float32) + input_grad).astype(jnp.bfloat16)
    for bit in bits_down(size):
        gain_part = gain_part + swap(gain_part, "mp", bit)
    part = depth // LINE
    tall = part // 2
    gain = jnp.zeros((gain_rows * width - depth,), jnp.float32)
    gain = jnp.concatenate([gain_part, gain]).reshape(gain_rows, width).astype(jnp.bfloat16)
    last = inner_part.shape[1] - gain_rows
    if last % gain_rows:
        inner_part = lax.dynamic_update_slice(inner_part, gain[None], (0, last, 0))
    else:
        inner_part = put_rows(inner_part, gain, last)
    inner_piece = scatter_line(
        touch(inner_part, [out_sum, block_out, input_grad] + list(gate_pieces.values()))
    )
    inner_piece = touch(inner_piece, tuple(out_pieces.values()))
    second_sum = gather_line(inner_piece[:, tall:])
    first_sum = gather_line(inner_piece[:, :tall])
    first_pieces, second_pieces = side_pieces(first_sum), side_pieces(second_sum)

    shape = (2, depth, channels)
    places = [lambda b, f: (f, b), lambda b, f: (1, b, f)]
    places += [lambda b, f: (0, 2 * b, f), lambda b, f: (0, 2 * b + 1, f)]
    heights = [width, part, tall, tall]
    own = [out_pieces, gate_pieces, first_pieces, second_pieces]
    own, rest = [{0: v[0]} for v in own], [{m: v[m] for m in v if m} for v in own]

    def assemble(which, pieces, buffer=None):
        full = shape if which else (channels, depth)
        return join_blocks(pieces[which], heights[which], places[which], full, buffer)

    w_out_grad = assemble(0, rest, assemble(0, own))
    w_in_grad = assemble(1, rest, assemble(1, own))
    for which, pieces in ((3, own), (2, own), (3, rest), (2, rest)):
        w_in_grad = assemble(which, pieces, w_in_grad)
    flank = lax.axis_index("dp") % side
    narrow = jnp.zeros((LINE * (last - part), channels), jnp.float32)
    for mask, piece in second_pieces.items():
        rows = piece[:, tall : last - tall].reshape(-1, width).astype(jnp.float32)
        narrow = lax.dynamic_update_slice(narrow, rows, (0, (flank ^ mask) * width))
    gains = [piece[0, last - tall :] for piece in second_pieces.values()]
    gain = sum((value.astype(jnp.float32) for value in gains)).reshape(-1)[:depth]
    split = R + R + 2 * state_size
    return (
        block_out,
        input_grad,
        gain,
        w_in_grad,
        narrow[split : split + 4],
        narrow[split + 4],
        narrow[R:split].T,
        narrow[:R],
        narrow[split + 8],
        narrow[split + 9],
        w_out_grad,
    )


def solution(mesh):
    in_specs = (
        P(("dp", "mp"), None),
        P(),
        P(None, None, "mp"),
        P(None, "mp"),
        P("mp"),
        P("mp", None),
        P(None, "mp"),
        P("mp"),
        P("mp"),
        P("mp", None),
        P(("dp", "mp"), None),
        P("dp", None),
    )
    out_specs = (
        P(("dp", "mp"), None),
        P(("dp", "mp"), None),
        P(),
        P(None, None, "mp"),
        P(None, "mp"),
        P("mp"),
        P("mp", None),
        P(None, "mp"),
        P("mp"),
        P("mp"),
        P("mp", None),
    )
    return jax.shard_map(
        on_device, mesh=mesh, in_specs=in_specs, out_specs=out_specs, check_vma=False
    )
```

```python
import jax
import jax.numpy as jnp
from jax import lax
from jax.experimental import pallas as pl
from jax.experimental.pallas import tpu as pltpu
from jax.sharding import PartitionSpec as P

R = 128
CHUNK = 64
LINE = 4

def boundaries(bucket_row, length):
    position = jnp.arange(length, dtype=jnp.int32)
    short_len = length // 16
    middle_len = length // 4
    short_end = bucket_row[2] * short_len
    middle_end = short_end + bucket_row[1] * middle_len
    first_short = (position < short_end) & (position % short_len == 0)
    first_middle = (
        (position >= short_end)
        & (position < middle_end)
        & ((position - short_end) % middle_len == 0)
    )
    first_long = (position == middle_end) & (position < length)
    opening = first_short | first_middle | first_long
    return jnp.where(opening, 0.0, 1.0).astype(jnp.float32)


def shift_down(values, lag):
    return jnp.concatenate([jnp.zeros((lag,) + values.shape[1:], values.dtype), values[:-lag]], 0)


def estimate(micros):
    return pl.CostEstimate(flops=1, bytes_accessed=1, transcendentals=0)


TOKENS = (((0,), (0,)), ((), ()))
ACROSS = (((1,), (1,)), ((), ()))


def product(left, right, dims=(((1,), (0,)), ((), ()))):
    return lax.dot_general(left, right, dims, preferred_element_type=jnp.float32)


def fixed(shape):
    return pl.BlockSpec(shape, lambda *_: (0,) * len(shape), pipeline_mode=pl.Buffered(1))


def anywhere():
    return pl.BlockSpec(memory_space=pl.ANY)


def whole(shape):
    return pl.BlockSpec(shape, lambda *_: (0,) * len(shape))


def row_sums(values):
    if values[0].shape[0] != 8:
        return jnp.concatenate([jnp.sum(value, 0, keepdims=True) for value in values], 0)
    row = lax.broadcasted_iota(jnp.int32, (8, 128), 0)
    span = 1
    while len(values) > 1:
        low = (row // span) % 2 == 0
        values = [
            jnp.where(low, a, b) + pltpu.roll(jnp.where(low, b, a), 8 - span, axis=0)
            for a, b in zip(values[0::2], values[1::2])
        ]
        span *= 2
    return values[0]


def forward_kernel(chunk, n, length, scalars, step_ref, acts_ref, mix_ref, states_ref, carry):
    index = pl.program_id(0)
    tiles = carry.shape[1]

    @pl.when(index == 0)
    def _():
        carry[...] = jnp.zeros_like(carry)

    def eight(block, state):
        keep = scalars[(2 * n + 1) * length + index * (chunk // 8) + block]
        state = [value * keep for value in state]
        for i in range(8):
            rows = pl.ds(i, tiles, stride=8)
            step = step_ref[block, rows, :]
            act = acts_ref[block, rows, :]
            token = block * 8 + i
            base = (index * chunk + token) * n
            total = None
            for j in range(n):
                k = scalars[base + j]
                state[j] = state[j] + (step * k) * (act - state[j] * k)
                states_ref[token, j] = state[j]
                part = state[j] * scalars[n * length + base + j]
                total = part if total is None else total + part
            mix_ref[block, rows, :] = total
        return tuple(state)

    final = lax.fori_loop(0, chunk // 8, eight, tuple(carry[j] for j in range(n)))
    for j in range(n):
        carry[j] = final[j]


def scan_forward(values, step, acts, chunk, n, after):
    blocks, height, _ = step.shape
    tiles = height // 8
    length = blocks * 8
    wide = pl.BlockSpec((chunk // 8, height, 128), lambda c: (c, 0, 0))
    scalars = pl.BlockSpec(memory_space=pltpu.SMEM)
    return pl.pallas_call(
        lambda *refs: forward_kernel(
            chunk, n, length, *refs[:3], *refs[3 + len(after) :]
        ),
        grid=(length // chunk,),
        in_specs=[scalars, wide, wide] + [anywhere()] * len(after),
        out_specs=[wide, pl.BlockSpec((chunk, n, tiles, 128), lambda c: (c, 0, 0, 0))],
        out_shape=[
            jax.ShapeDtypeStruct(step.shape, jnp.float32),
            jax.ShapeDtypeStruct((length, n, tiles, 128), jnp.float32),
        ],
        scratch_shapes=[pltpu.VMEM((n, tiles, 128), jnp.float32)],
        compiler_params=pltpu.CompilerParams(vmem_limit_bytes=48 << 20),
        cost_estimate=estimate(16),
        name="scan_forward",
    )(values, step, acts, *after)


def backward_kernel(
    chunk,
    n,
    last,
    carry_in,
    sums_in,
    length,
    scalars,
    step_ref,
    acts_ref,
    ygrad_ref,
    states_ref,
    prior_ref,
    skip_ref,
    pre_ref,
    agrad_ref,
    kgrad_ref,
    qgrad_ref,
    fade_ref,
    sums_ref,
    carry,
    kred,
    qred,
):
    order = pl.program_id(0)
    index = last - order
    tiles = carry.shape[1]

    @pl.when(order == 0)
    def _():
        if carry_in is None:
            carry[...] = jnp.zeros_like(carry)
            sums_ref[...] = jnp.zeros_like(sums_ref)
        else:
            carry[...] = carry_in[...]
            sums_ref[...] = sums_in[...]

    skip = skip_ref[...]

    def token_step(block, i, adjoint, prior_of):
        rows = pl.ds(i, tiles, stride=8)
        step = step_ref[block, rows, :]
        act = acts_ref[block, rows, :]
        ygrad = ygrad_ref[block, rows, :]
        token = block * 8 + i
        where = index * chunk + token
        base = where * n
        drive = None
        loss = None
        kparts = []
        qparts = []
        for j in range(n):
            k = scalars[base + j]
            adj = adjoint[j] + ygrad * scalars[n * length + base + j]
            prior = prior_of(token, j)
            ka = adj * k
            kp = prior * k
            kparts.append((step * adj) * (act - (kp + kp)))
            qparts.append(states_ref[token, j] * ygrad)
            part = ka * kp
            drive = ka if drive is None else drive + ka
            loss = part if loss is None else loss + part
            adjoint[j] = adj - (step * k) * ka
        step_grad = act * drive - loss
        scaled = step_grad * step
        pre = scaled * (1.0 - step * (1.0 + scalars[2 * n * length + where]))
        pre_ref[block, rows, :] = pre
        agrad_ref[block, rows, :] = step * drive + ygrad * skip
        sums_ref[0] += pre.astype(jnp.bfloat16).astype(jnp.float32)
        sums_ref[1] += ygrad * act
        for first in range(0, n, 8):
            kred[token, first : first + 8, :] = row_sums(kparts[first : first + 8])
            qred[token, first : first + 8, :] = row_sums(qparts[first : first + 8])
        return scaled * step

    def eight(turn, adjoint):
        block = chunk // 8 - 1 - turn
        adjoint = list(adjoint)
        keep = scalars[(2 * n + 1) * length + index * (chunk // 8) + block]
        fades = [None] * 8
        for i in range(7, 0, -1):
            fades[i] = token_step(block, i, adjoint, lambda token, j: states_ref[token - 1, j])
        first = block == 0
        back = jnp.maximum(block * 8 - 1, 0)
        fades[0] = token_step(
            block,
            0,
            adjoint,
            lambda token, j: jnp.where(first, prior_ref[0, j], states_ref[back, j]) * keep,
        )
        fade_ref[pl.ds(pl.multiple_of(block * 8, 8), 8), :] = row_sums(fades)
        return tuple(value * keep for value in adjoint)

    final = lax.fori_loop(0, chunk // 8, eight, tuple(carry[j] for j in range(n)))
    for j in range(n):
        carry[j] = final[j]
    kgrad_ref[...] = jnp.sum(kred[...], -1)
    qgrad_ref[...] = jnp.sum(qred[...], -1)


def scan_backward(
    values, step, acts, ygrad, states, skip, chunk, n, span, before, after
):
    blocks, height, _ = step.shape
    tiles = height // 8
    length = blocks * 8
    last = span[1] - 1
    wide = pl.BlockSpec((chunk // 8, height, 128), lambda c: (last - c, 0, 0))
    scalars = pl.BlockSpec(memory_space=pltpu.SMEM)
    narrow = pl.BlockSpec((chunk, n), lambda c: (last - c, 0))
    kept = pl.BlockSpec((n, tiles, 128), lambda c: (0, 0, 0))
    pair = pl.BlockSpec((2, tiles, 128), lambda c: (0, 0, 0))
    in_specs = [
        scalars,
        wide,
        wide,
        wide,
        pl.BlockSpec((chunk, n, tiles, 128), lambda c: (last - c, 0, 0, 0)),
        pl.BlockSpec(
            (1, n, tiles, 128), lambda c: (jnp.maximum((last - c) * chunk - 1, 0), 0, 0, 0)
        ),
        pl.BlockSpec((tiles, 128), lambda c: (0, 0)),
    ]
    operands = [values, step, acts, ygrad, states, states, skip]
    aliases = {}
    base = len(operands)
    if before is not None:
        in_specs += [pair, kept] + [anywhere()] * 5
        operands += [before[5], before[6]] + list(before[:5])
        aliases = {base + 2 + turn: turn for turn in range(5)}
    in_specs += [anywhere()] * len(after)
    operands += list(after)

    def kernel(*refs):
        sums_in, carry_in = refs[base : base + 2] if before is not None else (None, None)
        outs = refs[len(operands) :]
        backward_kernel(
            chunk, n, last, carry_in, sums_in, length, *refs[:base], *outs[:6], *outs[6:]
        )

    return pl.pallas_call(
        kernel,
        grid=(span[1] - span[0],),
        in_specs=in_specs,
        out_specs=[
            wide,
            wide,
            narrow,
            narrow,
            pl.BlockSpec((chunk, 128), lambda c: (last - c, 0)),
            pair,
            kept,
        ],
        out_shape=[jax.ShapeDtypeStruct(step.shape, jnp.float32)] * 2
        + [jax.ShapeDtypeStruct((length, n), jnp.float32)] * 2
        + [
            jax.ShapeDtypeStruct((length, 128), jnp.float32),
            jax.ShapeDtypeStruct((2, tiles, 128), jnp.float32),
            jax.ShapeDtypeStruct((n, tiles, 128), jnp.float32),
        ],
        scratch_shapes=[
            pltpu.VMEM((chunk, n, 128), jnp.float32),
            pltpu.VMEM((chunk, n, 128), jnp.float32),
        ],
        input_output_aliases=aliases,
        compiler_params=pltpu.CompilerParams(vmem_limit_bytes=48 << 20),
        cost_estimate=estimate(32 * chunk * (span[1] - span[0]) / length),
        name="scan_backward",
    )(*operands)


def taps_of(inner, allows):
    return [inner] + [
        pltpu.roll(inner, lag, axis=0) * allows[:, lag - 1 : lag] for lag in range(1, 4)
    ]


def project_in(pieces, masks, w_in, allows, conv_w, conv_b, w_x_rows):
    rank = lax.axis_index("mp")
    rows, depth = pieces[0].shape
    count = len(pieces)
    length = rows * count
    channels = w_in.shape[2]
    tile = min(256, channels)
    width = w_x_rows.shape[0]
    places = jnp.stack([(rank ^ mask) * rows for mask in masks]).astype(jnp.int32)

    def kernel(places_ref, *refs):
        sources = refs[:count]
        w_ref, allow_ref, cw_ref, cb_ref, wx_ref = refs[count : count + 5]
        normed_ref, inner_ref, acts_ref, proj_ref = refs[count + 5 :]
        step = pl.program_id(0)

        @pl.when(step == 0)
        def _():
            for turn in range(count):
                at = pl.multiple_of(places_ref[turn], rows)
                normed_ref[pl.ds(at, rows), :] = sources[turn][...]
            proj_ref[...] = jnp.zeros_like(proj_ref)

        inner = jnp.dot(normed_ref[...], w_ref[0], preferred_element_type=jnp.float32)
        inner_ref[...] = inner
        weights = cw_ref[...].astype(jnp.float32)
        pre = cb_ref[...].astype(jnp.float32)
        for lag, tap in enumerate(taps_of(inner, allow_ref[...])):
            pre = pre + weights[lag : lag + 1] * tap
        acts = (pre * jax.nn.sigmoid(pre)).astype(jnp.bfloat16)
        acts_ref[...] = acts.astype(jnp.float32)
        proj_ref[...] += product(acts, wx_ref[...], ACROSS)

    column = pl.BlockSpec((length, tile), lambda c, places_ref: (0, c))
    return pl.pallas_call(
        kernel,
        grid_spec=pltpu.PrefetchScalarGridSpec(
            num_scalar_prefetch=1,
            grid=(channels // tile,),
            in_specs=[fixed((rows, depth))] * count
            + [
                pl.BlockSpec((1, depth, tile), lambda c, places_ref: (0, 0, c)),
                fixed(allows.shape),
                pl.BlockSpec((4, tile), lambda c, places_ref: (0, c)),
                pl.BlockSpec((1, tile), lambda c, places_ref: (0, c)),
                pl.BlockSpec((width, tile), lambda c, places_ref: (0, c)),
            ],
            out_specs=[whole((length, depth)), column, column, whole((length, width))],
        ),
        out_shape=[
            jax.ShapeDtypeStruct((length, depth), jnp.bfloat16),
            jax.ShapeDtypeStruct((length, channels), jnp.float32),
            jax.ShapeDtypeStruct((length, channels), jnp.float32),
            jax.ShapeDtypeStruct((length, width), jnp.float32),
        ],
        compiler_params=pltpu.CompilerParams(vmem_limit_bytes=56 << 20),
        cost_estimate=estimate(8),
        name="project_in",
    )(places, *pieces, w_in, allows, conv_w, conv_b.reshape(1, -1), w_x_rows)


def project_gate(pieces, masks, normed, w_in, w_out, after):
    rank = lax.axis_index("mp")
    rows, depth = pieces[0].shape
    count = len(pieces)
    length = rows * count
    channels = w_in.shape[2]
    tile = min(256, channels)
    places = jnp.stack([(rank ^ mask) * rows for mask in masks]).astype(jnp.int32)

    def kernel(places_ref, *refs):
        sources = refs[:count]
        normed_ref, w_ref, wo_ref = refs[count : count + 3]
        ograd_ref, silu_ref, grad_ref, slope_ref = refs[-4:]

        @pl.when(pl.program_id(0) == 0)
        def _():
            for turn in range(count):
                at = pl.multiple_of(places_ref[turn], rows)
                ograd_ref[pl.ds(at, rows), :] = sources[turn][...]

        gate = product(normed_ref[...], w_ref[0])
        gated_rows = product(ograd_ref[...], wo_ref[...], ACROSS)
        sig = jax.nn.sigmoid(gate)
        silu = gate * sig
        silu_ref[...] = silu
        grad_ref[...] = gated_rows * silu
        slope_ref[...] = gated_rows * sig * (1.0 + gate * (1.0 - sig))

    column = pl.BlockSpec((length, tile), lambda c, places_ref: (0, c))
    return pl.pallas_call(
        kernel,
        grid_spec=pltpu.PrefetchScalarGridSpec(
            num_scalar_prefetch=1,
            grid=(channels // tile,),
            in_specs=[fixed((rows, depth))] * count
            + [
                fixed((length, depth)),
                pl.BlockSpec((1, depth, tile), lambda c, places_ref: (1, 0, c)),
                pl.BlockSpec((tile, depth), lambda c, places_ref: (c, 0)),
            ]
            + [anywhere()] * len(after),
            out_specs=[whole((length, depth)), column, column, column],
        ),
        out_shape=[jax.ShapeDtypeStruct((length, depth), jnp.bfloat16)]
        + [jax.ShapeDtypeStruct((length, channels), jnp.float32)] * 3,
        compiler_params=pltpu.CompilerParams(vmem_limit_bytes=60 << 20),
        cost_estimate=estimate(11),
        name="project_gate",
    )(places, *pieces, normed, w_in, w_out, *after)


def finish_inner(agrad, proj_grad, w_x_rows, inner, allows, conv_w, conv_b, after):
    length, channels = inner.shape
    tile = min(256, channels)
    width = w_x_rows.shape[0]

    def kernel(ag_ref, pg_ref, wx_ref, inner_ref, allow_ref, cw_ref, cb_ref, *refs):
        out_ref, sums_ref = refs[-2:]
        acts_grad = ag_ref[...] + product(pg_ref[...], wx_ref[...])
        allow = allow_ref[...]
        taps = taps_of(inner_ref[...], allow)
        weights = cw_ref[...].astype(jnp.float32)
        pre = cb_ref[...].astype(jnp.float32)
        for lag, tap in enumerate(taps):
            pre = pre + weights[lag : lag + 1] * tap
        sig = jax.nn.sigmoid(pre)
        conv_grad = acts_grad * sig * (1.0 + pre * (1.0 - sig))
        rows = [jnp.sum(conv_grad * tap, 0, keepdims=True) for tap in taps]
        rows.append(jnp.sum(conv_grad, 0, keepdims=True))
        sums_ref[...] = jnp.concatenate(rows + [jnp.zeros((3, tile), jnp.float32)], 0)
        total = weights[0:1] * conv_grad
        for lag in range(1, 4):
            sent = conv_grad * allow[:, lag - 1 : lag] * weights[lag : lag + 1]
            total = total + pltpu.roll(sent, length - lag, axis=0)
        out_ref[...] = total.astype(jnp.bfloat16)

    column = pl.BlockSpec((length, tile), lambda c: (0, c))
    return pl.pallas_call(
        kernel,
        grid=(channels // tile,),
        in_specs=[
            column,
            fixed((length, width)),
            pl.BlockSpec((width, tile), lambda c: (0, c)),
            column,
            fixed(allows.shape),
            pl.BlockSpec((4, tile), lambda c: (0, c)),
            pl.BlockSpec((1, tile), lambda c: (0, c)),
        ]
        + [anywhere()] * len(after),
        out_specs=[column, pl.BlockSpec((8, tile), lambda c: (0, c))],
        out_shape=[
            jax.ShapeDtypeStruct((length, channels), jnp.bfloat16),
            jax.ShapeDtypeStruct((8, channels), jnp.float32),
        ],
        compiler_params=pltpu.CompilerParams(vmem_limit_bytes=56 << 20),
        cost_estimate=estimate(6),
        name="finish_inner",
    )(agrad, proj_grad, w_x_rows, inner, allows, conv_w, conv_b.reshape(1, -1), *after)


def factor_products(jobs, others, masks, depth, stacked, extra=None, after=()):
    rank = lax.axis_index("mp")
    count = len(masks)
    length = jobs[0][0].shape[0]
    rows = length // count
    part = depth // LINE
    channels = jobs[0][2][0].shape[1]
    factors_first = [job[3] for job in jobs]
    places = jnp.stack([(rank ^ mask) * rows for mask in masks]).astype(jnp.int32)
    in_specs = []
    operands = [places]
    for rows_of, half, factors, _ in jobs:
        in_specs.append(pl.BlockSpec((length, part), lambda b, _: (0, b)))
        operands.append(rows_of)
        for other in others:
            for mask in masks:
                in_specs.append(
                    pl.BlockSpec(
                        (rows, part),
                        lambda b, _, half=half: (0, half * LINE + b),
                    )
                )
                operands.append(other[mask])
        for factor in factors:
            in_specs.append(fixed(factor.shape))
            operands.append(factor)
    more = 0 if extra is None else extra.shape[1]
    if more:
        in_specs.append(pl.BlockSpec((1, more, channels), lambda b, _: (b, 0, 0)))
        operands.append(extra)
    in_specs += [anywhere()] * len(after)
    operands += list(after)

    def kernel(places_ref, *refs):
        scratch = refs[-1]
        outs = refs[len(operands) - 1 : -1]

        at = 0
        for turn, first in enumerate(factors_first):
            source = refs[at]
            at += 1
            total = None
            groups = [refs[at + g * count : at + (g + 1) * count] for g in range(len(others))]
            at += len(others) * count
            for g in range(len(others) + 1):
                if g:
                    for piece, ref in enumerate(groups[g - 1]):
                        place = pl.multiple_of(places_ref[piece], rows)
                        scratch[pl.ds(place, rows), :] = ref[...]
                    value = scratch[...]
                else:
                    value = source[...]
                factor = refs[at + g][...]
                pair = (factor, value) if first else (value, factor)
                term = product(*pair, TOKENS)
                total = term if total is None else total + term
            at += len(others) + 1
            if stacked:
                outs[0][0, turn] = total.astype(jnp.bfloat16)
            elif more:
                outs[0][0, :part, :] = total.astype(jnp.bfloat16)
                outs[0][0, part:, :] = refs[at][0]
            else:
                outs[turn][...] = total.astype(jnp.bfloat16)

    if stacked:
        out_specs = [pl.BlockSpec((1, len(jobs), part, part), lambda b, _: (b, 0, 0, 0))]
        out_shape = [jax.ShapeDtypeStruct((LINE, len(jobs), part, part), jnp.bfloat16)]
    elif more:
        out_specs = [pl.BlockSpec((1, part + more, channels), lambda b, _: (b, 0, 0))]
        out_shape = [jax.ShapeDtypeStruct((LINE, part + more, channels), jnp.bfloat16)]
    else:
        out_specs = [
            pl.BlockSpec((channels, part), lambda b, _: (0, b))
            if first
            else pl.BlockSpec((part, channels), lambda b, _: (b, 0))
            for first in factors_first
        ]
        out_shape = [
            jax.ShapeDtypeStruct(
                (channels, depth) if first else (depth, channels), jnp.bfloat16
            )
            for first in factors_first
        ]
    return pl.pallas_call(
        kernel,
        grid_spec=pltpu.PrefetchScalarGridSpec(
            num_scalar_prefetch=1,
            grid=(LINE,),
            in_specs=in_specs,
            out_specs=out_specs,
            scratch_shapes=[pltpu.VMEM((length, part), jnp.bfloat16)],
        ),
        out_shape=out_shape,
        compiler_params=pltpu.CompilerParams(vmem_limit_bytes=56 << 20),
        cost_estimate=estimate(5 * len(jobs)),
        name="factor_products",
    )(*operands)


def touch(values, after):
    return pl.pallas_call(
        lambda *refs: None,
        in_specs=[anywhere()] * (1 + len(after)),
        out_specs=anywhere(),
        out_shape=jax.ShapeDtypeStruct(values.shape, values.dtype),
        input_output_aliases={0: 0},
        name="touch",
    )(values, *after)


def project_back(pre, w_dt, key_grad, query_grad, keys, fade, after):
    length, channels = pre.shape
    rank_width = w_dt.shape[0]
    n = keys.shape[1]
    tile = min(256, length)

    def kernel(pre_ref, w_ref, kg_ref, qg_ref, keys_ref, fade_ref, *refs):
        out_ref = refs[-1]
        out_ref[:, :rank_width] = product(pre_ref[...].astype(jnp.bfloat16), w_ref[...], ACROSS)
        spread = jnp.sum(fade_ref[...], 1, keepdims=True)
        out_ref[:, rank_width : rank_width + n] = kg_ref[...] - 2.0 * keys_ref[...] * spread
        out_ref[:, rank_width + n :] = qg_ref[...]

    rows = lambda width: pl.BlockSpec((tile, width), lambda c: (c, 0))
    return pl.pallas_call(
        kernel,
        grid=(length // tile,),
        in_specs=[rows(channels), fixed(w_dt.shape), rows(n), rows(n), rows(n), rows(128)]
        + [anywhere()] * len(after),
        out_specs=rows(rank_width + 2 * n),
        out_shape=jax.ShapeDtypeStruct((length, rank_width + 2 * n), jnp.float32),
        compiler_params=pltpu.CompilerParams(vmem_limit_bytes=40 << 20),
        cost_estimate=estimate(3),
        name="project_back",
    )(pre, w_dt, key_grad, query_grad, keys, fade, *after)


def narrow_products(low_rank, pre, proj_grad, acts, conv_sums, sums):
    length, channels = pre.shape
    tile = min(256, channels)
    rank_width, width = low_rank.shape[1], proj_grad.shape[1]
    used = rank_width + width
    total = used + 32

    def kernel(low_ref, pre_ref, pg_ref, acts_ref, conv_ref, sums_ref, out_ref):
        first = product(low_ref[...], pre_ref[...].astype(jnp.bfloat16), TOKENS)
        out_ref[:rank_width, :] = first.astype(jnp.bfloat16)
        second = product(pg_ref[...], acts_ref[...].astype(jnp.bfloat16), TOKENS)
        out_ref[rank_width:used, :] = second.astype(jnp.bfloat16)
        rows = jnp.concatenate(
            [conv_ref[...], sums_ref[...], jnp.zeros((22, tile), jnp.float32)], 0
        )
        out_ref[used:, :] = rows.astype(jnp.bfloat16)

    column = lambda height: pl.BlockSpec((height, tile), lambda c: (0, c))
    return pl.pallas_call(
        kernel,
        grid=(channels // tile,),
        in_specs=[
            fixed(low_rank.shape),
            column(length),
            fixed(proj_grad.shape),
            column(length),
            column(8),
            column(2),
        ],
        out_specs=column(total),
        out_shape=jax.ShapeDtypeStruct((total, channels), jnp.bfloat16),
        compiler_params=pltpu.CompilerParams(vmem_limit_bytes=48 << 20),
        cost_estimate=estimate(4),
        name="narrow_products",
    )(low_rank, pre, proj_grad, acts, conv_sums, sums)


def project_normed(inner_grad, gate_grad, w_in, after):
    length, channels = inner_grad.shape
    depth = w_in.shape[1]
    tile = min(512, depth)
    height = min(512, length)

    def kernel(inner_ref, gate_ref, w_ref, *refs):
        refs[-1][...] = product(inner_ref[...], w_ref[0], ACROSS) + product(
            gate_ref[...], w_ref[1], ACROSS
        )

    rows = pl.BlockSpec((height, channels), lambda c, r: (r, 0))
    return pl.pallas_call(
        kernel,
        grid=(depth // tile, length // height),
        in_specs=[rows, rows, pl.BlockSpec((2, tile, channels), lambda c, r: (0, c, 0))]
        + [anywhere()] * len(after),
        out_specs=pl.BlockSpec((height, tile), lambda c, r: (r, c)),
        out_shape=jax.ShapeDtypeStruct((length, depth), jnp.float32),
        compiler_params=pltpu.CompilerParams(vmem_limit_bytes=48 << 20),
        cost_estimate=estimate(6),
        name="project_normed",
    )(inner_grad, gate_grad, w_in, *after)


def put_rows(values, rows, at):
    height, width = rows.shape

    def kernel(rows_ref, values_ref, out_ref):
        out_ref[0] = rows_ref[...]

    return pl.pallas_call(
        kernel,
        grid=(1,),
        in_specs=[whole((height, width)), anywhere()],
        out_specs=pl.BlockSpec((1, height, width), lambda c: (0, at // height, 0)),
        out_shape=jax.ShapeDtypeStruct(values.shape, values.dtype),
        input_output_aliases={1: 0},
        name="put_rows",
    )(rows, values)


def to_tiles(values):
    length, channels = values.shape
    parts = values.reshape(length // 8, 8, channels // 128, 128).transpose(0, 2, 1, 3)
    return parts.reshape(length // 8, channels // 16, 128)


def from_tiles(values):
    blocks, height, _ = values.shape
    parts = values.reshape(blocks, height // 8, 8, 128).transpose(0, 2, 1, 3)
    return parts.reshape(blocks * 8, height * 16)


def swap(values, axis, offset):
    size = lax.axis_size(axis)
    return lax.ppermute(values, axis, [(i, i ^ offset) for i in range(size)])


def bits_down(size):
    bits = []
    bit = size // 2
    while bit:
        bits.append(bit)
        bit //= 2
    return bits


def gather_pieces(values, axis):
    pieces = {0: values}
    for bit in bits_down(lax.axis_size(axis)):
        for mask in list(pieces):
            pieces[mask | bit] = swap(pieces[mask], axis, bit)
    return pieces


def nothing(other):
    return other[(slice(0, 1),) * other.ndim].reshape(()).astype(jnp.float32) * 0.0


def sum_mp(values, after=None):
    rank = lax.axis_index("mp")
    half = values.shape[0] // 2
    odd = rank % 2
    mine = lax.dynamic_slice_in_dim(values, odd * half, half, 0)
    other = lax.dynamic_slice_in_dim(values, (1 - odd) * half, half, 0)
    mine = mine + swap(other, "mp", 1)
    bit = 2
    while bit < lax.axis_size("mp"):
        mine = mine + swap(mine, "mp", bit)
        bit *= 2
    if after is not None:
        mine = mine + nothing(after)
    other = swap(mine, "mp", 1)
    whole = jnp.zeros(values.shape, values.dtype)
    whole = lax.dynamic_update_slice_in_dim(whole, mine, odd * half, 0)
    return lax.dynamic_update_slice_in_dim(whole, other, (1 - odd) * half, 0)


def scatter_mp(values):
    rank = lax.axis_index("mp")
    size = lax.axis_size("mp")
    rows = values.shape[0] // size
    blocks = values.reshape(1, size, rows, values.shape[1])
    bit = 1
    while bit < size:
        left, here, _, width = blocks.shape
        pairs = blocks.reshape(left, here // 2, 2, rows, width)
        own = (rank // bit) % 2
        keep = lax.dynamic_index_in_dim(pairs, own, 2, keepdims=False)
        give = lax.dynamic_index_in_dim(pairs, 1 - own, 2, keepdims=False).astype(jnp.bfloat16)
        blocks = keep.astype(jnp.float32) + swap(give, "mp", bit).astype(jnp.float32)
        bit *= 2
    return blocks.reshape(rows, values.shape[1])


def trade_side(values):
    side = lax.axis_size("dp") // LINE
    rank = lax.axis_index("dp") % side
    width = values.shape[1] // side
    parts = []
    for mask in range(side):
        part = lax.dynamic_slice_in_dim(values, (rank ^ mask) * width, width, 1)
        parts.append(swap(part, "dp", mask) if mask else part)
    return parts


def line_groups():
    side = lax.axis_size("dp") // LINE
    return [[z * side + x for z in range(LINE)] for x in range(side)]


def scatter_line(values):
    return lax.psum_scatter(
        values, "dp", scatter_dimension=0, tiled=True, axis_index_groups=line_groups()
    )


def gather_line(values):
    return lax.all_gather(values, "dp", axis=0, tiled=True, axis_index_groups=line_groups())


def side_pieces(values):
    pieces = {0: values}
    for bit in bits_down(lax.axis_size("dp") // LINE):
        for mask in list(pieces):
            pieces[mask | bit] = swap(pieces[mask], "dp", bit)
    return pieces


def join_blocks(pieces, tall, place, shape, buffer=None, cuts=LINE, pick=lambda number: number):
    side = lax.axis_size("dp") // LINE
    rank = lax.axis_index("dp") % side
    masks = list(pieces)
    count = len(masks)
    width = pieces[masks[0]].shape[2]
    flank = jnp.stack([rank ^ mask for mask in masks]).astype(jnp.int32)
    block = (1,) * (len(shape) - 2) + (tall, width)
    if width % 128:
        total = jnp.zeros(shape, jnp.float32) if buffer is None else buffer
        for step, mask in enumerate(masks):
            for number in range(cuts):
                value = pieces[mask][pick(number), :tall].astype(jnp.float32).reshape(block)
                at = tuple(i * n for i, n in zip(place(number, flank[step]), block))
                total = lax.dynamic_update_slice(total, value, at)
        return total

    def kernel(flank_ref, *refs):
        step = pl.program_id(0)
        for turn in range(count):

            @pl.when(step == turn)
            def _():
                refs[-1][...] = refs[turn][...].astype(jnp.float32).reshape(block)

    def source(turn):
        def index(step, cut, flank_ref):
            number = jnp.where(step < turn, 0, jnp.where(step == turn, cut, cuts - 1))
            return (pick(number), 0, 0)

        return pl.BlockSpec((1, tall, width), index)

    in_specs = [source(turn) for turn in range(count)]
    operands = [flank] + [pieces[mask] for mask in masks]
    aliases = {}
    if buffer is not None:
        in_specs.append(anywhere())
        operands.append(buffer)
        aliases = {len(operands) - 1: 0}
    return pl.pallas_call(
        kernel,
        grid_spec=pltpu.PrefetchScalarGridSpec(
            num_scalar_prefetch=1,
            grid=(count, cuts),
            in_specs=in_specs,
            out_specs=pl.BlockSpec(
                block, lambda step, cut, flank_ref: place(cut, flank_ref[step])
            ),
        ),
        out_shape=jax.ShapeDtypeStruct(shape, jnp.float32),
        input_output_aliases=aliases,
        compiler_params=pltpu.CompilerParams(vmem_limit_bytes=40 << 20),
        cost_estimate=estimate(count * 2),
        name="join_blocks",
    )(*operands)


def tie(values, other):
    return values + nothing(other).astype(values.dtype)


def on_device(
    block_input,
    norm_gain,
    w_in,
    conv_w,
    conv_b,
    w_x,
    w_dt,
    b_dt,
    d_skip,
    w_out,
    out_grad,
    seq_counts,
):
    row_count, depth = block_input.shape
    size = lax.axis_size("mp")
    side = lax.axis_size("dp") // LINE
    length = row_count * size
    channels = w_in.shape[2]
    state_size = (w_x.shape[1] - R) // 2
    source_rows = block_input.astype(jnp.float32)
    inv_root = lax.rsqrt(jnp.mean(source_rows * source_rows, -1, keepdims=True) + 1e-05)
    normed = (source_rows * inv_root * norm_gain).astype(jnp.bfloat16)
    normed_pieces = gather_pieces(normed, "mp")
    masks = list(normed_pieces)
    ograd_pieces = gather_pieces(tie(out_grad, normed_pieces[masks[1]]), "mp")
    both = jnp.concatenate([normed, out_grad], 1)
    beside = [swap(both, "dp", mask) for mask in range(1, side)]
    keep_mask = boundaries(seq_counts[0], length)
    allow_two = keep_mask * shift_down(keep_mask, 1)
    allow_three = allow_two * shift_down(keep_mask, 2)
    allows = jnp.stack([keep_mask, allow_two, allow_three], 1)
    w_x_rows = w_x.T
    group_normed, inner, acts, proj_part = project_in(
        list(normed_pieces.values()),
        masks,
        w_in,
        allows,
        conv_w,
        conv_b,
        w_x_rows,
    )
    group_ograd, gate_silu, mixer_grad, gate_slope = project_gate(
        list(ograd_pieces.values()), list(ograd_pieces), group_normed, w_in, w_out, beside
    )
    proj = sum_mp(proj_part, gate_silu)
    others = []
    for rows in beside:
        rows = tie(rows, proj)
        others.append({mask: swap(rows, "mp", mask) if mask else rows for mask in masks})
    low_rank = proj[:, :R].astype(jnp.bfloat16)
    keys = proj[:, R : R + state_size]
    queries = proj[:, R + state_size :]
    beta = jax.nn.sigmoid(product(low_rank, w_dt) + b_dt)
    key_square = jnp.sum(keys * keys, 1)
    step_size = beta / (1.0 + beta * key_square[:, None])
    scalars = jnp.concatenate(
        [keys.reshape(-1), queries.reshape(-1), key_square, keep_mask[::8]]
    )
    step_tiles = to_tiles(step_size)
    acts_tiles = to_tiles(acts)
    mix_tiles, states = scan_forward(
        scalars,
        step_tiles,
        acts_tiles,
        CHUNK,
        state_size,
        (gate_silu, gate_slope),
    )
    mixer = from_tiles(mix_tiles) + d_skip * acts
    gated = (mixer * gate_silu).astype(jnp.bfloat16)
    gate_grad = (mixer * gate_slope).astype(jnp.bfloat16)
    back_args = (
        scalars,
        step_tiles,
        acts_tiles,
        to_tiles(mixer_grad),
        states,
        d_skip.astype(jnp.float32).reshape(channels // 128, 128),
        CHUNK,
        state_size,
    )
    chunks = length // CHUNK
    cut = chunks * 5 // 8
    later = scan_backward(*back_args, (cut, chunks), None, [gated, gate_grad])
    gate_job = (group_normed, 0, trade_side(gate_grad), False)
    out_job = (group_ograd, 1, trade_side(gated), True)
    stacked = channels // side == depth // LINE
    parts = factor_products(
        [gate_job, out_job], others, masks, depth, stacked, None, (later[6],)
    )
    scattered = [scatter_line(value) for value in parts]
    pre_tiles, agrad_tiles, key_grad, query_grad, fade, sums, _ = scan_backward(
        *back_args, (0, cut), later, parts
    )
    pre_full = from_tiles(pre_tiles)
    proj_back = project_back(pre_full, w_dt, key_grad, query_grad, keys, fade, ())
    proj_grad = sum_mp(proj_back).astype(jnp.bfloat16)
    inner_grad, conv_sums = finish_inner(
        from_tiles(agrad_tiles), proj_grad, w_x_rows, inner, allows, conv_w, conv_b, ()
    )
    inner_parts = trade_side(inner_grad)
    narrow = narrow_products(
        low_rank, pre_full, proj_grad, acts, conv_sums, sums.reshape(2, channels)
    )
    branch_out = scatter_mp(product(tie(gated, inner_grad), w_out))
    block_out = (source_rows + branch_out).astype(jnp.bfloat16)
    extra = sum((part.astype(jnp.float32) for part in trade_side(narrow))).astype(jnp.bfloat16)
    width = channels // side
    extra = extra.reshape(LINE, extra.shape[0] // LINE, width)
    gain_rows = -(-depth // (16 * width)) * 16
    extra = jnp.concatenate([extra, jnp.zeros((LINE, gain_rows, width), jnp.bfloat16)], 1)
    inner_job = (group_normed, 0, inner_parts, False)
    (inner_part,) = factor_products([inner_job], others, masks, depth, False, extra)
    sums_of = [gather_line(touch(value, (extra,))) for value in scattered]
    if stacked:
        blocks = sums_of[0].reshape(2 * LINE, width, width)
        halves = [blocks[:LINE], blocks[LINE:]]
    else:
        halves = [
            sums_of[0].reshape(LINE, depth // LINE, width),
            sums_of[1].reshape(width, LINE, depth // LINE).transpose(1, 0, 2),
        ]
    half_pieces = [side_pieces(value) for value in halves]
    normed_part = project_normed(inner_grad, gate_grad, w_in, (inner_part,))
    normed_grad = scatter_mp(normed_part)
    scaled = normed_grad * norm_gain
    gain_part = jnp.sum(normed_grad * source_rows * inv_root, 0)
    cubed = inv_root * inv_root * inv_root
    input_grad = inv_root * scaled - source_rows * cubed * jnp.mean(
        scaled * source_rows, -1, keepdims=True
    )
    input_grad = (out_grad.astype(jnp.float32) + input_grad).astype(jnp.bfloat16)
    for bit in bits_down(size):
        gain_part = gain_part + swap(gain_part, "mp", bit)
    part = depth // LINE
    tall = part // 2
    gain = jnp.zeros((gain_rows * width - depth,), jnp.float32)
    gain = jnp.concatenate([gain_part, gain]).reshape(gain_rows, width).astype(jnp.bfloat16)
    last = inner_part.shape[1] - gain_rows
    if last % gain_rows:
        inner_part = lax.dynamic_update_slice(inner_part, gain[None], (0, last, 0))
    else:
        inner_part = put_rows(inner_part, gain, last)
    inner_piece = scatter_line(
        touch(inner_part, sums_of + [block_out, input_grad])
    )
    inner_piece = touch(inner_piece, tuple(half_pieces[0].values()))
    second_sum = gather_line(inner_piece[:, tall:])
    first_sum = gather_line(inner_piece[:, :tall])
    second_pieces = side_pieces(second_sum)
    first_pieces = side_pieces(touch(first_sum, tuple(half_pieces[1].values())))

    shape = (2, depth, channels)
    part_out = lambda start: lambda b, f: (f, b + start)
    part_gate = lambda start: lambda b, f: (1, b + start, f)
    others_of = lambda pieces: {mask: pieces[mask] for mask in pieces if mask}

    def finished(place_of, height, full, job):
        if not stacked:
            pieces = half_pieces[1 - job]
            buffer = join_blocks({0: pieces[0]}, height, place_of(0), full)
            return join_blocks(others_of(pieces), height, place_of(0), full, buffer)
        pick = lambda number: 2 * number + job
        buffer = join_blocks({0: blocks}, height, place_of(0), full, None, LINE, pick)
        for turn, pieces in enumerate(half_pieces):
            start = turn * LINE // 2
            buffer = join_blocks(
                others_of(pieces), height, place_of(start), full, buffer, LINE // 2, pick
            )
        return buffer

    w_out_grad = finished(part_out, width, (channels, depth), 1 if stacked else 0)
    w_in_grad = finished(part_gate, part, shape, 0 if stacked else 1)
    upper = lambda b, f: (0, 2 * b, f)
    lower = lambda b, f: (0, 2 * b + 1, f)
    w_in_grad = join_blocks({0: second_pieces[0]}, tall, lower, shape, w_in_grad)
    w_in_grad = join_blocks({0: first_pieces[0]}, tall, upper, shape, w_in_grad)
    w_in_grad = join_blocks(others_of(second_pieces), tall, lower, shape, w_in_grad)
    w_in_grad = join_blocks(others_of(first_pieces), tall, upper, shape, w_in_grad)
    flank = lax.axis_index("dp") % side
    narrow = jnp.zeros((LINE * (last - part), channels), jnp.float32)
    for mask, piece in second_pieces.items():
        rows = piece[:, tall : last - tall].reshape(-1, width).astype(jnp.float32)
        narrow = lax.dynamic_update_slice(narrow, rows, (0, (flank ^ mask) * width))
    gains = [piece[0, last - tall :] for piece in second_pieces.values()]
    gain = sum((value.astype(jnp.float32) for value in gains)).reshape(-1)[:depth]
    split = R + R + 2 * state_size
    return (
        block_out,
        input_grad,
        gain,
        w_in_grad,
        narrow[split : split + 4],
        narrow[split + 4],
        narrow[R:split].T,
        narrow[:R],
        narrow[split + 8],
        narrow[split + 9],
        w_out_grad,
    )


def solution(mesh):
    in_specs = (
        P(("dp", "mp"), None),
        P(),
        P(None, None, "mp"),
        P(None, "mp"),
        P("mp"),
        P("mp", None),
        P(None, "mp"),
        P("mp"),
        P("mp"),
        P("mp", None),
        P(("dp", "mp"), None),
        P("dp", None),
    )
    out_specs = (
        P(("dp", "mp"), None),
        P(("dp", "mp"), None),
        P(),
        P(None, None, "mp"),
        P(None, "mp"),
        P("mp"),
        P("mp", None),
        P(None, "mp"),
        P("mp"),
        P("mp"),
        P("mp", None),
    )
    return jax.shard_map(
        on_device, mesh=mesh, in_specs=in_specs, out_specs=out_specs, check_vma=False
    )
```

```python
import jax
import jax.numpy as jnp
from jax import lax
from jax.experimental import pallas as pl
from jax.experimental.pallas import tpu as pltpu
from jax.sharding import PartitionSpec as P

R = 128
CHUNK = 64
LINE = 4

def boundaries(bucket_row, length):
    position = jnp.arange(length, dtype=jnp.int32)
    short_len = length // 16
    middle_len = length // 4
    short_end = bucket_row[2] * short_len
    middle_end = short_end + bucket_row[1] * middle_len
    first_short = (position < short_end) & (position % short_len == 0)
    first_middle = (
        (position >= short_end)
        & (position < middle_end)
        & ((position - short_end) % middle_len == 0)
    )
    first_long = (position == middle_end) & (position < length)
    opening = first_short | first_middle | first_long
    return jnp.where(opening, 0.0, 1.0).astype(jnp.float32)


def shift_down(values, lag):
    return jnp.concatenate([jnp.zeros((lag,) + values.shape[1:], values.dtype), values[:-lag]], 0)


def estimate(micros):
    return pl.CostEstimate(flops=1, bytes_accessed=1, transcendentals=0)


TOKENS = (((0,), (0,)), ((), ()))
ACROSS = (((1,), (1,)), ((), ()))


def product(left, right, dims=(((1,), (0,)), ((), ()))):
    return lax.dot_general(left, right, dims, preferred_element_type=jnp.float32)


def fixed(shape):
    return pl.BlockSpec(shape, lambda *_: (0,) * len(shape), pipeline_mode=pl.Buffered(1))


def anywhere():
    return pl.BlockSpec(memory_space=pl.ANY)


def whole(shape):
    return pl.BlockSpec(shape, lambda *_: (0,) * len(shape))


def row_sums(values):
    if values[0].shape[0] != 8:
        return jnp.concatenate([jnp.sum(value, 0, keepdims=True) for value in values], 0)
    row = lax.broadcasted_iota(jnp.int32, (8, 128), 0)
    span = 1
    while len(values) > 1:
        low = (row // span) % 2 == 0
        values = [
            jnp.where(low, a, b) + pltpu.roll(jnp.where(low, b, a), 8 - span, axis=0)
            for a, b in zip(values[0::2], values[1::2])
        ]
        span *= 2
    return values[0]


def forward_kernel(chunk, n, length, scalars, step_ref, acts_ref, mix_ref, states_ref, carry):
    index = pl.program_id(0)
    tiles = carry.shape[1]

    @pl.when(index == 0)
    def _():
        carry[...] = jnp.zeros_like(carry)

    def eight(block, state):
        keep = scalars[(2 * n + 1) * length + index * (chunk // 8) + block]
        state = [value * keep for value in state]
        for i in range(8):
            rows = pl.ds(i, tiles, stride=8)
            step = step_ref[block, rows, :]
            act = acts_ref[block, rows, :]
            token = block * 8 + i
            base = (index * chunk + token) * n
            total = None
            for j in range(n):
                k = scalars[base + j]
                state[j] = state[j] + (step * k) * (act - state[j] * k)
                states_ref[token, j] = state[j]
                part = state[j] * scalars[n * length + base + j]
                total = part if total is None else total + part
            mix_ref[block, rows, :] = total
        return tuple(state)

    final = lax.fori_loop(0, chunk // 8, eight, tuple(carry[j] for j in range(n)))
    for j in range(n):
        carry[j] = final[j]


def scan_forward(values, step, acts, chunk, n, after):
    blocks, height, _ = step.shape
    tiles = height // 8
    length = blocks * 8
    wide = pl.BlockSpec((chunk // 8, height, 128), lambda c: (c, 0, 0))
    scalars = pl.BlockSpec(memory_space=pltpu.SMEM)
    return pl.pallas_call(
        lambda *refs: forward_kernel(
            chunk, n, length, *refs[:3], *refs[3 + len(after) :]
        ),
        grid=(length // chunk,),
        in_specs=[scalars, wide, wide] + [anywhere()] * len(after),
        out_specs=[wide, pl.BlockSpec((chunk, n, tiles, 128), lambda c: (c, 0, 0, 0))],
        out_shape=[
            jax.ShapeDtypeStruct(step.shape, jnp.float32),
            jax.ShapeDtypeStruct((length, n, tiles, 128), jnp.float32),
        ],
        scratch_shapes=[pltpu.VMEM((n, tiles, 128), jnp.float32)],
        compiler_params=pltpu.CompilerParams(vmem_limit_bytes=48 << 20),
        cost_estimate=estimate(16),
        name="scan_forward",
    )(values, step, acts, *after)


def backward_kernel(
    chunk,
    n,
    last,
    carry_in,
    sums_in,
    length,
    scalars,
    step_ref,
    acts_ref,
    ygrad_ref,
    states_ref,
    prior_ref,
    skip_ref,
    pre_ref,
    agrad_ref,
    kgrad_ref,
    qgrad_ref,
    fade_ref,
    sums_ref,
    carry,
    kred,
    qred,
):
    order = pl.program_id(0)
    index = last - order
    tiles = carry.shape[1]

    @pl.when(order == 0)
    def _():
        if carry_in is None:
            carry[...] = jnp.zeros_like(carry)
            sums_ref[...] = jnp.zeros_like(sums_ref)
        else:
            carry[...] = carry_in[...]
            sums_ref[...] = sums_in[...]

    skip = skip_ref[...]

    def token_step(block, i, adjoint, prior_of):
        rows = pl.ds(i, tiles, stride=8)
        step = step_ref[block, rows, :]
        act = acts_ref[block, rows, :]
        ygrad = ygrad_ref[block, rows, :]
        token = block * 8 + i
        where = index * chunk + token
        base = where * n
        drive = None
        loss = None
        kparts = []
        qparts = []
        for j in range(n):
            k = scalars[base + j]
            adj = adjoint[j] + ygrad * scalars[n * length + base + j]
            prior = prior_of(token, j)
            ka = adj * k
            kp = prior * k
            kparts.append((step * adj) * (act - (kp + kp)))
            qparts.append(states_ref[token, j] * ygrad)
            part = ka * kp
            drive = ka if drive is None else drive + ka
            loss = part if loss is None else loss + part
            adjoint[j] = adj - (step * k) * ka
        step_grad = act * drive - loss
        scaled = step_grad * step
        pre = scaled * (1.0 - step * (1.0 + scalars[2 * n * length + where]))
        pre_ref[block, rows, :] = pre
        agrad_ref[block, rows, :] = step * drive + ygrad * skip
        sums_ref[0] += pre.astype(jnp.bfloat16).astype(jnp.float32)
        sums_ref[1] += ygrad * act
        for first in range(0, n, 8):
            kred[token, first : first + 8, :] = row_sums(kparts[first : first + 8])
            qred[token, first : first + 8, :] = row_sums(qparts[first : first + 8])
        return scaled * step

    def eight(turn, adjoint):
        block = chunk // 8 - 1 - turn
        adjoint = list(adjoint)
        keep = scalars[(2 * n + 1) * length + index * (chunk // 8) + block]
        fades = [None] * 8
        for i in range(7, 0, -1):
            fades[i] = token_step(block, i, adjoint, lambda token, j: states_ref[token - 1, j])
        first = block == 0
        back = jnp.maximum(block * 8 - 1, 0)
        fades[0] = token_step(
            block,
            0,
            adjoint,
            lambda token, j: jnp.where(first, prior_ref[0, j], states_ref[back, j]) * keep,
        )
        fade_ref[pl.ds(pl.multiple_of(block * 8, 8), 8), :] = row_sums(fades)
        return tuple(value * keep for value in adjoint)

    final = lax.fori_loop(0, chunk // 8, eight, tuple(carry[j] for j in range(n)))
    for j in range(n):
        carry[j] = final[j]
    kgrad_ref[...] = jnp.sum(kred[...], -1)
    qgrad_ref[...] = jnp.sum(qred[...], -1)


def scan_backward(
    values, step, acts, ygrad, states, skip, chunk, n, span, before, after
):
    blocks, height, _ = step.shape
    tiles = height // 8
    length = blocks * 8
    last = span[1] - 1
    wide = pl.BlockSpec((chunk // 8, height, 128), lambda c: (last - c, 0, 0))
    scalars = pl.BlockSpec(memory_space=pltpu.SMEM)
    narrow = pl.BlockSpec((chunk, n), lambda c: (last - c, 0))
    kept = pl.BlockSpec((n, tiles, 128), lambda c: (0, 0, 0))
    pair = pl.BlockSpec((2, tiles, 128), lambda c: (0, 0, 0))
    in_specs = [
        scalars,
        wide,
        wide,
        wide,
        pl.BlockSpec((chunk, n, tiles, 128), lambda c: (last - c, 0, 0, 0)),
        pl.BlockSpec(
            (1, n, tiles, 128), lambda c: (jnp.maximum((last - c) * chunk - 1, 0), 0, 0, 0)
        ),
        pl.BlockSpec((tiles, 128), lambda c: (0, 0)),
    ]
    operands = [values, step, acts, ygrad, states, states, skip]
    aliases = {}
    base = len(operands)
    if before is not None:
        in_specs += [pair, kept] + [anywhere()] * 5
        operands += [before[5], before[6]] + list(before[:5])
        aliases = {base + 2 + turn: turn for turn in range(5)}
    in_specs += [anywhere()] * len(after)
    operands += list(after)

    def kernel(*refs):
        sums_in, carry_in = refs[base : base + 2] if before is not None else (None, None)
        outs = refs[len(operands) :]
        backward_kernel(
            chunk, n, last, carry_in, sums_in, length, *refs[:base], *outs[:6], *outs[6:]
        )

    return pl.pallas_call(
        kernel,
        grid=(span[1] - span[0],),
        in_specs=in_specs,
        out_specs=[
            wide,
            wide,
            narrow,
            narrow,
            pl.BlockSpec((chunk, 128), lambda c: (last - c, 0)),
            pair,
            kept,
        ],
        out_shape=[jax.ShapeDtypeStruct(step.shape, jnp.float32)] * 2
        + [jax.ShapeDtypeStruct((length, n), jnp.float32)] * 2
        + [
            jax.ShapeDtypeStruct((length, 128), jnp.float32),
            jax.ShapeDtypeStruct((2, tiles, 128), jnp.float32),
            jax.ShapeDtypeStruct((n, tiles, 128), jnp.float32),
        ],
        scratch_shapes=[
            pltpu.VMEM((chunk, n, 128), jnp.float32),
            pltpu.VMEM((chunk, n, 128), jnp.float32),
        ],
        input_output_aliases=aliases,
        compiler_params=pltpu.CompilerParams(vmem_limit_bytes=48 << 20),
        cost_estimate=estimate(32 * chunk * (span[1] - span[0]) / length),
        name="scan_backward",
    )(*operands)


def taps_of(inner, allows):
    return [inner] + [
        pltpu.roll(inner, lag, axis=0) * allows[:, lag - 1 : lag] for lag in range(1, 4)
    ]


def project_in(pieces, masks, w_in, allows, conv_w, conv_b, w_x_rows):
    rank = lax.axis_index("mp")
    rows, depth = pieces[0].shape
    count = len(pieces)
    length = rows * count
    channels = w_in.shape[2]
    tile = min(256, channels)
    width = w_x_rows.shape[0]
    places = jnp.stack([(rank ^ mask) * rows for mask in masks]).astype(jnp.int32)

    def kernel(places_ref, *refs):
        sources = refs[:count]
        w_ref, allow_ref, cw_ref, cb_ref, wx_ref = refs[count : count + 5]
        normed_ref, inner_ref, acts_ref, proj_ref = refs[count + 5 :]
        step = pl.program_id(0)

        @pl.when(step == 0)
        def _():
            for turn in range(count):
                at = pl.multiple_of(places_ref[turn], rows)
                normed_ref[pl.ds(at, rows), :] = sources[turn][...]
            proj_ref[...] = jnp.zeros_like(proj_ref)

        inner = jnp.dot(normed_ref[...], w_ref[0], preferred_element_type=jnp.float32)
        inner_ref[...] = inner
        weights = cw_ref[...].astype(jnp.float32)
        pre = cb_ref[...].astype(jnp.float32)
        for lag, tap in enumerate(taps_of(inner, allow_ref[...])):
            pre = pre + weights[lag : lag + 1] * tap
        acts = (pre * jax.nn.sigmoid(pre)).astype(jnp.bfloat16)
        acts_ref[...] = acts.astype(jnp.float32)
        proj_ref[...] += product(acts, wx_ref[...], ACROSS)

    column = pl.BlockSpec((length, tile), lambda c, places_ref: (0, c))
    return pl.pallas_call(
        kernel,
        grid_spec=pltpu.PrefetchScalarGridSpec(
            num_scalar_prefetch=1,
            grid=(channels // tile,),
            in_specs=[fixed((rows, depth))] * count
            + [
                pl.BlockSpec((1, depth, tile), lambda c, places_ref: (0, 0, c)),
                fixed(allows.shape),
                pl.BlockSpec((4, tile), lambda c, places_ref: (0, c)),
                pl.BlockSpec((1, tile), lambda c, places_ref: (0, c)),
                pl.BlockSpec((width, tile), lambda c, places_ref: (0, c)),
            ],
            out_specs=[whole((length, depth)), column, column, whole((length, width))],
        ),
        out_shape=[
            jax.ShapeDtypeStruct((length, depth), jnp.bfloat16),
            jax.ShapeDtypeStruct((length, channels), jnp.float32),
            jax.ShapeDtypeStruct((length, channels), jnp.float32),
            jax.ShapeDtypeStruct((length, width), jnp.float32),
        ],
        compiler_params=pltpu.CompilerParams(vmem_limit_bytes=56 << 20),
        cost_estimate=estimate(8),
        name="project_in",
    )(places, *pieces, w_in, allows, conv_w, conv_b.reshape(1, -1), w_x_rows)


def project_gate(pieces, masks, normed, w_in, w_out, after):
    rank = lax.axis_index("mp")
    rows, depth = pieces[0].shape
    count = len(pieces)
    length = rows * count
    channels = w_in.shape[2]
    tile = min(256, channels)
    places = jnp.stack([(rank ^ mask) * rows for mask in masks]).astype(jnp.int32)

    def kernel(places_ref, *refs):
        sources = refs[:count]
        normed_ref, w_ref, wo_ref = refs[count : count + 3]
        ograd_ref, silu_ref, grad_ref, slope_ref = refs[-4:]

        @pl.when(pl.program_id(0) == 0)
        def _():
            for turn in range(count):
                at = pl.multiple_of(places_ref[turn], rows)
                ograd_ref[pl.ds(at, rows), :] = sources[turn][...]

        gate = product(normed_ref[...], w_ref[0])
        gated_rows = product(ograd_ref[...], wo_ref[...], ACROSS)
        sig = jax.nn.sigmoid(gate)
        silu = gate * sig
        silu_ref[...] = silu
        grad_ref[...] = gated_rows * silu
        slope_ref[...] = gated_rows * sig * (1.0 + gate * (1.0 - sig))

    column = pl.BlockSpec((length, tile), lambda c, places_ref: (0, c))
    return pl.pallas_call(
        kernel,
        grid_spec=pltpu.PrefetchScalarGridSpec(
            num_scalar_prefetch=1,
            grid=(channels // tile,),
            in_specs=[fixed((rows, depth))] * count
            + [
                fixed((length, depth)),
                pl.BlockSpec((1, depth, tile), lambda c, places_ref: (1, 0, c)),
                pl.BlockSpec((tile, depth), lambda c, places_ref: (c, 0)),
            ]
            + [anywhere()] * len(after),
            out_specs=[whole((length, depth)), column, column, column],
        ),
        out_shape=[jax.ShapeDtypeStruct((length, depth), jnp.bfloat16)]
        + [jax.ShapeDtypeStruct((length, channels), jnp.float32)] * 3,
        compiler_params=pltpu.CompilerParams(vmem_limit_bytes=60 << 20),
        cost_estimate=estimate(11),
        name="project_gate",
    )(places, *pieces, normed, w_in, w_out, *after)


def finish_inner(agrad, proj_grad, w_x_rows, inner, allows, conv_w, conv_b, after):
    length, channels = inner.shape
    tile = min(256, channels)
    width = w_x_rows.shape[0]

    def kernel(ag_ref, pg_ref, wx_ref, inner_ref, allow_ref, cw_ref, cb_ref, *refs):
        out_ref, sums_ref = refs[-2:]
        acts_grad = ag_ref[...] + product(pg_ref[...], wx_ref[...])
        allow = allow_ref[...]
        taps = taps_of(inner_ref[...], allow)
        weights = cw_ref[...].astype(jnp.float32)
        pre = cb_ref[...].astype(jnp.float32)
        for lag, tap in enumerate(taps):
            pre = pre + weights[lag : lag + 1] * tap
        sig = jax.nn.sigmoid(pre)
        conv_grad = acts_grad * sig * (1.0 + pre * (1.0 - sig))
        rows = [jnp.sum(conv_grad * tap, 0, keepdims=True) for tap in taps]
        rows.append(jnp.sum(conv_grad, 0, keepdims=True))
        sums_ref[...] = jnp.concatenate(rows + [jnp.zeros((3, tile), jnp.float32)], 0)
        total = weights[0:1] * conv_grad
        for lag in range(1, 4):
            sent = conv_grad * allow[:, lag - 1 : lag] * weights[lag : lag + 1]
            total = total + pltpu.roll(sent, length - lag, axis=0)
        out_ref[...] = total.astype(jnp.bfloat16)

    column = pl.BlockSpec((length, tile), lambda c: (0, c))
    return pl.pallas_call(
        kernel,
        grid=(channels // tile,),
        in_specs=[
            column,
            fixed((length, width)),
            pl.BlockSpec((width, tile), lambda c: (0, c)),
            column,
            fixed(allows.shape),
            pl.BlockSpec((4, tile), lambda c: (0, c)),
            pl.BlockSpec((1, tile), lambda c: (0, c)),
        ]
        + [anywhere()] * len(after),
        out_specs=[column, pl.BlockSpec((8, tile), lambda c: (0, c))],
        out_shape=[
            jax.ShapeDtypeStruct((length, channels), jnp.bfloat16),
            jax.ShapeDtypeStruct((8, channels), jnp.float32),
        ],
        compiler_params=pltpu.CompilerParams(vmem_limit_bytes=56 << 20),
        cost_estimate=estimate(6),
        name="finish_inner",
    )(agrad, proj_grad, w_x_rows, inner, allows, conv_w, conv_b.reshape(1, -1), *after)


def factor_products(jobs, others, masks, depth, stacked, extra=None, after=()):
    rank = lax.axis_index("mp")
    count = len(masks)
    length = jobs[0][0].shape[0]
    rows = length // count
    part = depth // LINE
    channels = jobs[0][2][0].shape[1]
    factors_first = [job[3] for job in jobs]
    places = jnp.stack([(rank ^ mask) * rows for mask in masks]).astype(jnp.int32)
    in_specs = []
    operands = [places]
    for rows_of, half, factors, _ in jobs:
        in_specs.append(pl.BlockSpec((length, part), lambda b, _: (0, b)))
        operands.append(rows_of)
        for other in others:
            for mask in masks:
                in_specs.append(
                    pl.BlockSpec(
                        (rows, part),
                        lambda b, _, half=half: (0, half * LINE + b),
                    )
                )
                operands.append(other[mask])
        for factor in factors:
            in_specs.append(fixed(factor.shape))
            operands.append(factor)
    more = 0 if extra is None else extra.shape[1]
    if more:
        in_specs.append(pl.BlockSpec((1, more, channels), lambda b, _: (b, 0, 0)))
        operands.append(extra)
    in_specs += [anywhere()] * len(after)
    operands += list(after)

    def kernel(places_ref, *refs):
        scratch = refs[-1]
        outs = refs[len(operands) - 1 : -1]

        at = 0
        for turn, first in enumerate(factors_first):
            source = refs[at]
            at += 1
            total = None
            groups = [refs[at + g * count : at + (g + 1) * count] for g in range(len(others))]
            at += len(others) * count
            for g in range(len(others) + 1):
                if g:
                    for piece, ref in enumerate(groups[g - 1]):
                        place = pl.multiple_of(places_ref[piece], rows)
                        scratch[pl.ds(place, rows), :] = ref[...]
                    value = scratch[...]
                else:
                    value = source[...]
                factor = refs[at + g][...]
                pair = (factor, value) if first else (value, factor)
                term = product(*pair, TOKENS)
                total = term if total is None else total + term
            at += len(others) + 1
            if stacked:
                outs[0][0, turn] = total.astype(jnp.bfloat16)
            elif more:
                outs[0][0, :part, :] = total.astype(jnp.bfloat16)
                outs[0][0, part:, :] = refs[at][0]
            else:
                outs[turn][...] = total.astype(jnp.bfloat16)

    if stacked:
        out_specs = [pl.BlockSpec((1, len(jobs), part, part), lambda b, _: (b, 0, 0, 0))]
        out_shape = [jax.ShapeDtypeStruct((LINE, len(jobs), part, part), jnp.bfloat16)]
    elif more:
        out_specs = [pl.BlockSpec((1, part + more, channels), lambda b, _: (b, 0, 0))]
        out_shape = [jax.ShapeDtypeStruct((LINE, part + more, channels), jnp.bfloat16)]
    else:
        out_specs = [
            pl.BlockSpec((channels, part), lambda b, _: (0, b))
            if first
            else pl.BlockSpec((part, channels), lambda b, _: (b, 0))
            for first in factors_first
        ]
        out_shape = [
            jax.ShapeDtypeStruct(
                (channels, depth) if first else (depth, channels), jnp.bfloat16
            )
            for first in factors_first
        ]
    return pl.pallas_call(
        kernel,
        grid_spec=pltpu.PrefetchScalarGridSpec(
            num_scalar_prefetch=1,
            grid=(LINE,),
            in_specs=in_specs,
            out_specs=out_specs,
            scratch_shapes=[pltpu.VMEM((length, part), jnp.bfloat16)],
        ),
        out_shape=out_shape,
        compiler_params=pltpu.CompilerParams(vmem_limit_bytes=56 << 20),
        cost_estimate=estimate(5 * len(jobs)),
        name="factor_products",
    )(*operands)


def touch(values, after):
    return pl.pallas_call(
        lambda *refs: None,
        in_specs=[anywhere()] * (1 + len(after)),
        out_specs=anywhere(),
        out_shape=jax.ShapeDtypeStruct(values.shape, values.dtype),
        input_output_aliases={0: 0},
        name="touch",
    )(values, *after)


def project_back(pre, w_dt, key_grad, query_grad, keys, fade, after):
    length, channels = pre.shape
    rank_width = w_dt.shape[0]
    n = keys.shape[1]
    tile = min(256, length)

    def kernel(pre_ref, w_ref, kg_ref, qg_ref, keys_ref, fade_ref, *refs):
        out_ref = refs[-1]
        out_ref[:, :rank_width] = product(pre_ref[...].astype(jnp.bfloat16), w_ref[...], ACROSS)
        spread = jnp.sum(fade_ref[...], 1, keepdims=True)
        out_ref[:, rank_width : rank_width + n] = kg_ref[...] - 2.0 * keys_ref[...] * spread
        out_ref[:, rank_width + n :] = qg_ref[...]

    rows = lambda width: pl.BlockSpec((tile, width), lambda c: (c, 0))
    return pl.pallas_call(
        kernel,
        grid=(length // tile,),
        in_specs=[rows(channels), fixed(w_dt.shape), rows(n), rows(n), rows(n), rows(128)]
        + [anywhere()] * len(after),
        out_specs=rows(rank_width + 2 * n),
        out_shape=jax.ShapeDtypeStruct((length, rank_width + 2 * n), jnp.float32),
        compiler_params=pltpu.CompilerParams(vmem_limit_bytes=40 << 20),
        cost_estimate=estimate(3),
        name="project_back",
    )(pre, w_dt, key_grad, query_grad, keys, fade, *after)


def narrow_products(low_rank, pre, proj_grad, acts, conv_sums, sums):
    length, channels = pre.shape
    tile = min(256, channels)
    rank_width, width = low_rank.shape[1], proj_grad.shape[1]
    used = rank_width + width
    total = used + 32

    def kernel(low_ref, pre_ref, pg_ref, acts_ref, conv_ref, sums_ref, out_ref):
        first = product(low_ref[...], pre_ref[...].astype(jnp.bfloat16), TOKENS)
        out_ref[:rank_width, :] = first.astype(jnp.bfloat16)
        second = product(pg_ref[...], acts_ref[...].astype(jnp.bfloat16), TOKENS)
        out_ref[rank_width:used, :] = second.astype(jnp.bfloat16)
        rows = jnp.concatenate(
            [conv_ref[...], sums_ref[...], jnp.zeros((22, tile), jnp.float32)], 0
        )
        out_ref[used:, :] = rows.astype(jnp.bfloat16)

    column = lambda height: pl.BlockSpec((height, tile), lambda c: (0, c))
    return pl.pallas_call(
        kernel,
        grid=(channels // tile,),
        in_specs=[
            fixed(low_rank.shape),
            column(length),
            fixed(proj_grad.shape),
            column(length),
            column(8),
            column(2),
        ],
        out_specs=column(total),
        out_shape=jax.ShapeDtypeStruct((total, channels), jnp.bfloat16),
        compiler_params=pltpu.CompilerParams(vmem_limit_bytes=48 << 20),
        cost_estimate=estimate(4),
        name="narrow_products",
    )(low_rank, pre, proj_grad, acts, conv_sums, sums)


def project_normed(inner_grad, gate_grad, w_in, after):
    length, channels = inner_grad.shape
    depth = w_in.shape[1]
    tile = min(512, depth)
    height = min(512, length)

    def kernel(inner_ref, gate_ref, w_ref, *refs):
        refs[-1][...] = product(inner_ref[...], w_ref[0], ACROSS) + product(
            gate_ref[...], w_ref[1], ACROSS
        )

    rows = pl.BlockSpec((height, channels), lambda c, r: (r, 0))
    return pl.pallas_call(
        kernel,
        grid=(depth // tile, length // height),
        in_specs=[rows, rows, pl.BlockSpec((2, tile, channels), lambda c, r: (0, c, 0))]
        + [anywhere()] * len(after),
        out_specs=pl.BlockSpec((height, tile), lambda c, r: (r, c)),
        out_shape=jax.ShapeDtypeStruct((length, depth), jnp.float32),
        compiler_params=pltpu.CompilerParams(vmem_limit_bytes=48 << 20),
        cost_estimate=estimate(6),
        name="project_normed",
    )(inner_grad, gate_grad, w_in, *after)


def put_rows(values, rows, at):
    height, width = rows.shape

    def kernel(rows_ref, values_ref, out_ref):
        out_ref[0] = rows_ref[...]

    return pl.pallas_call(
        kernel,
        grid=(1,),
        in_specs=[whole((height, width)), anywhere()],
        out_specs=pl.BlockSpec((1, height, width), lambda c: (0, at // height, 0)),
        out_shape=jax.ShapeDtypeStruct(values.shape, values.dtype),
        input_output_aliases={1: 0},
        name="put_rows",
    )(rows, values)


def to_tiles(values):
    length, channels = values.shape
    parts = values.reshape(length // 8, 8, channels // 128, 128).transpose(0, 2, 1, 3)
    return parts.reshape(length // 8, channels // 16, 128)


def from_tiles(values):
    blocks, height, _ = values.shape
    parts = values.reshape(blocks, height // 8, 8, 128).transpose(0, 2, 1, 3)
    return parts.reshape(blocks * 8, height * 16)


def swap(values, axis, offset):
    size = lax.axis_size(axis)
    return lax.ppermute(values, axis, [(i, i ^ offset) for i in range(size)])


def bits_down(size):
    bits = []
    bit = size // 2
    while bit:
        bits.append(bit)
        bit //= 2
    return bits


def gather_pieces(values, axis):
    pieces = {0: values}
    for bit in bits_down(lax.axis_size(axis)):
        for mask in list(pieces):
            pieces[mask | bit] = swap(pieces[mask], axis, bit)
    return pieces


def nothing(other):
    return other[(slice(0, 1),) * other.ndim].reshape(()).astype(jnp.float32) * 0.0


def sum_mp(values, after=()):
    bit, size = 1, lax.axis_size("mp")
    while bit < size:
        got = swap(values, "mp", bit)
        bit *= 2
        if after and bit == size:
            got = touch(got, after)
        values = values + got
    return values


def scatter_mp(values):
    rank = lax.axis_index("mp")
    size = lax.axis_size("mp")
    rows = values.shape[0] // size
    blocks = values.reshape(1, size, rows, values.shape[1])
    bit = 1
    while bit < size:
        left, here, _, width = blocks.shape
        pairs = blocks.reshape(left, here // 2, 2, rows, width)
        own = (rank // bit) % 2
        keep = lax.dynamic_index_in_dim(pairs, own, 2, keepdims=False)
        give = lax.dynamic_index_in_dim(pairs, 1 - own, 2, keepdims=False).astype(jnp.bfloat16)
        blocks = keep.astype(jnp.float32) + swap(give, "mp", bit).astype(jnp.float32)
        bit *= 2
    return blocks.reshape(rows, values.shape[1])


def trade_side(values):
    side = lax.axis_size("dp") // LINE
    rank = lax.axis_index("dp") % side
    width = values.shape[1] // side
    parts = []
    for mask in range(side):
        part = lax.dynamic_slice_in_dim(values, (rank ^ mask) * width, width, 1)
        parts.append(swap(part, "dp", mask) if mask else part)
    return parts


def line_groups():
    side = lax.axis_size("dp") // LINE
    return [[z * side + x for z in range(LINE)] for x in range(side)]


def scatter_line(values):
    return lax.psum_scatter(
        values, "dp", scatter_dimension=0, tiled=True, axis_index_groups=line_groups()
    )


def gather_line(values):
    return lax.all_gather(values, "dp", axis=0, tiled=True, axis_index_groups=line_groups())


def side_pieces(values):
    pieces = {0: values}
    for bit in bits_down(lax.axis_size("dp") // LINE):
        for mask in list(pieces):
            pieces[mask | bit] = swap(pieces[mask], "dp", bit)
    return pieces


def join_blocks(pieces, tall, place, shape, buffer=None, cuts=LINE, pick=lambda number: number):
    side = lax.axis_size("dp") // LINE
    rank = lax.axis_index("dp") % side
    masks = list(pieces)
    count = len(masks)
    width = pieces[masks[0]].shape[2]
    flank = jnp.stack([rank ^ mask for mask in masks]).astype(jnp.int32)
    block = (1,) * (len(shape) - 2) + (tall, width)
    if width % 128:
        total = jnp.zeros(shape, jnp.float32) if buffer is None else buffer
        for step, mask in enumerate(masks):
            for number in range(cuts):
                value = pieces[mask][pick(number), :tall].astype(jnp.float32).reshape(block)
                at = tuple(i * n for i, n in zip(place(number, flank[step]), block))
                total = lax.dynamic_update_slice(total, value, at)
        return total

    def kernel(flank_ref, *refs):
        step = pl.program_id(0)
        for turn in range(count):

            @pl.when(step == turn)
            def _():
                refs[-1][...] = refs[turn][...].astype(jnp.float32).reshape(block)

    def source(turn):
        def index(step, cut, flank_ref):
            number = jnp.where(step < turn, 0, jnp.where(step == turn, cut, cuts - 1))
            return (pick(number), 0, 0)

        return pl.BlockSpec((1, tall, width), index)

    in_specs = [source(turn) for turn in range(count)]
    operands = [flank] + [pieces[mask] for mask in masks]
    aliases = {}
    if buffer is not None:
        in_specs.append(anywhere())
        operands.append(buffer)
        aliases = {len(operands) - 1: 0}
    return pl.pallas_call(
        kernel,
        grid_spec=pltpu.PrefetchScalarGridSpec(
            num_scalar_prefetch=1,
            grid=(count, cuts),
            in_specs=in_specs,
            out_specs=pl.BlockSpec(
                block, lambda step, cut, flank_ref: place(cut, flank_ref[step])
            ),
        ),
        out_shape=jax.ShapeDtypeStruct(shape, jnp.float32),
        input_output_aliases=aliases,
        compiler_params=pltpu.CompilerParams(vmem_limit_bytes=40 << 20),
        cost_estimate=estimate(count * 2),
        name="join_blocks",
    )(*operands)


def tie(values, other):
    return values + nothing(other).astype(values.dtype)


def on_device(
    block_input,
    norm_gain,
    w_in,
    conv_w,
    conv_b,
    w_x,
    w_dt,
    b_dt,
    d_skip,
    w_out,
    out_grad,
    seq_counts,
):
    row_count, depth = block_input.shape
    size = lax.axis_size("mp")
    side = lax.axis_size("dp") // LINE
    length = row_count * size
    channels = w_in.shape[2]
    state_size = (w_x.shape[1] - R) // 2
    source_rows = block_input.astype(jnp.float32)
    inv_root = lax.rsqrt(jnp.mean(source_rows * source_rows, -1, keepdims=True) + 1e-05)
    normed = (source_rows * inv_root * norm_gain).astype(jnp.bfloat16)
    normed_pieces = gather_pieces(normed, "mp")
    masks = list(normed_pieces)
    ograd_pieces = gather_pieces(tie(out_grad, normed_pieces[masks[1]]), "mp")
    both = jnp.concatenate([normed, out_grad], 1)
    beside = [swap(both, "dp", mask) for mask in range(1, side)]
    keep_mask = boundaries(seq_counts[0], length)
    allow_two = keep_mask * shift_down(keep_mask, 1)
    allow_three = allow_two * shift_down(keep_mask, 2)
    allows = jnp.stack([keep_mask, allow_two, allow_three], 1)
    w_x_rows = w_x.T
    group_normed, inner, acts, proj_part = project_in(
        list(normed_pieces.values()),
        masks,
        w_in,
        allows,
        conv_w,
        conv_b,
        w_x_rows,
    )
    group_ograd, gate_silu, mixer_grad, gate_slope = project_gate(
        list(ograd_pieces.values()), list(ograd_pieces), group_normed, w_in, w_out, beside
    )
    proj = sum_mp(proj_part, (gate_silu,))
    others = []
    for rows in beside:
        others.append({mask: swap(rows, "mp", mask) if mask else rows for mask in masks})
    low_rank = proj[:, :R].astype(jnp.bfloat16)
    keys = proj[:, R : R + state_size]
    queries = proj[:, R + state_size :]
    beta = jax.nn.sigmoid(product(low_rank, w_dt) + b_dt)
    key_square = jnp.sum(keys * keys, 1)
    step_size = beta / (1.0 + beta * key_square[:, None])
    scalars = jnp.concatenate(
        [keys.reshape(-1), queries.reshape(-1), key_square, keep_mask[::8]]
    )
    step_tiles = to_tiles(step_size)
    acts_tiles = to_tiles(acts)
    mix_tiles, states = scan_forward(
        scalars,
        step_tiles,
        acts_tiles,
        CHUNK,
        state_size,
        (gate_silu, gate_slope),
    )
    mixer = from_tiles(mix_tiles) + d_skip * acts
    gated = (mixer * gate_silu).astype(jnp.bfloat16)
    gate_grad = (mixer * gate_slope).astype(jnp.bfloat16)
    back_args = (
        scalars,
        step_tiles,
        acts_tiles,
        to_tiles(mixer_grad),
        states,
        d_skip.astype(jnp.float32).reshape(channels // 128, 128),
        CHUNK,
        state_size,
    )
    chunks = length // CHUNK
    cut = chunks * 5 // 8
    later = scan_backward(*back_args, (cut, chunks), None, [gated, gate_grad])
    gate_job = (group_normed, 0, trade_side(gate_grad), False)
    out_job = (group_ograd, 1, trade_side(gated), True)
    stacked = channels // side == depth // LINE
    parts = factor_products(
        [gate_job, out_job], others, masks, depth, stacked, None, (later[6],)
    )
    scattered = [scatter_line(value) for value in parts]
    pre_tiles, agrad_tiles, key_grad, query_grad, fade, sums, _ = scan_backward(
        *back_args, (0, cut), later, parts
    )
    pre_full = from_tiles(pre_tiles)
    proj_back = project_back(pre_full, w_dt, key_grad, query_grad, keys, fade, ())
    proj_grad = sum_mp(proj_back).astype(jnp.bfloat16)
    inner_grad, conv_sums = finish_inner(
        from_tiles(agrad_tiles), proj_grad, w_x_rows, inner, allows, conv_w, conv_b, ()
    )
    inner_parts = trade_side(inner_grad)
    narrow = narrow_products(
        low_rank, pre_full, proj_grad, acts, conv_sums, sums.reshape(2, channels)
    )
    branch_out = scatter_mp(product(tie(gated, inner_grad), w_out))
    block_out = (source_rows + branch_out).astype(jnp.bfloat16)
    extra = sum((part.astype(jnp.float32) for part in trade_side(narrow))).astype(jnp.bfloat16)
    width = channels // side
    extra = extra.reshape(LINE, extra.shape[0] // LINE, width)
    gain_rows = -(-depth // (16 * width)) * 16
    extra = jnp.concatenate([extra, jnp.zeros((LINE, gain_rows, width), jnp.bfloat16)], 1)
    inner_job = (group_normed, 0, inner_parts, False)
    (inner_part,) = factor_products([inner_job], others, masks, depth, False, extra)
    sums_of = [gather_line(touch(value, (extra,))) for value in scattered]
    if stacked:
        blocks = sums_of[0].reshape(2 * LINE, width, width)
        halves = [blocks[:LINE], blocks[LINE:]]
    else:
        halves = [
            sums_of[0].reshape(LINE, depth // LINE, width),
            sums_of[1].reshape(width, LINE, depth // LINE).transpose(1, 0, 2),
        ]
    half_pieces = [side_pieces(value) for value in halves]
    normed_part = project_normed(inner_grad, gate_grad, w_in, (inner_part,))
    normed_grad = scatter_mp(normed_part)
    scaled = normed_grad * norm_gain
    gain_part = jnp.sum(normed_grad * source_rows * inv_root, 0)
    cubed = inv_root * inv_root * inv_root
    input_grad = inv_root * scaled - source_rows * cubed * jnp.mean(
        scaled * source_rows, -1, keepdims=True
    )
    input_grad = (out_grad.astype(jnp.float32) + input_grad).astype(jnp.bfloat16)
    for bit in bits_down(size):
        gain_part = gain_part + swap(gain_part, "mp", bit)
    part = depth // LINE
    tall = part // 2
    gain = jnp.zeros((gain_rows * width - depth,), jnp.float32)
    gain = jnp.concatenate([gain_part, gain]).reshape(gain_rows, width).astype(jnp.bfloat16)
    last = inner_part.shape[1] - gain_rows
    if last % gain_rows:
        inner_part = lax.dynamic_update_slice(inner_part, gain[None], (0, last, 0))
    else:
        inner_part = put_rows(inner_part, gain, last)
    inner_piece = scatter_line(
        touch(inner_part, sums_of + [block_out, input_grad])
    )
    inner_piece = touch(inner_piece, tuple(half_pieces[0].values()))
    second_sum = gather_line(inner_piece[:, tall:])
    first_sum = gather_line(inner_piece[:, :tall])
    second_pieces = side_pieces(second_sum)
    first_pieces = side_pieces(touch(first_sum, tuple(half_pieces[1].values())))

    shape = (2, depth, channels)
    part_out = lambda start: lambda b, f: (f, b + start)
    part_gate = lambda start: lambda b, f: (1, b + start, f)
    others_of = lambda pieces: {mask: pieces[mask] for mask in pieces if mask}

    def finished(place_of, height, full, job):
        if not stacked:
            pieces = half_pieces[1 - job]
            buffer = join_blocks({0: pieces[0]}, height, place_of(0), full)
            return join_blocks(others_of(pieces), height, place_of(0), full, buffer)
        pick = lambda number: 2 * number + job
        buffer = join_blocks({0: blocks}, height, place_of(0), full, None, LINE, pick)
        for turn, pieces in enumerate(half_pieces):
            start = turn * LINE // 2
            buffer = join_blocks(
                others_of(pieces), height, place_of(start), full, buffer, LINE // 2, pick
            )
        return buffer

    w_out_grad = finished(part_out, width, (channels, depth), 1 if stacked else 0)
    w_in_grad = finished(part_gate, part, shape, 0 if stacked else 1)
    upper = lambda b, f: (0, 2 * b, f)
    lower = lambda b, f: (0, 2 * b + 1, f)
    w_in_grad = join_blocks({0: second_pieces[0]}, tall, lower, shape, w_in_grad)
    w_in_grad = join_blocks({0: first_pieces[0]}, tall, upper, shape, w_in_grad)
    w_in_grad = join_blocks(others_of(second_pieces), tall, lower, shape, w_in_grad)
    w_in_grad = join_blocks(others_of(first_pieces), tall, upper, shape, w_in_grad)
    flank = lax.axis_index("dp") % side
    narrow = jnp.zeros((LINE * (last - part), channels), jnp.float32)
    for mask, piece in second_pieces.items():
        rows = piece[:, tall : last - tall].reshape(-1, width).astype(jnp.float32)
        narrow = lax.dynamic_update_slice(narrow, rows, (0, (flank ^ mask) * width))
    gains = [piece[0, last - tall :] for piece in second_pieces.values()]
    gain = sum((value.astype(jnp.float32) for value in gains)).reshape(-1)[:depth]
    split = R + R + 2 * state_size
    return (
        block_out,
        input_grad,
        gain,
        w_in_grad,
        narrow[split : split + 4],
        narrow[split + 4],
        narrow[R:split].T,
        narrow[:R],
        narrow[split + 8],
        narrow[split + 9],
        w_out_grad,
    )


def solution(mesh):
    in_specs = (
        P(("dp", "mp"), None),
        P(),
        P(None, None, "mp"),
        P(None, "mp"),
        P("mp"),
        P("mp", None),
        P(None, "mp"),
        P("mp"),
        P("mp"),
        P("mp", None),
        P(("dp", "mp"), None),
        P("dp", None),
    )
    out_specs = (
        P(("dp", "mp"), None),
        P(("dp", "mp"), None),
        P(),
        P(None, None, "mp"),
        P(None, "mp"),
        P("mp"),
        P("mp", None),
        P(None, "mp"),
        P("mp"),
        P("mp"),
        P("mp", None),
    )
    return jax.shard_map(
        on_device, mesh=mesh, in_specs=in_specs, out_specs=out_specs, check_vma=False
    )
```

```python
import jax
import jax.numpy as jnp
from jax import lax
from jax.experimental import pallas as pl
from jax.experimental.pallas import tpu as pltpu
from jax.sharding import PartitionSpec as P

R = 128
CHUNK = 64
LINE = 4

def boundaries(bucket_row, length):
    position = jnp.arange(length, dtype=jnp.int32)
    short_len = length // 16
    middle_len = length // 4
    short_end = bucket_row[2] * short_len
    middle_end = short_end + bucket_row[1] * middle_len
    first_short = (position < short_end) & (position % short_len == 0)
    first_middle = (
        (position >= short_end)
        & (position < middle_end)
        & ((position - short_end) % middle_len == 0)
    )
    first_long = (position == middle_end) & (position < length)
    opening = first_short | first_middle | first_long
    return jnp.where(opening, 0.0, 1.0).astype(jnp.float32)


def shift_down(values, lag):
    return jnp.concatenate([jnp.zeros((lag,) + values.shape[1:], values.dtype), values[:-lag]], 0)


def estimate(micros):
    return pl.CostEstimate(flops=1, bytes_accessed=1, transcendentals=0)


TOKENS = (((0,), (0,)), ((), ()))
ACROSS = (((1,), (1,)), ((), ()))


def product(left, right, dims=(((1,), (0,)), ((), ()))):
    return lax.dot_general(left, right, dims, preferred_element_type=jnp.float32)


def fixed(shape):
    return pl.BlockSpec(shape, lambda *_: (0,) * len(shape), pipeline_mode=pl.Buffered(1))


def anywhere():
    return pl.BlockSpec(memory_space=pl.ANY)


def whole(shape):
    return pl.BlockSpec(shape, lambda *_: (0,) * len(shape))


def row_sums(values):
    if values[0].shape[0] != 8:
        return jnp.concatenate([jnp.sum(value, 0, keepdims=True) for value in values], 0)
    row = lax.broadcasted_iota(jnp.int32, (8, 128), 0)
    span = 1
    while len(values) > 1:
        low = (row // span) % 2 == 0
        values = [
            jnp.where(low, a, b) + pltpu.roll(jnp.where(low, b, a), 8 - span, axis=0)
            for a, b in zip(values[0::2], values[1::2])
        ]
        span *= 2
    return values[0]


def forward_kernel(chunk, n, length, scalars, step_ref, acts_ref, mix_ref, states_ref, carry):
    index = pl.program_id(0)
    tiles = carry.shape[1]

    @pl.when(index == 0)
    def _():
        carry[...] = jnp.zeros_like(carry)

    def eight(block, state):
        keep = scalars[(2 * n + 1) * length + index * (chunk // 8) + block]
        state = [value * keep for value in state]
        for i in range(8):
            rows = pl.ds(i, tiles, stride=8)
            step = step_ref[block, rows, :]
            act = acts_ref[block, rows, :]
            token = block * 8 + i
            base = (index * chunk + token) * n
            total = None
            for j in range(n):
                k = scalars[base + j]
                state[j] = state[j] + (step * k) * (act - state[j] * k)
                states_ref[token, j] = state[j]
                part = state[j] * scalars[n * length + base + j]
                total = part if total is None else total + part
            mix_ref[block, rows, :] = total
        return tuple(state)

    final = lax.fori_loop(0, chunk // 8, eight, tuple(carry[j] for j in range(n)))
    for j in range(n):
        carry[j] = final[j]


def scan_forward(values, step, acts, chunk, n, after):
    blocks, height, _ = step.shape
    tiles = height // 8
    length = blocks * 8
    wide = pl.BlockSpec((chunk // 8, height, 128), lambda c: (c, 0, 0))
    scalars = pl.BlockSpec(memory_space=pltpu.SMEM)
    return pl.pallas_call(
        lambda *refs: forward_kernel(
            chunk, n, length, *refs[:3], *refs[3 + len(after) :]
        ),
        grid=(length // chunk,),
        in_specs=[scalars, wide, wide] + [anywhere()] * len(after),
        out_specs=[wide, pl.BlockSpec((chunk, n, tiles, 128), lambda c: (c, 0, 0, 0))],
        out_shape=[
            jax.ShapeDtypeStruct(step.shape, jnp.float32),
            jax.ShapeDtypeStruct((length, n, tiles, 128), jnp.float32),
        ],
        scratch_shapes=[pltpu.VMEM((n, tiles, 128), jnp.float32)],
        compiler_params=pltpu.CompilerParams(vmem_limit_bytes=48 << 20),
        cost_estimate=estimate(16),
        name="scan_forward",
    )(values, step, acts, *after)


def backward_kernel(
    chunk,
    n,
    last,
    carry_in,
    sums_in,
    length,
    scalars,
    step_ref,
    acts_ref,
    ygrad_ref,
    states_ref,
    prior_ref,
    skip_ref,
    pre_ref,
    agrad_ref,
    kgrad_ref,
    qgrad_ref,
    fade_ref,
    sums_ref,
    carry,
    kred,
    qred,
):
    order = pl.program_id(0)
    index = last - order
    tiles = carry.shape[1]

    @pl.when(order == 0)
    def _():
        if carry_in is None:
            carry[...] = jnp.zeros_like(carry)
            sums_ref[...] = jnp.zeros_like(sums_ref)
        else:
            carry[...] = carry_in[...]
            sums_ref[...] = sums_in[...]

    skip = skip_ref[...]

    def token_step(block, i, adjoint, prior_of):
        rows = pl.ds(i, tiles, stride=8)
        step = step_ref[block, rows, :]
        act = acts_ref[block, rows, :]
        ygrad = ygrad_ref[block, rows, :]
        token = block * 8 + i
        where = index * chunk + token
        base = where * n
        drive = None
        loss = None
        kparts = []
        qparts = []
        for j in range(n):
            k = scalars[base + j]
            adj = adjoint[j] + ygrad * scalars[n * length + base + j]
            prior = prior_of(token, j)
            ka = adj * k
            kp = prior * k
            kparts.append((step * adj) * (act - (kp + kp)))
            qparts.append(states_ref[token, j] * ygrad)
            part = ka * kp
            drive = ka if drive is None else drive + ka
            loss = part if loss is None else loss + part
            adjoint[j] = adj - (step * k) * ka
        step_grad = act * drive - loss
        scaled = step_grad * step
        pre = scaled * (1.0 - step * (1.0 + scalars[2 * n * length + where]))
        pre_ref[block, rows, :] = pre
        agrad_ref[block, rows, :] = step * drive + ygrad * skip
        sums_ref[0] += pre.astype(jnp.bfloat16).astype(jnp.float32)
        sums_ref[1] += ygrad * act
        for first in range(0, n, 8):
            kred[token, first : first + 8, :] = row_sums(kparts[first : first + 8])
            qred[token, first : first + 8, :] = row_sums(qparts[first : first + 8])
        return scaled * step

    def eight(turn, adjoint):
        block = chunk // 8 - 1 - turn
        adjoint = list(adjoint)
        keep = scalars[(2 * n + 1) * length + index * (chunk // 8) + block]
        fades = [None] * 8
        for i in range(7, 0, -1):
            fades[i] = token_step(block, i, adjoint, lambda token, j: states_ref[token - 1, j])
        first = block == 0
        back = jnp.maximum(block * 8 - 1, 0)
        fades[0] = token_step(
            block,
            0,
            adjoint,
            lambda token, j: jnp.where(first, prior_ref[0, j], states_ref[back, j]) * keep,
        )
        fade_ref[pl.ds(pl.multiple_of(block * 8, 8), 8), :] = row_sums(fades)
        return tuple(value * keep for value in adjoint)

    final = lax.fori_loop(0, chunk // 8, eight, tuple(carry[j] for j in range(n)))
    for j in range(n):
        carry[j] = final[j]
    kgrad_ref[...] = jnp.sum(kred[...], -1)
    qgrad_ref[...] = jnp.sum(qred[...], -1)


def scan_backward(
    values, step, acts, ygrad, states, skip, chunk, n, span, before, after
):
    blocks, height, _ = step.shape
    tiles = height // 8
    length = blocks * 8
    last = span[1] - 1
    wide = pl.BlockSpec((chunk // 8, height, 128), lambda c: (last - c, 0, 0))
    scalars = pl.BlockSpec(memory_space=pltpu.SMEM)
    narrow = pl.BlockSpec((chunk, n), lambda c: (last - c, 0))
    kept = pl.BlockSpec((n, tiles, 128), lambda c: (0, 0, 0))
    pair = pl.BlockSpec((2, tiles, 128), lambda c: (0, 0, 0))
    in_specs = [
        scalars,
        wide,
        wide,
        wide,
        pl.BlockSpec((chunk, n, tiles, 128), lambda c: (last - c, 0, 0, 0)),
        pl.BlockSpec(
            (1, n, tiles, 128), lambda c: (jnp.maximum((last - c) * chunk - 1, 0), 0, 0, 0)
        ),
        pl.BlockSpec((tiles, 128), lambda c: (0, 0)),
    ]
    operands = [values, step, acts, ygrad, states, states, skip]
    aliases = {}
    base = len(operands)
    if before is not None:
        in_specs += [pair, kept] + [anywhere()] * 5
        operands += [before[5], before[6]] + list(before[:5])
        aliases = {base + 2 + turn: turn for turn in range(5)}
    in_specs += [anywhere()] * len(after)
    operands += list(after)

    def kernel(*refs):
        sums_in, carry_in = refs[base : base + 2] if before is not None else (None, None)
        outs = refs[len(operands) :]
        backward_kernel(
            chunk, n, last, carry_in, sums_in, length, *refs[:base], *outs[:6], *outs[6:]
        )

    return pl.pallas_call(
        kernel,
        grid=(span[1] - span[0],),
        in_specs=in_specs,
        out_specs=[
            wide,
            wide,
            narrow,
            narrow,
            pl.BlockSpec((chunk, 128), lambda c: (last - c, 0)),
            pair,
            kept,
        ],
        out_shape=[jax.ShapeDtypeStruct(step.shape, jnp.float32)] * 2
        + [jax.ShapeDtypeStruct((length, n), jnp.float32)] * 2
        + [
            jax.ShapeDtypeStruct((length, 128), jnp.float32),
            jax.ShapeDtypeStruct((2, tiles, 128), jnp.float32),
            jax.ShapeDtypeStruct((n, tiles, 128), jnp.float32),
        ],
        scratch_shapes=[
            pltpu.VMEM((chunk, n, 128), jnp.float32),
            pltpu.VMEM((chunk, n, 128), jnp.float32),
        ],
        input_output_aliases=aliases,
        compiler_params=pltpu.CompilerParams(vmem_limit_bytes=48 << 20),
        cost_estimate=estimate(32 * chunk * (span[1] - span[0]) / length),
        name="scan_backward",
    )(*operands)


def taps_of(inner, allows):
    return [inner] + [
        pltpu.roll(inner, lag, axis=0) * allows[:, lag - 1 : lag] for lag in range(1, 4)
    ]


def project_in(pieces, masks, w_in, allows, conv_w, conv_b, w_x_rows):
    rank = lax.axis_index("mp")
    rows, depth = pieces[0].shape
    count = len(pieces)
    length = rows * count
    channels = w_in.shape[2]
    tile = min(256, channels)
    width = w_x_rows.shape[0]
    places = jnp.stack([(rank ^ mask) * rows for mask in masks]).astype(jnp.int32)

    def kernel(places_ref, *refs):
        sources = refs[:count]
        w_ref, allow_ref, cw_ref, cb_ref, wx_ref = refs[count : count + 5]
        normed_ref, inner_ref, acts_ref, proj_ref = refs[count + 5 :]
        step = pl.program_id(0)

        @pl.when(step == 0)
        def _():
            for turn in range(count):
                at = pl.multiple_of(places_ref[turn], rows)
                normed_ref[pl.ds(at, rows), :] = sources[turn][...]
            proj_ref[...] = jnp.zeros_like(proj_ref)

        inner = jnp.dot(normed_ref[...], w_ref[0], preferred_element_type=jnp.float32)
        inner_ref[...] = inner
        weights = cw_ref[...].astype(jnp.float32)
        pre = cb_ref[...].astype(jnp.float32)
        for lag, tap in enumerate(taps_of(inner, allow_ref[...])):
            pre = pre + weights[lag : lag + 1] * tap
        acts = (pre * jax.nn.sigmoid(pre)).astype(jnp.bfloat16)
        acts_ref[...] = acts.astype(jnp.float32)
        proj_ref[...] += product(acts, wx_ref[...], ACROSS)

    column = pl.BlockSpec((length, tile), lambda c, places_ref: (0, c))
    return pl.pallas_call(
        kernel,
        grid_spec=pltpu.PrefetchScalarGridSpec(
            num_scalar_prefetch=1,
            grid=(channels // tile,),
            in_specs=[fixed((rows, depth))] * count
            + [
                pl.BlockSpec((1, depth, tile), lambda c, places_ref: (0, 0, c)),
                fixed(allows.shape),
                pl.BlockSpec((4, tile), lambda c, places_ref: (0, c)),
                pl.BlockSpec((1, tile), lambda c, places_ref: (0, c)),
                pl.BlockSpec((width, tile), lambda c, places_ref: (0, c)),
            ],
            out_specs=[whole((length, depth)), column, column, whole((length, width))],
        ),
        out_shape=[
            jax.ShapeDtypeStruct((length, depth), jnp.bfloat16),
            jax.ShapeDtypeStruct((length, channels), jnp.float32),
            jax.ShapeDtypeStruct((length, channels), jnp.float32),
            jax.ShapeDtypeStruct((length, width), jnp.float32),
        ],
        compiler_params=pltpu.CompilerParams(vmem_limit_bytes=56 << 20),
        cost_estimate=estimate(8),
        name="project_in",
    )(places, *pieces, w_in, allows, conv_w, conv_b.reshape(1, -1), w_x_rows)


def project_gate(pieces, masks, normed, w_in, w_out, after):
    rank = lax.axis_index("mp")
    rows, depth = pieces[0].shape
    count = len(pieces)
    length = rows * count
    channels = w_in.shape[2]
    tile = min(256, channels)
    places = jnp.stack([(rank ^ mask) * rows for mask in masks]).astype(jnp.int32)

    def kernel(places_ref, *refs):
        sources = refs[:count]
        normed_ref, w_ref, wo_ref = refs[count : count + 3]
        ograd_ref, silu_ref, grad_ref, slope_ref = refs[-4:]

        @pl.when(pl.program_id(0) == 0)
        def _():
            for turn in range(count):
                at = pl.multiple_of(places_ref[turn], rows)
                ograd_ref[pl.ds(at, rows), :] = sources[turn][...]

        gate = product(normed_ref[...], w_ref[0])
        gated_rows = product(ograd_ref[...], wo_ref[...], ACROSS)
        sig = jax.nn.sigmoid(gate)
        silu = gate * sig
        silu_ref[...] = silu
        grad_ref[...] = gated_rows * silu
        slope_ref[...] = gated_rows * sig * (1.0 + gate * (1.0 - sig))

    column = pl.BlockSpec((length, tile), lambda c, places_ref: (0, c))
    return pl.pallas_call(
        kernel,
        grid_spec=pltpu.PrefetchScalarGridSpec(
            num_scalar_prefetch=1,
            grid=(channels // tile,),
            in_specs=[fixed((rows, depth))] * count
            + [
                fixed((length, depth)),
                pl.BlockSpec((1, depth, tile), lambda c, places_ref: (1, 0, c)),
                pl.BlockSpec((tile, depth), lambda c, places_ref: (c, 0)),
            ]
            + [anywhere()] * len(after),
            out_specs=[whole((length, depth)), column, column, column],
        ),
        out_shape=[jax.ShapeDtypeStruct((length, depth), jnp.bfloat16)]
        + [jax.ShapeDtypeStruct((length, channels), jnp.float32)] * 3,
        compiler_params=pltpu.CompilerParams(vmem_limit_bytes=60 << 20),
        cost_estimate=estimate(11),
        name="project_gate",
    )(places, *pieces, normed, w_in, w_out, *after)


def finish_inner(agrad, proj_grad, w_x_rows, inner, allows, conv_w, conv_b, after):
    length, channels = inner.shape
    tile = min(256, channels)
    width = w_x_rows.shape[0]

    def kernel(ag_ref, pg_ref, wx_ref, inner_ref, allow_ref, cw_ref, cb_ref, *refs):
        out_ref, sums_ref = refs[-2:]
        acts_grad = ag_ref[...] + product(pg_ref[...], wx_ref[...])
        allow = allow_ref[...]
        taps = taps_of(inner_ref[...], allow)
        weights = cw_ref[...].astype(jnp.float32)
        pre = cb_ref[...].astype(jnp.float32)
        for lag, tap in enumerate(taps):
            pre = pre + weights[lag : lag + 1] * tap
        sig = jax.nn.sigmoid(pre)
        conv_grad = acts_grad * sig * (1.0 + pre * (1.0 - sig))
        rows = [jnp.sum(conv_grad * tap, 0, keepdims=True) for tap in taps]
        rows.append(jnp.sum(conv_grad, 0, keepdims=True))
        sums_ref[...] = jnp.concatenate(rows + [jnp.zeros((3, tile), jnp.float32)], 0)
        total = weights[0:1] * conv_grad
        for lag in range(1, 4):
            sent = conv_grad * allow[:, lag - 1 : lag] * weights[lag : lag + 1]
            total = total + pltpu.roll(sent, length - lag, axis=0)
        out_ref[...] = total.astype(jnp.bfloat16)

    column = pl.BlockSpec((length, tile), lambda c: (0, c))
    return pl.pallas_call(
        kernel,
        grid=(channels // tile,),
        in_specs=[
            column,
            fixed((length, width)),
            pl.BlockSpec((width, tile), lambda c: (0, c)),
            column,
            fixed(allows.shape),
            pl.BlockSpec((4, tile), lambda c: (0, c)),
            pl.BlockSpec((1, tile), lambda c: (0, c)),
        ]
        + [anywhere()] * len(after),
        out_specs=[column, pl.BlockSpec((8, tile), lambda c: (0, c))],
        out_shape=[
            jax.ShapeDtypeStruct((length, channels), jnp.bfloat16),
            jax.ShapeDtypeStruct((8, channels), jnp.float32),
        ],
        compiler_params=pltpu.CompilerParams(vmem_limit_bytes=56 << 20),
        cost_estimate=estimate(6),
        name="finish_inner",
    )(agrad, proj_grad, w_x_rows, inner, allows, conv_w, conv_b.reshape(1, -1), *after)


def factor_products(jobs, others, masks, depth, stacked, extra=None, after=()):
    rank = lax.axis_index("mp")
    count = len(masks)
    length = jobs[0][0].shape[0]
    rows = length // count
    part = depth // LINE
    channels = jobs[0][2][0].shape[1]
    factors_first = [job[3] for job in jobs]
    places = jnp.stack([(rank ^ mask) * rows for mask in masks]).astype(jnp.int32)
    in_specs = []
    operands = [places]
    for rows_of, half, factors, _ in jobs:
        in_specs.append(pl.BlockSpec((length, part), lambda b, _: (0, b)))
        operands.append(rows_of)
        for other in others:
            for mask in masks:
                in_specs.append(
                    pl.BlockSpec(
                        (rows, part),
                        lambda b, _, half=half: (0, half * LINE + b),
                    )
                )
                operands.append(other[mask])
        for factor in factors:
            in_specs.append(fixed(factor.shape))
            operands.append(factor)
    more = 0 if extra is None else extra.shape[1]
    if more:
        in_specs.append(pl.BlockSpec((1, more, channels), lambda b, _: (b, 0, 0)))
        operands.append(extra)
    in_specs += [anywhere()] * len(after)
    operands += list(after)

    def kernel(places_ref, *refs):
        scratch = refs[-1]
        outs = refs[len(operands) - 1 : -1]

        at = 0
        for turn, first in enumerate(factors_first):
            source = refs[at]
            at += 1
            total = None
            groups = [refs[at + g * count : at + (g + 1) * count] for g in range(len(others))]
            at += len(others) * count
            for g in range(len(others) + 1):
                if g:
                    for piece, ref in enumerate(groups[g - 1]):
                        place = pl.multiple_of(places_ref[piece], rows)
                        scratch[pl.ds(place, rows), :] = ref[...]
                    value = scratch[...]
                else:
                    value = source[...]
                factor = refs[at + g][...]
                pair = (factor, value) if first else (value, factor)
                term = product(*pair, TOKENS)
                total = term if total is None else total + term
            at += len(others) + 1
            if stacked:
                outs[0][0, turn] = total.astype(jnp.bfloat16)
            elif more:
                outs[0][0, :part, :] = total.astype(jnp.bfloat16)
                outs[0][0, part:, :] = refs[at][0]
            else:
                outs[turn][...] = total.astype(jnp.bfloat16)

    if stacked:
        out_specs = [pl.BlockSpec((1, len(jobs), part, part), lambda b, _: (b, 0, 0, 0))]
        out_shape = [jax.ShapeDtypeStruct((LINE, len(jobs), part, part), jnp.bfloat16)]
    elif more:
        out_specs = [pl.BlockSpec((1, part + more, channels), lambda b, _: (b, 0, 0))]
        out_shape = [jax.ShapeDtypeStruct((LINE, part + more, channels), jnp.bfloat16)]
    else:
        out_specs = [
            pl.BlockSpec((channels, part), lambda b, _: (0, b))
            if first
            else pl.BlockSpec((part, channels), lambda b, _: (b, 0))
            for first in factors_first
        ]
        out_shape = [
            jax.ShapeDtypeStruct(
                (channels, depth) if first else (depth, channels), jnp.bfloat16
            )
            for first in factors_first
        ]
    return pl.pallas_call(
        kernel,
        grid_spec=pltpu.PrefetchScalarGridSpec(
            num_scalar_prefetch=1,
            grid=(LINE,),
            in_specs=in_specs,
            out_specs=out_specs,
            scratch_shapes=[pltpu.VMEM((length, part), jnp.bfloat16)],
        ),
        out_shape=out_shape,
        compiler_params=pltpu.CompilerParams(vmem_limit_bytes=56 << 20),
        cost_estimate=estimate(5 * len(jobs)),
        name="factor_products",
    )(*operands)


def touch(values, after):
    return pl.pallas_call(
        lambda *refs: None,
        in_specs=[anywhere()] * (1 + len(after)),
        out_specs=anywhere(),
        out_shape=jax.ShapeDtypeStruct(values.shape, values.dtype),
        input_output_aliases={0: 0},
        name="touch",
    )(values, *after)


def project_back(pre, w_dt, key_grad, query_grad, keys, fade, after):
    length, channels = pre.shape
    rank_width = w_dt.shape[0]
    n = keys.shape[1]
    tile = min(256, length)

    def kernel(pre_ref, w_ref, kg_ref, qg_ref, keys_ref, fade_ref, *refs):
        out_ref = refs[-1]
        out_ref[:, :rank_width] = product(pre_ref[...].astype(jnp.bfloat16), w_ref[...], ACROSS)
        spread = jnp.sum(fade_ref[...], 1, keepdims=True)
        out_ref[:, rank_width : rank_width + n] = kg_ref[...] - 2.0 * keys_ref[...] * spread
        out_ref[:, rank_width + n :] = qg_ref[...]

    rows = lambda width: pl.BlockSpec((tile, width), lambda c: (c, 0))
    return pl.pallas_call(
        kernel,
        grid=(length // tile,),
        in_specs=[rows(channels), fixed(w_dt.shape), rows(n), rows(n), rows(n), rows(128)]
        + [anywhere()] * len(after),
        out_specs=rows(rank_width + 2 * n),
        out_shape=jax.ShapeDtypeStruct((length, rank_width + 2 * n), jnp.float32),
        compiler_params=pltpu.CompilerParams(vmem_limit_bytes=40 << 20),
        cost_estimate=estimate(3),
        name="project_back",
    )(pre, w_dt, key_grad, query_grad, keys, fade, *after)


def narrow_products(low_rank, pre, proj_grad, acts, conv_sums, sums):
    length, channels = pre.shape
    tile = min(256, channels)
    rank_width, width = low_rank.shape[1], proj_grad.shape[1]
    used = rank_width + width
    total = used + 32

    def kernel(low_ref, pre_ref, pg_ref, acts_ref, conv_ref, sums_ref, out_ref):
        first = product(low_ref[...], pre_ref[...].astype(jnp.bfloat16), TOKENS)
        out_ref[:rank_width, :] = first.astype(jnp.bfloat16)
        second = product(pg_ref[...], acts_ref[...].astype(jnp.bfloat16), TOKENS)
        out_ref[rank_width:used, :] = second.astype(jnp.bfloat16)
        rows = jnp.concatenate(
            [conv_ref[...], sums_ref[...], jnp.zeros((22, tile), jnp.float32)], 0
        )
        out_ref[used:, :] = rows.astype(jnp.bfloat16)

    column = lambda height: pl.BlockSpec((height, tile), lambda c: (0, c))
    return pl.pallas_call(
        kernel,
        grid=(channels // tile,),
        in_specs=[
            fixed(low_rank.shape),
            column(length),
            fixed(proj_grad.shape),
            column(length),
            column(8),
            column(2),
        ],
        out_specs=column(total),
        out_shape=jax.ShapeDtypeStruct((total, channels), jnp.bfloat16),
        compiler_params=pltpu.CompilerParams(vmem_limit_bytes=48 << 20),
        cost_estimate=estimate(4),
        name="narrow_products",
    )(low_rank, pre, proj_grad, acts, conv_sums, sums)


def project_normed(inner_grad, gate_grad, w_in, after):
    length, channels = inner_grad.shape
    depth = w_in.shape[1]
    tile = min(512, depth)
    height = min(512, length)

    def kernel(inner_ref, gate_ref, w_ref, *refs):
        refs[-1][...] = product(inner_ref[...], w_ref[0], ACROSS) + product(
            gate_ref[...], w_ref[1], ACROSS
        )

    rows = pl.BlockSpec((height, channels), lambda c, r: (r, 0))
    return pl.pallas_call(
        kernel,
        grid=(depth // tile, length // height),
        in_specs=[rows, rows, pl.BlockSpec((2, tile, channels), lambda c, r: (0, c, 0))]
        + [anywhere()] * len(after),
        out_specs=pl.BlockSpec((height, tile), lambda c, r: (r, c)),
        out_shape=jax.ShapeDtypeStruct((length, depth), jnp.float32),
        compiler_params=pltpu.CompilerParams(vmem_limit_bytes=48 << 20),
        cost_estimate=estimate(6),
        name="project_normed",
    )(inner_grad, gate_grad, w_in, *after)


def put_rows(values, rows, at):
    height, width = rows.shape

    def kernel(rows_ref, values_ref, out_ref):
        out_ref[0] = rows_ref[...]

    return pl.pallas_call(
        kernel,
        grid=(1,),
        in_specs=[whole((height, width)), anywhere()],
        out_specs=pl.BlockSpec((1, height, width), lambda c: (0, at // height, 0)),
        out_shape=jax.ShapeDtypeStruct(values.shape, values.dtype),
        input_output_aliases={1: 0},
        name="put_rows",
    )(rows, values)


def to_tiles(values):
    length, channels = values.shape
    parts = values.reshape(length // 8, 8, channels // 128, 128).transpose(0, 2, 1, 3)
    return parts.reshape(length // 8, channels // 16, 128)


def from_tiles(values):
    blocks, height, _ = values.shape
    parts = values.reshape(blocks, height // 8, 8, 128).transpose(0, 2, 1, 3)
    return parts.reshape(blocks * 8, height * 16)


def swap(values, axis, offset):
    size = lax.axis_size(axis)
    return lax.ppermute(values, axis, [(i, i ^ offset) for i in range(size)])


def bits_down(size):
    bits = []
    bit = size // 2
    while bit:
        bits.append(bit)
        bit //= 2
    return bits


def gather_pieces(values, axis):
    pieces = {0: values}
    for bit in bits_down(lax.axis_size(axis)):
        for mask in list(pieces):
            pieces[mask | bit] = swap(pieces[mask], axis, bit)
    return pieces


def nothing(other):
    return other[(slice(0, 1),) * other.ndim].reshape(()).astype(jnp.float32) * 0.0


def sum_mp(values, after=()):
    bit, size = 1, lax.axis_size("mp")
    while bit < size:
        got = swap(values, "mp", bit)
        bit *= 2
        if after and bit == size:
            got = touch(got, after)
        values = values + got
    return values


def scatter_mp(values):
    rank = lax.axis_index("mp")
    size = lax.axis_size("mp")
    rows = values.shape[0] // size
    blocks = values.reshape(1, size, rows, values.shape[1])
    bit = 1
    while bit < size:
        left, here, _, width = blocks.shape
        pairs = blocks.reshape(left, here // 2, 2, rows, width)
        own = (rank // bit) % 2
        keep = lax.dynamic_index_in_dim(pairs, own, 2, keepdims=False)
        give = lax.dynamic_index_in_dim(pairs, 1 - own, 2, keepdims=False).astype(jnp.bfloat16)
        blocks = keep.astype(jnp.float32) + swap(give, "mp", bit).astype(jnp.float32)
        bit *= 2
    return blocks.reshape(rows, values.shape[1])


def trade_side(values):
    side = lax.axis_size("dp") // LINE
    rank = lax.axis_index("dp") % side
    width = values.shape[1] // side
    parts = []
    for mask in range(side):
        part = lax.dynamic_slice_in_dim(values, (rank ^ mask) * width, width, 1)
        parts.append(swap(part, "dp", mask) if mask else part)
    return parts


def line_groups():
    side = lax.axis_size("dp") // LINE
    return [[z * side + x for z in range(LINE)] for x in range(side)]


def scatter_line(values):
    return lax.psum_scatter(
        values, "dp", scatter_dimension=0, tiled=True, axis_index_groups=line_groups()
    )


def gather_line(values):
    return lax.all_gather(values, "dp", axis=0, tiled=True, axis_index_groups=line_groups())


def side_pieces(values):
    pieces = {0: values}
    for bit in bits_down(lax.axis_size("dp") // LINE):
        for mask in list(pieces):
            pieces[mask | bit] = swap(pieces[mask], "dp", bit)
    return pieces


def join_blocks(pieces, tall, place, shape, buffer=None, cuts=LINE, pick=lambda number: number):
    side = lax.axis_size("dp") // LINE
    rank = lax.axis_index("dp") % side
    masks = list(pieces)
    count = len(masks)
    width = pieces[masks[0]].shape[2]
    flank = jnp.stack([rank ^ mask for mask in masks]).astype(jnp.int32)
    block = (1,) * (len(shape) - 2) + (tall, width)
    if width % 128:
        total = jnp.zeros(shape, jnp.float32) if buffer is None else buffer
        for step, mask in enumerate(masks):
            for number in range(cuts):
                value = pieces[mask][pick(number), :tall].astype(jnp.float32).reshape(block)
                at = tuple(i * n for i, n in zip(place(number, flank[step]), block))
                total = lax.dynamic_update_slice(total, value, at)
        return total

    def kernel(flank_ref, *refs):
        step = pl.program_id(0)
        for turn in range(count):

            @pl.when(step == turn)
            def _():
                refs[-1][...] = refs[turn][...].astype(jnp.float32).reshape(block)

    def source(turn):
        def index(step, cut, flank_ref):
            number = jnp.where(step < turn, 0, jnp.where(step == turn, cut, cuts - 1))
            return (pick(number), 0, 0)

        return pl.BlockSpec((1, tall, width), index)

    in_specs = [source(turn) for turn in range(count)]
    operands = [flank] + [pieces[mask] for mask in masks]
    aliases = {}
    if buffer is not None:
        in_specs.append(anywhere())
        operands.append(buffer)
        aliases = {len(operands) - 1: 0}
    return pl.pallas_call(
        kernel,
        grid_spec=pltpu.PrefetchScalarGridSpec(
            num_scalar_prefetch=1,
            grid=(count, cuts),
            in_specs=in_specs,
            out_specs=pl.BlockSpec(
                block, lambda step, cut, flank_ref: place(cut, flank_ref[step])
            ),
        ),
        out_shape=jax.ShapeDtypeStruct(shape, jnp.float32),
        input_output_aliases=aliases,
        compiler_params=pltpu.CompilerParams(vmem_limit_bytes=40 << 20),
        cost_estimate=estimate(count * 2),
        name="join_blocks",
    )(*operands)


def tie(values, other):
    return values + nothing(other).astype(values.dtype)


def on_device(
    block_input,
    norm_gain,
    w_in,
    conv_w,
    conv_b,
    w_x,
    w_dt,
    b_dt,
    d_skip,
    w_out,
    out_grad,
    seq_counts,
):
    row_count, depth = block_input.shape
    size = lax.axis_size("mp")
    side = lax.axis_size("dp") // LINE
    length = row_count * size
    channels = w_in.shape[2]
    state_size = (w_x.shape[1] - R) // 2
    source_rows = block_input.astype(jnp.float32)
    inv_root = lax.rsqrt(jnp.mean(source_rows * source_rows, -1, keepdims=True) + 1e-05)
    normed = (source_rows * inv_root * norm_gain).astype(jnp.bfloat16)
    normed_pieces = gather_pieces(normed, "mp")
    masks = list(normed_pieces)
    ograd_pieces = gather_pieces(tie(out_grad, normed_pieces[masks[1]]), "mp")
    both = jnp.concatenate([normed, out_grad], 1)
    beside = [swap(both, "dp", mask) for mask in range(1, side)]
    keep_mask = boundaries(seq_counts[0], length)
    allow_two = keep_mask * shift_down(keep_mask, 1)
    allow_three = allow_two * shift_down(keep_mask, 2)
    allows = jnp.stack([keep_mask, allow_two, allow_three], 1)
    w_x_rows = w_x.T
    group_normed, inner, acts, proj_part = project_in(
        list(normed_pieces.values()),
        masks,
        w_in,
        allows,
        conv_w,
        conv_b,
        w_x_rows,
    )
    group_ograd, gate_silu, mixer_grad, gate_slope = project_gate(
        list(ograd_pieces.values()), list(ograd_pieces), group_normed, w_in, w_out, beside
    )
    proj = sum_mp(proj_part, (gate_silu,))
    others = []
    for rows in beside:
        others.append({mask: swap(rows, "mp", mask) if mask else rows for mask in masks})
    low_rank = proj[:, :R].astype(jnp.bfloat16)
    keys = proj[:, R : R + state_size]
    queries = proj[:, R + state_size :]
    beta = jax.nn.sigmoid(product(low_rank, w_dt) + b_dt)
    key_square = jnp.sum(keys * keys, 1)
    step_size = beta / (1.0 + beta * key_square[:, None])
    scalars = jnp.concatenate(
        [keys.reshape(-1), queries.reshape(-1), key_square, keep_mask[::8]]
    )
    step_tiles = to_tiles(step_size)
    acts_tiles = to_tiles(acts)
    mix_tiles, states = scan_forward(
        scalars,
        step_tiles,
        acts_tiles,
        CHUNK,
        state_size,
        (gate_silu, gate_slope),
    )
    mixer = from_tiles(mix_tiles) + d_skip * acts
    gated = (mixer * gate_silu).astype(jnp.bfloat16)
    gate_grad = (mixer * gate_slope).astype(jnp.bfloat16)
    back_args = (
        scalars,
        step_tiles,
        acts_tiles,
        to_tiles(mixer_grad),
        states,
        d_skip.astype(jnp.float32).reshape(channels // 128, 128),
        CHUNK,
        state_size,
    )
    chunks = length // CHUNK
    cut = chunks * 5 // 8
    later = scan_backward(*back_args, (cut, chunks), None, [gated, gate_grad])
    gate_job = (group_normed, 0, trade_side(gate_grad), False)
    out_job = (group_ograd, 1, trade_side(gated), True)
    stacked = channels // side == depth // LINE
    parts = factor_products(
        [gate_job, out_job], others, masks, depth, stacked, None, (later[6],)
    )
    scattered = [scatter_line(value) for value in parts]
    pre_tiles, agrad_tiles, key_grad, query_grad, fade, sums, _ = scan_backward(
        *back_args, (0, cut), later, parts
    )
    pre_full = from_tiles(pre_tiles)
    proj_back = project_back(pre_full, w_dt, key_grad, query_grad, keys, fade, ())
    proj_grad = sum_mp(proj_back).astype(jnp.bfloat16)
    inner_grad, conv_sums = finish_inner(
        from_tiles(agrad_tiles), proj_grad, w_x_rows, inner, allows, conv_w, conv_b, ()
    )
    inner_parts = trade_side(inner_grad)
    narrow = narrow_products(
        low_rank, pre_full, proj_grad, acts, conv_sums, sums.reshape(2, channels)
    )
    branch_out = scatter_mp(product(tie(gated, inner_grad), w_out))
    block_out = (source_rows + branch_out).astype(jnp.bfloat16)
    extra = sum((part.astype(jnp.float32) for part in trade_side(narrow))).astype(jnp.bfloat16)
    width = channels // side
    extra = extra.reshape(LINE, extra.shape[0] // LINE, width)
    gain_rows = -(-depth // (16 * width)) * 16
    extra = jnp.concatenate([extra, jnp.zeros((LINE, gain_rows, width), jnp.bfloat16)], 1)
    inner_job = (group_normed, 0, inner_parts, False)
    (inner_part,) = factor_products([inner_job], others, masks, depth, False, extra)
    sums_of = [gather_line(touch(value, (extra,))) for value in scattered]
    if stacked:
        blocks = sums_of[0].reshape(2 * LINE, width, width)
        halves = [blocks]
    else:
        halves = [
            sums_of[0].reshape(LINE, depth // LINE, width),
            sums_of[1].reshape(width, LINE, depth // LINE).transpose(1, 0, 2),
        ]
    half_pieces = [side_pieces(value) for value in halves]
    normed_part = project_normed(inner_grad, gate_grad, w_in, (inner_part,))
    normed_grad = scatter_mp(normed_part)
    scaled = normed_grad * norm_gain
    gain_part = jnp.sum(normed_grad * source_rows * inv_root, 0)
    cubed = inv_root * inv_root * inv_root
    input_grad = inv_root * scaled - source_rows * cubed * jnp.mean(
        scaled * source_rows, -1, keepdims=True
    )
    input_grad = (out_grad.astype(jnp.float32) + input_grad).astype(jnp.bfloat16)
    for bit in bits_down(size):
        gain_part = gain_part + swap(gain_part, "mp", bit)
    part = depth // LINE
    tall = part // 2
    gain = jnp.zeros((gain_rows * width - depth,), jnp.float32)
    gain = jnp.concatenate([gain_part, gain]).reshape(gain_rows, width).astype(jnp.bfloat16)
    last = inner_part.shape[1] - gain_rows
    if last % gain_rows:
        inner_part = lax.dynamic_update_slice(inner_part, gain[None], (0, last, 0))
    else:
        inner_part = put_rows(inner_part, gain, last)
    inner_piece = scatter_line(
        touch(inner_part, sums_of + [block_out, input_grad])
    )
    sent = [value for pieces in half_pieces for value in pieces.values()]
    upper_piece = touch(inner_piece[:, :tall], sent)
    second_sum = gather_line(inner_piece[:, tall:])
    first_sum = gather_line(upper_piece)
    second_pieces = side_pieces(second_sum)
    first_pieces = side_pieces(first_sum)

    shape = (2, depth, channels)
    part_out = lambda start: lambda b, f: (f, b + start)
    part_gate = lambda start: lambda b, f: (1, b + start, f)
    others_of = lambda pieces: {mask: pieces[mask] for mask in pieces if mask}

    def finished(place_of, height, full, job):
        if not stacked:
            pieces = half_pieces[1 - job]
            buffer = join_blocks({0: pieces[0]}, height, place_of(0), full)
            return join_blocks(others_of(pieces), height, place_of(0), full, buffer)
        pick = lambda number: 2 * number + job
        buffer = join_blocks({0: blocks}, height, place_of(0), full, None, LINE, pick)
        return join_blocks(
            others_of(half_pieces[0]), height, place_of(0), full, buffer, LINE, pick
        )

    w_out_grad = finished(part_out, width, (channels, depth), 1 if stacked else 0)
    w_in_grad = finished(part_gate, part, shape, 0 if stacked else 1)
    upper = lambda b, f: (0, 2 * b, f)
    lower = lambda b, f: (0, 2 * b + 1, f)
    w_in_grad = join_blocks({0: second_pieces[0]}, tall, lower, shape, w_in_grad)
    w_in_grad = join_blocks({0: first_pieces[0]}, tall, upper, shape, w_in_grad)
    w_in_grad = join_blocks(others_of(second_pieces), tall, lower, shape, w_in_grad)
    w_in_grad = join_blocks(others_of(first_pieces), tall, upper, shape, w_in_grad)
    flank = lax.axis_index("dp") % side
    narrow = jnp.zeros((LINE * (last - part), channels), jnp.float32)
    for mask, piece in second_pieces.items():
        rows = piece[:, tall : last - tall].reshape(-1, width).astype(jnp.float32)
        narrow = lax.dynamic_update_slice(narrow, rows, (0, (flank ^ mask) * width))
    gains = [piece[0, last - tall :] for piece in second_pieces.values()]
    gain = sum((value.astype(jnp.float32) for value in gains)).reshape(-1)[:depth]
    split = R + R + 2 * state_size
    return (
        block_out,
        input_grad,
        gain,
        w_in_grad,
        narrow[split : split + 4],
        narrow[split + 4],
        narrow[R:split].T,
        narrow[:R],
        narrow[split + 8],
        narrow[split + 9],
        w_out_grad,
    )


def solution(mesh):
    in_specs = (
        P(("dp", "mp"), None),
        P(),
        P(None, None, "mp"),
        P(None, "mp"),
        P("mp"),
        P("mp", None),
        P(None, "mp"),
        P("mp"),
        P("mp"),
        P("mp", None),
        P(("dp", "mp"), None),
        P("dp", None),
    )
    out_specs = (
        P(("dp", "mp"), None),
        P(("dp", "mp"), None),
        P(),
        P(None, None, "mp"),
        P(None, "mp"),
        P("mp"),
        P("mp", None),
        P(None, "mp"),
        P("mp"),
        P("mp"),
        P("mp", None),
    )
    return jax.shard_map(
        on_device, mesh=mesh, in_specs=in_specs, out_specs=out_specs, check_vma=False
    )
```
